32 devices in a mesh: expert: 16 (over z, x, core), batch: 2 (over y).
Axes of the slice: x: 2, y: 2, z: 4, core: 2. Of those that a mesh axis runs over, the one named last changes fastest.
Arguments:
- tokens: bfloat16 [16384, 1024], P(('expert', 'batch')), may hold values from -6 to 6
- cotangent: bfloat16 [16384, 1024], P(('expert', 'batch')), may hold values from -6 to 6
- segment_ids: int32 [32, 512], P(('expert', 'batch')), may hold values from 0 to 3, never falling along the last dimension, each value on 1 to 256 neighbouring positions
- routing: int32 [32, 512], P(('expert', 'batch')), may hold values from 0 to 511, each once within a row
- ln_gain: bfloat16 [1024], replicated, may hold values from 0.099609375 to 1.8984375
- ln_bias: bfloat16 [1024], replicated, may hold values from -1.1953125 to 1.1953125
- w_query: bfloat16 [1024, 1024], replicated, may hold values from -0.1875 to 0.1875
- w_key: bfloat16 [1024, 1024], replicated, may hold values from -0.1875 to 0.1875
- w_value: bfloat16 [1024, 1024], replicated, may hold values from -0.1875 to 0.1875
- w_output: bfloat16 [1024, 1024], replicated, may hold values from -0.75 to 0.75
- expert_gain: bfloat16 [16, 1024], P('expert'), may hold values from 0.099609375 to 1.8984375
- expert_bias: bfloat16 [16, 1024], P('expert'), may hold values from -1.1953125 to 1.1953125
- centroid: bfloat16 [16, 1024], P('expert'), may hold values from -0.125 to 0.125
- w_in: bfloat16 [16, 1024, 4096], P('expert'), may hold values from -0.1875 to 0.1875
- w_out: bfloat16 [16, 4096, 1024], P('expert'), may hold values from -0.1875 to 0.1875
Outputs:
- outputs: bfloat16 [16384, 1024], P(('expert', 'batch'))
- grad_tokens: bfloat16 [16384, 1024], P(('expert', 'batch'))
- grad_ln_gain: float32 [1024], P('batch')
- grad_ln_bias: float32 [1024], P('batch')
- grad_query: float32 [1024, 1024], P('batch')
- grad_key: float32 [1024, 1024], P('batch')
- grad_value: float32 [1024, 1024], P('batch')
- grad_output: float32 [1024, 1024], P('batch')
- grad_expert_gain: float32 [16, 1024], P('expert', 'batch')
- grad_expert_bias: float32 [16, 1024], P('expert', 'batch')
- grad_centroid: float32 [16, 1024], P('expert', 'batch')
- grad_w_in: float32 [16, 1024, 4096], P('expert', 'batch')
- grad_w_out: float32 [16, 4096, 1024], P('expert', 'batch')
- mean_gate: float32 [16], P('batch')
The draws below stay inside these ranges and needn't reach their ends.
Inputs may be any that keep to these rules, and one draw needn't show every extreme that they name: `routing`: each row holds every slot's token once. `segment_ids`: segment ids never fall along a row.
All inputs are finite; a program needn't handle non-finite values.
Results may differ from the reference program's by a relative error of at most 0.013.
Values may be sent and summed in bfloat16 or wider, within the bound.
No kernel may reach another device: no remote copies, remote signals or barrier semaphores. Data moves between devices by JAX's collectives and lax.ppermute only.
A program may use at most 256 MiB of HBM per device.

```python
import math
from functools import partial
import jax
import jax.numpy as jnp
import numpy as np
from jax import lax

D = 1024
HEADS = 16
HEAD_DIM = 64
FF = 4096
TOK_DEV = 512
EXPERTS = 16
SEQS = 32
TOKENS = 16384
SEND = 32


def steps_of(key, shape, cuts, low, high):
    level = 1.0
    for dim, parts in cuts:
        draws = jax.random.uniform(jax.random.fold_in(jax.random.fold_in(key, 6), dim), (parts,), jnp.float32, low / len(cuts), high / len(cuts))
        level = level * jnp.repeat(jnp.exp(draws), shape[dim] // parts).reshape((-1,) + (1,) * (len(shape) - 1 - dim))
    return level


def profile(count, total, limit, skew):
    loads = [(1 << 20) // math.isqrt(rank ** skew) + 1 for rank in range(2, count + 1)]
    rest, counts = total - limit - (count - 1), [1] * (count - 1)
    while rest > 0:
        free = [i for i in range(count - 1) if counts[i] < limit]
        whole, budget = sum([loads[i] for i in free]), rest
        for i in free:
            more = min(limit - counts[i], max(1, budget * loads[i] // whole), rest)
            counts[i] = counts[i] + more
            rest = rest - more
    return np.array([limit] + counts)


def uneven_parts(key, amount, total, most, lean):
    if amount == 2:
        one = jax.random.randint(key, (), max(1, total - most), min(most, total - 1) + 1)
        return jnp.stack([one, total - one])
    sizes = jnp.asarray(profile(amount, total, most, lean), jnp.int32)
    twos = (amount - 1) // 2
    source_of, sink = sizes[1:1 + 2 * twos:2], sizes[2:2 + 2 * twos:2]
    margin = jnp.minimum(source_of - 1, most - sink)
    passed = jax.random.randint(jax.random.fold_in(key, 1), (twos,), 0, 1 << 20) % (margin + 1)
    sizes = sizes.at[1:1 + 2 * twos:2].set(source_of - passed).at[2:2 + 2 * twos:2].set(sink + passed)
    return sizes[jax.random.permutation(jax.random.fold_in(key, 2), amount)]


def scatter_about(rng, shape, scale, limit, split=(), kind=jnp.bfloat16):
    drawn = scale * jax.random.normal(rng, shape, jnp.float32)
    if split:
        drawn = drawn * steps_of(rng, shape, split, -0.22, 0.18)
    return jnp.clip(drawn, -limit, limit).astype(kind)


def setup_inputs(seed: int = 0) -> dict:
    streams_of = jax.random.split(jax.random.key(seed), 16)
    tokens = scatter_about(streams_of[0], (TOKENS, D), 1.0, 6.0, ((0, 32),))
    cotangent = scatter_about(streams_of[1], (TOKENS, D), 1.0, 6.0, ((0, 32),))
    segment_ids = jax.vmap(lambda own: jnp.searchsorted(jnp.cumsum(uneven_parts(own, 4, TOK_DEV, TOK_DEV // 2, 0)), jnp.arange(TOK_DEV), side="right"))(jax.random.split(streams_of[2], SEQS)).reshape((SEQS, TOK_DEV)).astype(jnp.int32)
    routing = jax.vmap(lambda own: jax.random.permutation(own, TOK_DEV))(jax.random.split(streams_of[3], SEQS)).reshape((SEQS, TOK_DEV)).astype(jnp.int32)
    ln_gain = jnp.clip(1.0 + 0.18 * jax.random.normal(streams_of[4], (D,), jnp.float32), 0.099609375, 1.8984375).astype(jnp.bfloat16)
    ln_bias = scatter_about(streams_of[5], (D,), 0.2, 1.1953125)
    w_query = scatter_about(streams_of[6], (D, D), D ** -0.5, 0.1875)
    w_key = scatter_about(streams_of[7], (D, D), D ** -0.5, 0.1875)
    w_value = scatter_about(streams_of[8], (D, D), D ** -0.5, 0.1875)
    w_output = scatter_about(streams_of[9], (D, D), (D // 16) ** -0.5, 0.75)
    expert_gain = jnp.clip(1.0 + 0.18 * jax.random.normal(streams_of[10], (EXPERTS, D), jnp.float32), 0.099609375, 1.8984375).astype(jnp.bfloat16)
    expert_bias = scatter_about(streams_of[11], (EXPERTS, D), 0.2, 1.1953125, ((0, 16),))
    centroid = scatter_about(streams_of[12], (EXPERTS, D), (2 * D) ** -0.5, 0.125, ((0, 16),))
    w_in = scatter_about(streams_of[13], (EXPERTS, D, FF), D ** -0.5, 0.1875, ((0, 16),))
    w_out = scatter_about(streams_of[14], (EXPERTS, FF, D), (FF // 4) ** -0.5, 0.1875, ((0, 16),))
    return dict(tokens=tokens, cotangent=cotangent, segment_ids=segment_ids, routing=routing, ln_gain=ln_gain, ln_bias=ln_bias, w_query=w_query, w_key=w_key, w_value=w_value, w_output=w_output, expert_gain=expert_gain, expert_bias=expert_bias, centroid=centroid, w_in=w_in, w_out=w_out)


NORM_EPSILON = 1e-05
NEG_FILL = -1e+30
HIGHEST_PRECISION = lax.Precision.HIGHEST

@jax.custom_vjp
def low(v):
    return lax.optimization_barrier(v.astype(jnp.bfloat16)).astype(jnp.float32)

@jax.custom_vjp
def low_back(v):
    return v

def low_keep(v):
    return (low(v), None)

def low_pass(kept, grad):
    return (grad,)

def back_keep(v):
    return (v, None)

def back_low(kept, grad):
    return (low(grad),)
low.defvjp(low_keep, low_pass)
low_back.defvjp(back_keep, back_low)

def layer_norm(values, gain_vec, shift_vec):
    center = values - lax.optimization_barrier(jnp.mean(values, axis=-1, keepdims=True))
    spread = lax.optimization_barrier(jnp.mean(center * center, axis=-1, keepdims=True))
    return center * lax.rsqrt(spread + NORM_EPSILON) * gain_vec + shift_vec

def gelu_curve(values):
    return 0.5 * values * (1.0 + jnp.tanh(0.7978845608028654 * (values + 0.044715 * values * values * values)))

def sigmoid_curve(values):
    return 1.0 / (1.0 + jnp.exp(-values))

def sequence_attention(pieces):
    queries, key_rows, value_rows, segment = pieces
    length = queries.shape[0]
    scores = jnp.einsum('qhd,khd->hqk', queries, key_rows, precision=HIGHEST_PRECISION) * HEAD_DIM ** (-0.5)
    scores = low_back(scores)
    position = jnp.arange(length)
    allowed = (position[:, None] >= position[None, :]) & (segment[:, None] == segment[None, :])
    scores = jnp.where(allowed[None], scores, NEG_FILL)
    row_peak = lax.optimization_barrier(jnp.max(scores, axis=-1, keepdims=True))
    exp_terms = jnp.exp(scores - row_peak)
    probs_full = exp_terms / lax.optimization_barrier(jnp.sum(exp_terms, axis=-1, keepdims=True))
    weights = low(probs_full)
    return jnp.einsum('hqk,khd->qhd', weights, value_rows, precision=HIGHEST_PRECISION)

def expert_apply(pieces):
    rows_in, gain_vec, shift_vec, center_vec, weight_in, weight_out = pieces
    gating = sigmoid_curve(jnp.dot(rows_in, center_vec, precision=HIGHEST_PRECISION))
    normed = low(layer_norm(rows_in, gain_vec, shift_vec))
    hidden = low_back(jnp.dot(normed, weight_in, precision=HIGHEST_PRECISION))
    active = low(gelu_curve(hidden))
    produced = low_back(jnp.dot(active, weight_out, precision=HIGHEST_PRECISION))
    return (gating[:, None] * produced, gating)

def forward(tokens_f, ln_gain, ln_bias, w_query, w_key, w_value, w_output, expert_gain, expert_bias, centroid, w_in, w_out, segment_ids=None, routing=None):
    normed = low(layer_norm(tokens_f, ln_gain, ln_bias))
    heads_shape = (SEQS, TOK_DEV, HEADS, HEAD_DIM)
    queries = low(low_back(jnp.dot(normed, w_query, precision=HIGHEST_PRECISION)))
    key_rows = low(low_back(jnp.dot(normed, w_key, precision=HIGHEST_PRECISION)))
    value_rows = low(low_back(jnp.dot(normed, w_value, precision=HIGHEST_PRECISION)))
    mixed_rows = lax.map(jax.checkpoint(sequence_attention), (queries.reshape(heads_shape), key_rows.reshape(heads_shape), value_rows.reshape(heads_shape), segment_ids))
    mixed_rows = low(low_back(mixed_rows.reshape(TOKENS, D)))
    attended = low_back(jnp.dot(mixed_rows, w_output, precision=HIGHEST_PRECISION))
    stream = tokens_f + attended
    sent_rows = low(low_back(stream))
    per_device = sent_rows.reshape(SEQS, TOK_DEV, D)
    seq_index = jnp.arange(SEQS, dtype=jnp.int32)[:, None]
    ordered = per_device[seq_index, routing]
    grouped = ordered.reshape(SEQS, EXPERTS, SEND, D).transpose(1, 0, 2, 3).reshape(EXPERTS, SEQS * SEND, D)
    branch, gating = lax.map(jax.checkpoint(expert_apply), (grouped, expert_gain, expert_bias, centroid, w_in, w_out))
    branch = low(low_back(branch))
    returned = branch.reshape(EXPERTS, SEQS, SEND, D).transpose(1, 0, 2, 3).reshape(SEQS, TOK_DEV, D)
    inverse = jnp.argsort(routing, axis=1).astype(jnp.int32)
    restored = returned[seq_index, inverse].reshape(TOKENS, D)
    return (stream + restored, gating)

def reference(tokens, cotangent, segment_ids, routing, ln_gain, ln_bias, w_query, w_key, w_value, w_output, expert_gain, expert_bias, centroid, w_in, w_out):
    params = tuple((item.astype(jnp.float32) for item in (tokens, ln_gain, ln_bias, w_query, w_key, w_value, w_output, expert_gain, expert_bias, centroid, w_in, w_out)))
    wrapped = partial(forward, segment_ids=segment_ids, routing=routing)
    result, pullback, gating = jax.vjp(wrapped, *params, has_aux=True)
    gradients = pullback(cotangent.astype(jnp.float32))
    return (result.astype(jnp.bfloat16), gradients[0].astype(jnp.bfloat16), gradients[1], gradients[2], gradients[3], gradients[4], gradients[5], gradients[6], gradients[7], gradients[8], gradients[9], gradients[10], gradients[11], lax.optimization_barrier(jnp.mean(gating, axis=1)))
```

```python
import jax
import jax.numpy as jnp
from jax import lax
from jax.sharding import PartitionSpec as P

HEADS = 16


NORM_EPSILON = 1e-05
NEG_FILL = -1e30


def layer_norm(values, gain_vec, shift_vec):
    center = values - jnp.mean(values, axis=-1, keepdims=True)
    spread = jnp.mean(center * center, axis=-1, keepdims=True)
    return center * lax.rsqrt(spread + NORM_EPSILON) * gain_vec + shift_vec


def gelu_curve(values):
    return (
        0.5
        * values
        * (1.0 + jnp.tanh(0.7978845608028654 * (values + 0.044715 * values * values * values)))
    )


def sigmoid_curve(values):
    return 1.0 / (1.0 + jnp.exp(-values))


def dot(a, b, ca, cb):
    return lax.dot_general(a, b, (((ca,), (cb,)), ((), ())), preferred_element_type=jnp.float32)


def expert_stages(size):
    if size % 2:
        return [(1, size)]
    rest = size // 2
    middle = 1
    while (2 * middle) ** 2 <= rest and rest % (2 * middle) == 0:
        middle *= 2
    levels = [(1, 2), (2, middle), (2 * middle, rest // middle)]
    return [level for level in levels if level[1] > 1]


def turned(axis, stride, length, step):
    pairs = []
    for index in range(lax.axis_size(axis)):
        place = (index // stride) % length
        pairs.append((index, index + ((place + step) % length - place) * stride))
    return pairs


def scatter_level(rows, axis, stride, length):
    place = (lax.axis_index(axis) // stride) % length
    count = rows.shape[0] // length
    total = lax.dynamic_slice_in_dim(rows, place * count, count, 0).astype(jnp.float32)
    for step in range(1, length):
        part = lax.dynamic_slice_in_dim(rows, ((place + step) % length) * count, count, 0)
        part = lax.ppermute(part, axis, turned(axis, stride, length, step))
        total = total + part.astype(jnp.float32)
    return total.astype(rows.dtype)


def gather_level(rows, axis, stride, length):
    place = (lax.axis_index(axis) // stride) % length
    count = rows.shape[0]
    parts = [rows] + [
        lax.ppermute(rows, axis, turned(axis, stride, length, step)) for step in range(1, length)
    ]
    if length == 2:
        return jnp.where(
            place == 0, jnp.concatenate(parts, 0), jnp.concatenate([parts[1], parts[0]], 0)
        )
    whole = jnp.zeros((length * count, rows.shape[1]), rows.dtype)
    for step, part in enumerate(parts):
        whole = lax.dynamic_update_slice_in_dim(whole, part, ((place - step) % length) * count, 0)
    return whole


def total_rows(rows):
    replicas = lax.axis_size("batch")
    levels = expert_stages(lax.axis_size("expert"))
    stride, length = levels[0]
    place = (lax.axis_index("expert") // stride) % length
    columns = rows.shape[1]
    split = rows.reshape(replicas, length, -1, columns)
    mine = lax.dynamic_index_in_dim(split, place, 1, False)
    total = mine.astype(jnp.float32)
    for step in range(1, length):
        part = lax.dynamic_index_in_dim(split, (place + step) % length, 1, False)
        part = lax.ppermute(
            part.astype(jnp.bfloat16), "expert", turned("expert", stride, length, step)
        )
        total = total + part.astype(jnp.float32)
    held = total.astype(jnp.bfloat16).reshape(-1, columns)
    held = scatter_level(held, "batch", 1, replicas)
    for stride, length in levels[1:]:
        held = scatter_level(held, "expert", stride, length)
    for stride, length in reversed(levels):
        held = gather_level(held, "expert", stride, length)
    return held.astype(jnp.float32)


def total_small(values):
    replicas = lax.axis_size("batch")
    owners = lax.axis_size("expert")
    place = lax.axis_index("batch")
    total = lax.dynamic_index_in_dim(values, place, 0, True)
    for step in range(1, replicas):
        part = lax.dynamic_index_in_dim(values, (place + step) % replicas, 0, True)
        total = total + lax.ppermute(part, "batch", turned("batch", 1, replicas, step))
    bit = 1
    while bit < owners:
        total = total + lax.ppermute(total, "expert", [(i, i ^ bit) for i in range(owners)])
        bit *= 2
    return total[0]


def local(
    tokens,
    cotangent,
    segment_ids,
    routing,
    ln_gain,
    ln_bias,
    w_query,
    w_key,
    w_value,
    w_output,
    expert_gain,
    expert_bias,
    centroid,
    w_in,
    w_out,
):
    count_tok, model_width = tokens.shape
    heads_num = HEADS
    head_size = model_width // heads_num
    scale_factor = head_size ** (-0.5)
    owners = lax.axis_size("expert")
    replicas = lax.axis_size("batch")
    batch_index = lax.axis_index("batch")
    send_rows = count_tok // owners
    segment = segment_ids[0]
    slot_order = routing[0]
    position = jnp.arange(count_tok)
    picks = (slot_order[:, None] == position[None, :]).astype(jnp.bfloat16)
    gain_f = expert_gain[0].astype(jnp.float32)
    bias_f = expert_bias[0].astype(jnp.float32)
    center_f = centroid[0].astype(jnp.float32)
    win = w_in[0]
    wout = w_out[0]
    hidden_width = win.shape[1]

    def to_owners(values):
        ordered = dot(picks, values, 1, 0).astype(jnp.bfloat16)
        arrived = lax.all_to_all(
            ordered.reshape(owners, send_rows, model_width),
            "expert",
            split_axis=0,
            concat_axis=0,
            tiled=True,
        )
        return arrived.reshape(count_tok, model_width)

    def to_tokens(values):
        returned = lax.all_to_all(
            values.reshape(owners, send_rows, model_width),
            "expert",
            split_axis=0,
            concat_axis=0,
            tiled=True,
        )
        return dot(picks, returned.reshape(count_tok, model_width), 0, 0)

    def from_copy(values, step):
        return lax.ppermute(values, "batch", turned("batch", 1, replicas, step))

    cot_rows = to_owners(cotangent)
    paired = replicas == 2
    cot_other = from_copy(cot_rows, 1) if paired else None

    tokens_f = tokens.astype(jnp.float32)
    normed_f, norm_back = jax.vjp(
        layer_norm, tokens_f, ln_gain.astype(jnp.float32), ln_bias.astype(jnp.float32)
    )
    normed = normed_f.astype(jnp.bfloat16)
    queries = dot(normed, w_query, 1, 0).astype(jnp.bfloat16)
    key_rows = dot(normed, w_key, 1, 0).astype(jnp.bfloat16)
    value_rows = dot(normed, w_value, 1, 0).astype(jnp.bfloat16)
    head_shape = (count_tok, heads_num, head_size)
    query_heads = queries.reshape(head_shape)
    key_heads = key_rows.reshape(head_shape)
    value_heads = value_rows.reshape(head_shape)
    allowed = (position[:, None] >= position[None, :]) & (segment[:, None] == segment[None, :])
    scores = (
        jnp.einsum("qhd,khd->hqk", query_heads, key_heads, preferred_element_type=jnp.float32)
        * scale_factor
    )
    scores = jnp.where(allowed[None], scores, NEG_FILL)
    row_peak = jnp.max(scores, axis=-1, keepdims=True)
    exp_terms = jnp.exp(scores - row_peak)
    row_total = jnp.sum(exp_terms, axis=-1, keepdims=True)
    weights = (exp_terms / row_total).astype(jnp.bfloat16)
    mixed = jnp.einsum("hqk,khd->qhd", weights, value_heads, preferred_element_type=jnp.float32)
    mixed_rows = mixed.astype(jnp.bfloat16).reshape(count_tok, model_width)
    log_totals = row_peak + jnp.log(row_total)
    stream = tokens_f + dot(mixed_rows, w_output, 1, 0)
    rows = to_owners(stream.astype(jnp.bfloat16))
    rows_other = from_copy(rows, 1) if paired else None

    def expert_forward(rows_in, cot_in):
        rows_f = rows_in.astype(jnp.float32)
        gating = sigmoid_curve(jnp.sum(rows_f * center_f, axis=-1, keepdims=True))
        center = rows_f - jnp.mean(rows_f, axis=-1, keepdims=True)
        inverse = lax.rsqrt(jnp.mean(center * center, axis=-1, keepdims=True) + NORM_EPSILON)
        unit = center * inverse
        expert_normed = (unit * gain_f + bias_f).astype(jnp.bfloat16)
        hidden = dot(expert_normed, win, 1, 0)
        active_f, gelu_back = jax.vjp(gelu_curve, hidden)
        active = active_f.astype(jnp.bfloat16)
        grad_produced = (gating * cot_in.astype(jnp.float32)).astype(jnp.bfloat16)
        grad_active = dot(grad_produced, wout, 1, 1)
        grad_hidden = gelu_back(grad_active)[0].astype(jnp.bfloat16)
        return rows_f, gating, inverse, unit, expert_normed, active, grad_produced, grad_hidden

    rows_f, gating, inverse, unit, expert_normed, active, grad_produced, grad_hidden = (
        expert_forward(rows, cot_rows)
    )
    grad_branch = cot_rows.astype(jnp.float32)
    produced = dot(active, wout, 1, 0)
    grad_gating = jnp.sum(grad_branch * produced, axis=-1, keepdims=True)
    grad_expert_normed = dot(grad_hidden, win, 1, 1)
    grad_unit = grad_expert_normed * gain_f
    grad_rows = inverse * (
        grad_unit
        - jnp.mean(grad_unit, axis=-1, keepdims=True)
        - unit * jnp.mean(grad_unit * unit, axis=-1, keepdims=True)
    )
    grad_score = grad_gating * gating * (1.0 - gating)
    grad_rows = (grad_rows + grad_score * center_f).astype(jnp.bfloat16)
    grad_sent = to_tokens(grad_rows)
    small = jnp.stack(
        [
            jnp.sum(grad_expert_normed * unit, axis=0),
            jnp.sum(grad_expert_normed, axis=0),
            jnp.sum(grad_score * rows_f, axis=0),
        ]
    ).reshape(3, replicas, model_width // replicas)
    branch = (gating * produced).astype(jnp.bfloat16)
    outputs = (stream + to_tokens(branch)).astype(jnp.bfloat16)

    part_in = model_width // replicas
    part_out = hidden_width // replicas

    def cut(values, width):
        return lax.dynamic_slice_in_dim(values, batch_index * width, width, 1)

    small_total = lax.dynamic_index_in_dim(small, batch_index, 1, False)
    for step in range(1, replicas):
        away = lax.dynamic_index_in_dim(small, (batch_index + step) % replicas, 1, False)
        small_total = small_total + from_copy(away, step)
    if paired:
        other = expert_forward(rows_other, cot_other)
        grad_w_in = dot(
            jnp.concatenate([cut(expert_normed, part_in), cut(other[4], part_in)]),
            jnp.concatenate([grad_hidden, other[7]]),
            0,
            0,
        )
        grad_w_out = dot(
            jnp.concatenate([cut(active, part_out), cut(other[5], part_out)]),
            jnp.concatenate([grad_produced, other[6]]),
            0,
            0,
        )
    else:
        grad_w_in, grad_w_out = (
            lax.psum_scatter(
                dot(left, right, 0, 0).astype(jnp.bfloat16),
                "batch",
                scatter_dimension=0,
                tiled=True,
            ).astype(jnp.float32)
            for left, right in ((expert_normed, grad_hidden), (active, grad_produced))
        )

    grad_stream = cotangent.astype(jnp.float32) + grad_sent
    grad_attended = grad_stream.astype(jnp.bfloat16)
    grad_wo = dot(mixed_rows, grad_attended, 0, 0)
    grad_wo = total_rows(grad_wo)
    grad_mixed = dot(grad_attended, w_output, 1, 1).astype(jnp.bfloat16).reshape(head_shape)

    probs = jnp.exp(scores - log_totals)
    weights = probs.astype(jnp.bfloat16)
    grad_probs = jnp.einsum(
        "qhd,khd->hqk", grad_mixed, value_heads, preferred_element_type=jnp.float32
    )
    centre = jnp.sum(probs * grad_probs, axis=-1, keepdims=True)
    grad_scores = (probs * (grad_probs - centre)).astype(jnp.bfloat16)

    def joined(values):
        return values.astype(jnp.bfloat16).reshape(count_tok, model_width)

    grad_queries = joined(
        jnp.einsum("hqk,khd->qhd", grad_scores, key_heads, preferred_element_type=jnp.float32)
        * scale_factor
    )
    grad_keys = joined(
        jnp.einsum("hqk,qhd->khd", grad_scores, query_heads, preferred_element_type=jnp.float32)
        * scale_factor
    )
    grad_values = joined(
        jnp.einsum("hqk,qhd->khd", weights, grad_mixed, preferred_element_type=jnp.float32)
    )
    grad_wq = total_rows(dot(normed, grad_queries, 0, 0))
    grad_wk = total_rows(dot(normed, grad_keys, 0, 0))
    grad_wv = total_rows(dot(normed, grad_values, 0, 0))
    grad_normed = (
        dot(grad_queries, w_query, 1, 1)
        + dot(grad_keys, w_key, 1, 1)
        + dot(grad_values, w_value, 1, 1)
    )
    grad_token_norm, grad_gain, grad_bias = norm_back(grad_normed)
    grad_tokens = (grad_stream + grad_token_norm).astype(jnp.bfloat16)

    rows_total = count_tok * replicas
    gate_vector = jnp.where(
        jnp.arange(owners) == lax.axis_index("expert"), jnp.sum(gating) / rows_total, 0.0
    )
    packed = jnp.concatenate(
        [
            grad_gain.reshape(replicas, -1),
            grad_bias.reshape(replicas, -1),
            gate_vector.reshape(replicas, -1),
        ],
        axis=1,
    )
    packed = total_small(packed)
    return (
        outputs,
        grad_tokens,
        packed[:part_in],
        packed[part_in : 2 * part_in],
        grad_wq,
        grad_wk,
        grad_wv,
        grad_wo,
        small_total[0][None],
        small_total[1][None],
        small_total[2][None],
        grad_w_in[None],
        grad_w_out[None],
        packed[2 * part_in :],
    )


def solution(mesh):
    both = P(("expert", "batch"), None)
    per_expert = P("expert", None)
    matrices = P("expert", None, None)
    return jax.shard_map(
        local,
        mesh=mesh,
        in_specs=(both,) * 4 + (P(),) * 6 + (per_expert,) * 3 + (matrices,) * 2,
        out_specs=(both, both)
        + (P("batch"),) * 2
        + (P("batch", None),) * 4
        + (P("expert", "batch"),) * 3
        + (P("expert", "batch", None),) * 2
        + (P("batch"),),
        check_vma=False,
    )
```

```python
import functools

import jax
import jax.numpy as jnp
from jax import lax
from jax.experimental import pallas as pl
from jax.experimental.pallas import tpu as pltpu
from jax.sharding import PartitionSpec as P

HEADS = 16
NORM_EPSILON = 1e-05
NEG_FILL = -1e30
LOG2E = 1.4426950408889634
GROUP = 256
CORES = 2
TILE = 512
BF = jnp.bfloat16
F32 = jnp.float32


def dot(a, b, ca, cb):
    return lax.dot_general(a, b, (((ca,), (cb,)), ((), ())), preferred_element_type=F32)


def kernel_call(body, name, mib=60, **more):
    return pl.pallas_call(
        body, name=name, compiler_params=pltpu.CompilerParams(vmem_limit_bytes=mib << 20), **more
    )


def shaped(shape, kind):
    return jax.ShapeDtypeStruct(shape, kind)


def fixed(*shape):
    return pl.BlockSpec(shape, lambda *place: (0,) * len(shape))


def scalar():
    return pl.BlockSpec(memory_space=pltpu.SMEM)


def as_column(row):
    return jnp.transpose(jnp.broadcast_to(row, (8, row.shape[1])))[:, :1]


def standardized(values):
    center = values - jnp.mean(values, axis=-1, keepdims=True)
    spread = jnp.mean(center * center, axis=-1, keepdims=True)
    inverse = lax.rsqrt(spread + NORM_EPSILON)
    return center * inverse, inverse


def norm_backward(grad, unit, inverse):
    mean = jnp.mean(grad, axis=-1, keepdims=True)
    slope = jnp.mean(grad * unit, axis=-1, keepdims=True)
    return inverse * (grad - mean - unit * slope)


def query_blocks(count):
    size = min(256, count)
    blocks, place = [], 0
    for first in range(0, count, size):
        blocks.append((first, size, first + size, place))
        place += first + size
    return blocks, place


def stacked(part, first, size, head_size):
    lane = lax.broadcasted_iota(jnp.int32, (1, GROUP), 1) // head_size
    rows = part[first : first + size]
    return jnp.concatenate(
        [
            jnp.where(lane == head, rows, jnp.zeros_like(rows))
            for head in range(GROUP // head_size)
        ],
        0,
    )


def picked(rows, size, head_size):
    lane = lax.broadcasted_iota(jnp.int32, (1, GROUP), 1) // head_size
    out = rows[:size]
    for head in range(1, GROUP // head_size):
        out = jnp.where(lane == head, rows[head * size : (head + 1) * size], out)
    return out


def split_cores(whole_ref, place_ref, send_ref, keep_ref):
    copies, rows, _ = send_ref.shape
    place = place_ref[0]
    for copy in range(copies):
        start = copy * CORES * rows
        keep = pl.multiple_of(start + place * rows, rows)
        send = pl.multiple_of(start + (1 - place) * rows, rows)
        keep_ref[copy] = whole_ref[pl.ds(keep, rows), :]
        send_ref[copy] = whole_ref[pl.ds(send, rows), :]


def order_kernel(values_ref, slots_ref, ordered_ref):
    count = values_ref.shape[0]
    picks = as_column(slots_ref[...]) == lax.broadcasted_iota(jnp.int32, (count, count), 1)
    ordered_ref[...] = dot(picks.astype(BF), values_ref[...], 1, 0).astype(BF)


def order_rows(values, slots):
    return kernel_call(
        order_kernel, "order_rows", out_shape=shaped(values.shape, BF)
    )(values, slots)


def restored(slots_ref, returned_ref):
    count = returned_ref.shape[0]
    picks = slots_ref[...] == lax.broadcasted_iota(jnp.int32, (count, count), 0)
    return dot(picks.astype(BF), returned_ref[...], 1, 0)


def output_kernel(returned_ref, slots_ref, stream_ref, out_ref):
    out_ref[...] = (stream_ref[...] + restored(slots_ref, returned_ref)).astype(BF)


def output_rows(returned, slots, stream):
    return kernel_call(output_kernel, "output_rows", out_shape=shaped(returned.shape, BF))(
        returned, slots, stream
    )


def entry_kernel(
    returned_ref,
    slots_ref,
    cot_ref,
    mixed_ref,
    place_ref,
    stream_ref,
    attended_ref,
    send_ref,
    keep_ref,
    whole_ref,
):
    stream = cot_ref[...].astype(F32) + restored(slots_ref, returned_ref)
    stream_ref[...] = stream
    attended = stream.astype(BF)
    attended_ref[...] = attended
    whole_ref[...] = dot(mixed_ref[...], attended, 0, 0).astype(BF)
    split_cores(whole_ref, place_ref, send_ref, keep_ref)


def gradient_entry(returned, slots, cot, mixed, place, copies):
    count, width = cot.shape
    half = (copies, width // (CORES * copies), width)
    return kernel_call(
        entry_kernel,
        "gradient_entry",
        grid=(1,),
        in_specs=[fixed(count, width), fixed(1, count), fixed(count, width), fixed(count, width)]
        + [scalar()],
        out_specs=[fixed(count, width), fixed(count, width), fixed(*half), fixed(*half)],
        out_shape=[shaped((count, width), F32), shaped((count, width), BF)] + [shaped(half, BF)] * 2,
        scratch_shapes=[pltpu.VMEM((width, width), BF)],
    )(returned, slots, cot, mixed, place)


def attention_kernel(
    head_size,
    tokens_ref,
    gain_ref,
    bias_ref,
    segment_ref,
    slots_ref,
    wq_ref,
    wk_ref,
    wv_ref,
    wo_ref,
    normed_ref,
    q_ref,
    k_ref,
    v_ref,
    mixed_ref,
    probs_ref,
    stream_ref,
    ordered_ref,
    mask_ref,
):
    step = pl.program_id(0)
    count = tokens_ref.shape[0]
    blocks, _ = query_blocks(count)
    per = GROUP // head_size

    @pl.when(step == 0)
    def _():
        values = tokens_ref[...].astype(F32)
        unit, _ = standardized(values)
        normed = unit * gain_ref[...].astype(F32) + bias_ref[...].astype(F32)
        normed_ref[...] = normed.astype(BF)
        stream_ref[...] = values
        segment = segment_ref[...]
        column = as_column(segment)
        for first, size, keys, place in blocks:
            shape = (keys, size)
            query = first + lax.broadcasted_iota(jnp.int32, shape, 1)
            later = lax.broadcasted_iota(jnp.int32, shape, 0) <= query
            same = column[:keys] == segment[:, first : first + size]
            mask_ref[place : place + keys, :] = jnp.where(later & same, 0.0, NEG_FILL)

    normed = normed_ref[...]
    queries = dot(normed, wq_ref[...], 1, 0).astype(BF)
    key_rows = dot(normed, wk_ref[...], 1, 0).astype(BF)
    value_rows = dot(normed, wv_ref[...], 1, 0).astype(BF)
    q_ref[...] = queries
    k_ref[...] = key_rows
    v_ref[...] = value_rows
    scale = head_size**-0.5 * LOG2E
    for first, size, keys, place in blocks:
        scores = dot(key_rows[:keys], stacked(queries, first, size, head_size), 1, 1)
        masks = mask_ref[place : place + keys, :]
        parts = []
        for head in range(per):
            own = scores[:, head * size : (head + 1) * size] * scale + masks
            terms = jnp.exp2(own - jnp.max(own, axis=0, keepdims=True))
            probs = (terms * (1.0 / jnp.sum(terms, axis=0, keepdims=True))).astype(BF)
            probs_ref[head, place : place + keys, :] = probs
            parts.append(probs)
        mixed = dot(jnp.concatenate(parts, 1), value_rows[:keys], 0, 0)
        mixed_ref[first : first + size, :] = picked(mixed, size, head_size).astype(BF)
    stream_ref[...] += dot(mixed_ref[...], wo_ref[...], 1, 0)

    @pl.when(step == pl.num_programs(0) - 1)
    def _():
        picks = as_column(slots_ref[...]) == lax.broadcasted_iota(jnp.int32, (count, count), 1)
        ordered_ref[...] = dot(picks.astype(BF), stream_ref[...].astype(BF), 1, 0).astype(BF)


def attention_forward(tokens, gain, bias, segment, slots, wq, wk, wv, wo):
    count, width = tokens.shape
    head_size = width // HEADS
    per = GROUP // head_size
    blocks, area = query_blocks(count)
    size = blocks[0][1]
    columns = pl.BlockSpec((width, GROUP), lambda g: (0, g))
    part = pl.BlockSpec((count, GROUP), lambda g: (0, g))
    all_rows = fixed(count, width)
    return kernel_call(
        functools.partial(attention_kernel, head_size),
        "attention_forward",
        grid=(width // GROUP,),
        in_specs=[all_rows, fixed(1, width), fixed(1, width), fixed(1, count), fixed(1, count)]
        + [columns] * 3
        + [pl.BlockSpec((GROUP, width), lambda g: (g, 0))],
        out_specs=[all_rows, part, part, part, part]
        + [pl.BlockSpec((per, area, size), lambda g: (g, 0, 0)), all_rows, all_rows],
        out_shape=[shaped((count, width), BF)] * 5
        + [shaped((HEADS, area, size), BF), shaped((count, width), F32)]
        + [shaped((count, width), BF)],
        scratch_shapes=[pltpu.VMEM((area, size), F32)],
    )(tokens, gain, bias, segment, slots, wq, wk, wv, wo)


def backward_kernel(head_size, first_call, last_call, *refs):
    attended_ref, normed_ref, q_ref, k_ref, v_ref, mixed_ref, probs_ref = refs[:7]
    wo_ref, wq_ref, wk_ref, wv_ref, place_ref = refs[7:12]
    refs = refs[12:]
    if not first_call:
        before_ref, refs = refs[0], refs[1:]
    if last_call:
        tokens_ref, gain_ref, grad_stream_ref, send_ref, keep_ref, grad_ref, sums_ref = refs[:7]
        whole_ref, total_ref = refs[7:]
    else:
        send_ref, keep_ref, total_ref, whole_ref = refs
    step = pl.program_id(0)
    count = attended_ref.shape[0]
    blocks, _ = query_blocks(count)
    per = GROUP // head_size

    @pl.when(step == 0)
    def _():
        total_ref[...] = jnp.zeros_like(total_ref) if first_call else before_ref[...]

    queries, key_rows, value_rows = q_ref[...], k_ref[...], v_ref[...]
    grad_mixed = dot(attended_ref[...], wo_ref[...], 1, 1).astype(BF)
    products = grad_mixed.astype(F32) * mixed_ref[...].astype(F32)
    high = products.astype(BF)
    low = (products - high.astype(F32)).astype(BF)
    lane = lax.broadcasted_iota(jnp.int32, (16, GROUP), 1) // head_size
    heads = (lane == lax.broadcasted_iota(jnp.int32, (16, GROUP), 0)).astype(BF)
    centre = dot(heads, high, 1, 1) + dot(heads, low, 1, 1)
    grad_q = []
    grad_k = jnp.zeros((count, GROUP), F32)
    grad_v = jnp.zeros((count, GROUP), F32)
    for first, size, keys, place in blocks:
        grads = stacked(grad_mixed, first, size, head_size)
        grad_probs = dot(value_rows[:keys], grads, 1, 1)
        probs, scores = [], []
        for head in range(per):
            own = probs_ref[head, place : place + keys, :]
            off = grad_probs[:, head * size : (head + 1) * size]
            off = off - centre[head : head + 1, first : first + size]
            probs.append(own)
            scores.append((own.astype(F32) * off).astype(BF))
        probs = jnp.concatenate(probs, 1)
        scores = jnp.concatenate(scores, 1)
        grad_q.append(picked(dot(scores, key_rows[:keys], 0, 0), size, head_size))
        more_v = dot(probs, grads, 1, 0)
        more_k = dot(scores, stacked(queries, first, size, head_size), 1, 0)
        if keys < count:
            rest = jnp.zeros((count - keys, GROUP), F32)
            more_v = jnp.concatenate([more_v, rest], 0)
            more_k = jnp.concatenate([more_k, rest], 0)
        grad_v = grad_v + more_v
        grad_k = grad_k + more_k
    scale = head_size**-0.5
    grad_q = (jnp.concatenate(grad_q, 0) * scale).astype(BF)
    grad_k = (grad_k * scale).astype(BF)
    grad_v = grad_v.astype(BF)
    joined = jnp.concatenate([grad_q, grad_k, grad_v], 1)
    whole_ref[...] = dot(normed_ref[...], joined, 0, 0).astype(BF)
    split_cores(whole_ref, place_ref, send_ref, keep_ref)
    total_ref[...] += (
        dot(grad_q, wq_ref[...], 1, 1)
        + dot(grad_k, wk_ref[...], 1, 1)
        + dot(grad_v, wv_ref[...], 1, 1)
    )

    if last_call:

        @pl.when(step == pl.num_programs(0) - 1)
        def _():
            unit, inverse = standardized(tokens_ref[...].astype(F32))
            total = total_ref[...]
            sums_ref[0:1, :] = jnp.sum(total * unit, axis=0, keepdims=True)
            sums_ref[1:2, :] = jnp.sum(total, axis=0, keepdims=True)
            grad = norm_backward(total * gain_ref[...].astype(F32), unit, inverse)
            grad_ref[...] = (grad_stream_ref[...] + grad).astype(BF)


def attention_backward(groups, saved, attended, weights, place, copies, before=None, end=None):
    normed, q, k, v, mixed, probs = saved
    count, width = attended.shape
    head_size = width // HEADS
    _, area, size = probs.shape
    start, stop = groups
    first_call, last_call = before is None, end is not None
    all_rows = fixed(count, width)
    part = pl.BlockSpec((count, GROUP), lambda g: (0, start + g))
    columns = pl.BlockSpec((width, GROUP), lambda g: (0, start + g))
    rows = width // (CORES * copies)
    half = shaped((copies, rows, 3 * GROUP * (stop - start)), BF)
    half_spec = pl.BlockSpec((copies, rows, 3 * GROUP), lambda g: (0, 0, g))
    specs = [all_rows, all_rows, part, part, part, part]
    specs += [pl.BlockSpec((GROUP // head_size, area, size), lambda g: (start + g, 0, 0))]
    specs += [pl.BlockSpec((GROUP, width), lambda g: (start + g, 0)), columns, columns, columns]
    specs += [scalar()]
    operands = [attended, normed, q, k, v, mixed, probs, *weights, place]
    scratch = [pltpu.VMEM((width, 3 * GROUP), BF)]
    if not first_call:
        specs.append(all_rows)
        operands.append(before)
    if last_call:
        specs += [all_rows, fixed(1, width), all_rows]
        operands += end
        outs = [half, half, shaped((count, width), BF), shaped((8, width), F32)]
        out_specs = [half_spec, half_spec, all_rows, fixed(8, width)]
        scratch.append(pltpu.VMEM((count, width), F32))
    else:
        outs = [half, half, shaped((count, width), F32)]
        out_specs = [half_spec, half_spec, all_rows]
    return kernel_call(
        functools.partial(backward_kernel, head_size, first_call, last_call),
        "attention_backward",
        grid=(stop - start,),
        in_specs=specs,
        out_specs=out_specs,
        out_shape=outs,
        scratch_shapes=scratch,
    )(*operands)


def times_out_kernel(rows_ref, wout_ref, out_ref):
    out_ref[...] = dot(rows_ref[...], wout_ref[...], 1, 1).astype(BF)


def times_out(rows, wout):
    count, width = rows.shape
    hidden = wout.shape[0]
    tile = min(TILE, hidden)
    return kernel_call(
        times_out_kernel,
        "rows_times_w_out",
        grid=(hidden // tile,),
        in_specs=[fixed(count, width), pl.BlockSpec((tile, width), lambda i: (i, 0))],
        out_specs=pl.BlockSpec((count, tile), lambda i: (0, i)),
        out_shape=shaped((count, hidden), BF),
    )(rows, wout)


def expert_kernel(
    own, rows_ref, cot_ref, u_ref, win_ref, gain_ref, bias_ref, center_ref, *refs
):
    if own:
        (active_ref, hidden_ref, normed_ref, produced_ref, gate_ref, grad_ref, sums_ref) = refs[:7]
        unit_ref, total_ref, score_ref = refs[7:]
    else:
        active_ref, hidden_ref, normed_ref, produced_ref, gate_ref = refs
    step = pl.program_id(0)
    count = rows_ref.shape[0]

    @pl.when(step == 0)
    def _():
        rows = rows_ref[...].astype(F32)
        unit, _ = standardized(rows)
        normed = unit * gain_ref[...].astype(F32) + bias_ref[...].astype(F32)
        normed_ref[...] = normed.astype(BF)
        score = jnp.sum(rows * center_ref[...].astype(F32), axis=-1, keepdims=True)
        gating = 1.0 / (1.0 + jnp.exp(-score))
        gate_ref[...] = jnp.broadcast_to(gating, gate_ref.shape)
        produced_ref[...] = (gating * cot_ref[...].astype(F32)).astype(BF)
        if own:
            unit_ref[...] = unit
            total_ref[...] = jnp.zeros_like(total_ref)
            score_ref[...] = jnp.zeros_like(score_ref)

    weight = win_ref[...]
    hidden = dot(normed_ref[...], weight, 1, 0)
    square = hidden * hidden
    curve = jnp.tanh(hidden * (0.7978845608028654 + 0.7978845608028654 * 0.044715 * square))
    half = 0.5 + 0.5 * curve
    active = (hidden * half).astype(BF)
    active_ref[...] = active
    slope = half + hidden * (0.5 - 0.5 * curve * curve) * (
        0.7978845608028654 + 0.7978845608028654 * 3 * 0.044715 * square
    )
    u = u_ref[...].astype(F32)
    grad_hidden = (slope * (u * gate_ref[:, :1])).astype(BF)
    hidden_ref[...] = grad_hidden
    if own:
        products = active.astype(F32) * u
        lanes = score_ref.shape[1]
        score_ref[...] += sum(
            products[:, at : at + lanes] for at in range(0, products.shape[1], lanes)
        )
        total_ref[...] += dot(grad_hidden, weight, 1, 1)

        @pl.when(step == pl.num_programs(0) - 1)
        def _():
            rows = rows_ref[...].astype(F32)
            unit = unit_ref[...]
            _, inverse = standardized(rows)
            total = total_ref[...]
            gating = gate_ref[:, :1]
            grad_gating = jnp.sum(score_ref[...], axis=-1, keepdims=True)
            grad_score = grad_gating * gating * (1.0 - gating)
            sums_ref[0:1, :] = jnp.sum(total * unit, axis=0, keepdims=True)
            sums_ref[1:2, :] = jnp.sum(total, axis=0, keepdims=True)
            sums_ref[2:3, :] = jnp.sum(rows * grad_score, axis=0, keepdims=True)
            grad = norm_backward(total * gain_ref[...].astype(F32), unit, inverse)
            grad_ref[...] = (grad + grad_score * center_ref[...].astype(F32)).astype(BF)


def expert_pass(own, rows, cot, u, win, gain, bias, center):
    count, width = rows.shape
    hidden = win.shape[1]
    tile = min(TILE, hidden)
    all_rows = fixed(count, width)
    tiles = pl.BlockSpec((count, tile), lambda i: (0, i))
    lanes = 128
    outs = [shaped((count, hidden), BF)] * 2 + [shaped((count, width), BF)] * 2
    outs += [shaped((count, lanes), F32)]
    out_specs = [tiles, tiles, all_rows, all_rows, fixed(count, lanes)]
    scratch = []
    if own:
        outs += [shaped((count, width), BF), shaped((8, width), F32)]
        out_specs += [all_rows, fixed(8, width)]
        scratch = [pltpu.VMEM((count, width), F32)] * 2 + [pltpu.VMEM((count, lanes), F32)]
    return kernel_call(
        functools.partial(expert_kernel, own),
        "expert_own" if own else "expert_other",
        grid=(hidden // tile,),
        in_specs=[all_rows, all_rows, tiles, pl.BlockSpec((width, tile), lambda i: (0, i))]
        + [fixed(1, width)] * 3,
        out_specs=out_specs,
        out_shape=outs,
        scratch_shapes=scratch,
    )(rows, cot, u, win, gain, bias, center)


def branch_kernel(active_ref, wout_ref, gate_ref, out_ref, total_ref):
    step = pl.program_id(0)

    @pl.when(step == 0)
    def _():
        total_ref[...] = jnp.zeros_like(total_ref)

    total_ref[...] += dot(active_ref[...], wout_ref[...], 1, 0)

    @pl.when(step == pl.num_programs(0) - 1)
    def _():
        out_ref[...] = (total_ref[...] * gate_ref[:, :1]).astype(BF)


def branch_rows(active, wout, gating):
    count, hidden = active.shape
    width = wout.shape[1]
    tile = min(2 * TILE, hidden)
    return kernel_call(
        branch_kernel,
        "branch",
        grid=(hidden // tile,),
        in_specs=[
            pl.BlockSpec((count, tile), lambda i: (0, i)),
            pl.BlockSpec((tile, width), lambda i: (i, 0)),
            fixed(*gating.shape),
        ],
        out_specs=fixed(count, width),
        out_shape=shaped((count, width), BF),
        scratch_shapes=[pltpu.VMEM((count, width), F32)],
    )(active, wout, gating)


def product_kernel(copy_ref, left_ref, left_other_ref, right_ref, right_other_ref, out_ref):
    del copy_ref
    out_ref[...] = dot(left_ref[...], right_ref[...], 0, 0) + dot(
        left_other_ref[...], right_other_ref[...], 0, 0
    )


def grad_in(copy, copies, normed, normed_other, hidden, hidden_other):
    count, width = normed.shape
    part = width // copies
    tile = min(2 * TILE, hidden.shape[1])
    left = pl.BlockSpec((count, part), lambda i, copy: (0, copy[0]))
    right = pl.BlockSpec((count, tile), lambda i, copy: (0, i))
    return kernel_call(
        product_kernel,
        "grad_w_in",
        grid_spec=pltpu.PrefetchScalarGridSpec(
            num_scalar_prefetch=1,
            grid=(hidden.shape[1] // tile,),
            in_specs=[left, left, right, right],
            out_specs=pl.BlockSpec((part, tile), lambda i, copy: (0, i)),
        ),
        out_shape=shaped((part, hidden.shape[1]), F32),
    )(copy, normed, normed_other, hidden, hidden_other)


def grad_out(copy, copies, active, active_other, produced, produced_other):
    count, width = produced.shape
    part = active.shape[1] // copies
    tile = min(TILE, part)
    tiles = part // tile
    left = pl.BlockSpec((count, tile), lambda i, copy: (0, copy[0] * tiles + i))
    right = pl.BlockSpec((count, width), lambda i, copy: (0, 0))
    return kernel_call(
        product_kernel,
        "grad_w_out",
        grid_spec=pltpu.PrefetchScalarGridSpec(
            num_scalar_prefetch=1,
            grid=(tiles,),
            in_specs=[left, left, right, right],
            out_specs=pl.BlockSpec((tile, width), lambda i, copy: (i, 0)),
        ),
        out_shape=shaped((part, width), F32),
    )(copy, active, active_other, produced, produced_other)


def expert_stages(size):
    rest = size // CORES
    middle = 1
    while (2 * middle) ** 2 <= rest and rest % (2 * middle) == 0:
        middle *= 2
    return [(1, CORES), (CORES, middle), (CORES * middle, rest // middle)]


def turned(axis, stride, length, step):
    pairs = []
    for index in range(lax.axis_size(axis)):
        place = (index // stride) % length
        pairs.append((index, index + ((place + step) % length - place) * stride))
    return pairs


def scatter_level(rows, axis, stride, length):
    place = (lax.axis_index(axis) // stride) % length
    count = rows.shape[0] // length
    total = lax.dynamic_slice_in_dim(rows, place * count, count, 0).astype(F32)
    for step in range(1, length):
        part = lax.dynamic_slice_in_dim(rows, ((place + step) % length) * count, count, 0)
        part = lax.ppermute(part, axis, turned(axis, stride, length, step))
        total = total + part.astype(F32)
    return total.astype(rows.dtype)


def gather_level(rows, axis, stride, length):
    place = (lax.axis_index(axis) // stride) % length
    count = rows.shape[0]
    parts = [rows] + [
        lax.ppermute(rows, axis, turned(axis, stride, length, step)) for step in range(1, length)
    ]
    if length == 2:
        return jnp.where(
            place == 0, jnp.concatenate(parts, 0), jnp.concatenate([parts[1], parts[0]], 0)
        )
    whole = jnp.zeros((length * count, rows.shape[1]), rows.dtype)
    for step, part in enumerate(parts):
        whole = lax.dynamic_update_slice_in_dim(whole, part, ((place - step) % length) * count, 0)
    return whole


def total_rows(send, keep):
    copies, _, columns = send.shape
    levels = expert_stages(lax.axis_size("expert"))
    got = lax.ppermute(send, "expert", turned("expert", 1, CORES, 1))
    held = (keep.astype(F32) + got.astype(F32)).astype(BF).reshape(-1, columns)
    held = scatter_level(held, "batch", 1, copies)
    for stride, length in levels[1:]:
        held = scatter_level(held, "expert", stride, length)
    for stride, length in reversed(levels):
        held = gather_level(held, "expert", stride, length)
    return held


def total_small(values):
    copies = lax.axis_size("batch")
    owners = lax.axis_size("expert")
    place = lax.axis_index("batch")
    total = lax.dynamic_index_in_dim(values, place, 0, True)
    for step in range(1, copies):
        part = lax.dynamic_index_in_dim(values, (place + step) % copies, 0, True)
        total = total + lax.ppermute(part, "batch", turned("batch", 1, copies, step))
    bit = 1
    while bit < owners:
        total = total + lax.ppermute(total, "expert", [(i, i ^ bit) for i in range(owners)])
        bit *= 2
    return total[0]


def local(
    tokens,
    cotangent,
    segment_ids,
    routing,
    ln_gain,
    ln_bias,
    w_query,
    w_key,
    w_value,
    w_output,
    expert_gain,
    expert_bias,
    centroid,
    w_in,
    w_out,
):
    count, width = tokens.shape
    owners = lax.axis_size("expert")
    copies = lax.axis_size("batch")
    copy = lax.axis_index("batch")
    place = (lax.axis_index("expert") % CORES).astype(jnp.int32)[None]
    send_rows = count // owners
    win = w_in[0]
    wout = w_out[0]

    def exchanged(values):
        return lax.all_to_all(
            values.reshape(owners, send_rows, width),
            "expert",
            split_axis=0,
            concat_axis=0,
            tiled=True,
        ).reshape(count, width)

    def from_copy(values, step):
        return lax.ppermute(values, "batch", turned("batch", 1, copies, step))

    paired = copies == 2
    cot_rows = exchanged(order_rows(cotangent, routing))
    *saved, stream, ordered = attention_forward(
        tokens,
        ln_gain[None],
        ln_bias[None],
        segment_ids,
        routing,
        w_query,
        w_key,
        w_value,
        w_output,
    )
    mixed = saved[4]
    rows = exchanged(ordered)
    u = times_out(cot_rows, wout)
    vectors = (expert_gain, expert_bias, centroid)
    active, grad_hidden, expert_normed, grad_produced, gating, grad_rows, sums = expert_pass(
        True, rows, cot_rows, u, win, *vectors
    )
    grad_returned = exchanged(grad_rows)
    branch = branch_rows(active, wout, gating)
    outputs = output_rows(exchanged(branch), routing, stream)

    small = sums[:3].reshape(3, copies, width // copies)
    small_total = lax.dynamic_index_in_dim(small, copy, 1, False)
    for step in range(1, copies):
        away = lax.dynamic_index_in_dim(small, (copy + step) % copies, 1, False)
        small_total = small_total + from_copy(away, step)
    if paired:
        cot_other = from_copy(cot_rows, 1)
        rows_other = from_copy(rows, 1)
        active_o, hidden_o, normed_o, produced_o, _ = expert_pass(
            False, rows_other, cot_other, times_out(cot_other, wout), win, *vectors
        )
        which = copy.astype(jnp.int32)[None]
        grad_w_in = grad_in(which, copies, expert_normed, normed_o, grad_hidden, hidden_o)
        grad_w_out = grad_out(which, copies, active, active_o, grad_produced, produced_o)
    else:
        grad_w_in, grad_w_out = (
            lax.psum_scatter(
                dot(left, right, 0, 0).astype(BF), "batch", scatter_dimension=0, tiled=True
            ).astype(F32)
            for left, right in ((expert_normed, grad_hidden), (active, grad_produced))
        )

    grad_stream, attended, send, keep = gradient_entry(
        grad_returned, routing, cotangent, mixed, place, copies
    )
    grad_wo = total_rows(send, keep).astype(F32)
    weights = (w_output, w_query, w_key, w_value)
    groups = width // GROUP
    middle = groups // 2
    send, keep, before = attention_backward(
        (0, middle), saved, attended, weights, place, copies
    )
    first = total_rows(send, keep)
    send, keep, grad_tokens, norm_sums = attention_backward(
        (middle, groups),
        saved,
        attended,
        weights,
        place,
        copies,
        before,
        [tokens, ln_gain[None], grad_stream],
    )
    second = total_rows(send, keep)
    parts = jnp.concatenate([first, second], 1).astype(F32)
    parts = parts.reshape(-1, groups, 3, GROUP)
    grad_wq, grad_wk, grad_wv = (parts[:, :, i].reshape(-1, width) for i in range(3))

    gate_vector = jnp.where(
        jnp.arange(owners) == lax.axis_index("expert"),
        jnp.sum(gating[:, 0]) / (count * copies),
        0.0,
    )
    part = width // copies
    packed = total_small(
        jnp.concatenate(
            [
                norm_sums[0].reshape(copies, -1),
                norm_sums[1].reshape(copies, -1),
                gate_vector.reshape(copies, -1),
            ],
            axis=1,
        )
    )
    return (
        outputs,
        grad_tokens,
        packed[:part],
        packed[part : 2 * part],
        grad_wq,
        grad_wk,
        grad_wv,
        grad_wo,
        small_total[0][None],
        small_total[1][None],
        small_total[2][None],
        grad_w_in[None],
        grad_w_out[None],
        packed[2 * part :],
    )


def solution(mesh):
    both = P(("expert", "batch"), None)
    per_expert = P("expert", None)
    matrices = P("expert", None, None)
    return jax.shard_map(
        local,
        mesh=mesh,
        in_specs=(both,) * 4 + (P(),) * 6 + (per_expert,) * 3 + (matrices,) * 2,
        out_specs=(both, both)
        + (P("batch"),) * 2
        + (P("batch", None),) * 4
        + (P("expert", "batch"),) * 3
        + (P("expert", "batch", None),) * 2
        + (P("batch"),),
        check_vma=False,
    )
```

```python
import functools

import jax
import jax.numpy as jnp
from jax import lax
from jax.experimental import pallas as pl
from jax.experimental.pallas import tpu as pltpu
from jax.sharding import PartitionSpec as P

HEADS = 16
NORM_EPSILON = 1e-05
NEG_FILL = -1e30
LOG2E = 1.4426950408889634
GROUP = 256
CORES = 2
TILE = 512
BF = jnp.bfloat16
F32 = jnp.float32


def dot(a, b, ca, cb):
    return lax.dot_general(a, b, (((ca,), (cb,)), ((), ())), preferred_element_type=F32)


def kernel_call(body, name, operands, micros, after=(), mib=60, in_specs=None, grid_spec=None, **more):
    given, extra = len(operands), len(after)

    def run(*refs):
        body(*refs[:given], *refs[given + extra :])

    unread = [anywhere()] * extra
    if grid_spec is not None:
        prefetched, grid, in_specs, out_specs = grid_spec
        more["grid_spec"] = pltpu.PrefetchScalarGridSpec(
            num_scalar_prefetch=prefetched,
            grid=grid,
            in_specs=in_specs + unread,
            out_specs=out_specs,
            scratch_shapes=more.pop("scratch_shapes", ()),
        )
    else:
        if in_specs is None:
            in_specs = [in_vmem()] * given
        more["in_specs"] = in_specs + unread
    return pl.pallas_call(
        run,
        name=name,
        compiler_params=pltpu.CompilerParams(vmem_limit_bytes=mib << 20),
        cost_estimate=pl.CostEstimate(
            flops=int(micros * 1.15e9), transcendentals=0, bytes_accessed=0
        ),
        **more,
    )(*operands, *after)


def shaped(shape, kind):
    return jax.ShapeDtypeStruct(shape, kind)


def fixed(*shape):
    return pl.BlockSpec(shape, lambda *place: (0,) * len(shape))


def in_vmem():
    return pl.BlockSpec(memory_space=pltpu.VMEM)


def anywhere():
    return pl.BlockSpec(memory_space=pl.ANY)


def scalar():
    return pl.BlockSpec(memory_space=pltpu.SMEM)


def as_column(row):
    return jnp.transpose(jnp.broadcast_to(row, (8, row.shape[1])))[:, :1]


def standardized(values):
    center = values - jnp.mean(values, axis=-1, keepdims=True)
    spread = jnp.mean(center * center, axis=-1, keepdims=True)
    inverse = lax.rsqrt(spread + NORM_EPSILON)
    return center * inverse, inverse


def norm_backward(grad, unit, inverse):
    mean = jnp.mean(grad, axis=-1, keepdims=True)
    slope = jnp.mean(grad * unit, axis=-1, keepdims=True)
    return inverse * (grad - mean - unit * slope)


def query_blocks(count):
    size = min(256, count)
    blocks, place = [], 0
    for first in range(0, count, size):
        blocks.append((first, size, first + size, place))
        place += first + size
    return blocks, place


def stacked(part, first, size, head_size):
    lane = lax.broadcasted_iota(jnp.int32, (1, GROUP), 1) // head_size
    rows = part[first : first + size]
    return jnp.concatenate(
        [
            jnp.where(lane == head, rows, jnp.zeros_like(rows))
            for head in range(GROUP // head_size)
        ],
        0,
    )


def picked(rows, size, head_size):
    lane = lax.broadcasted_iota(jnp.int32, (1, GROUP), 1) // head_size
    out = rows[:size]
    for head in range(1, GROUP // head_size):
        out = jnp.where(lane == head, rows[head * size : (head + 1) * size], out)
    return out


def split_cores(whole_ref, place_ref, send_ref, keep_ref):
    copies, rows, _ = send_ref.shape
    place = place_ref[0]
    for copy in range(copies):
        start = copy * CORES * rows
        keep = pl.multiple_of(start + place * rows, rows)
        send = pl.multiple_of(start + (1 - place) * rows, rows)
        keep_ref[copy] = whole_ref[pl.ds(keep, rows), :]
        send_ref[copy] = whole_ref[pl.ds(send, rows), :]


def order_kernel(values_ref, slots_ref, ordered_ref):
    count = values_ref.shape[0]
    picks = as_column(slots_ref[...]) == lax.broadcasted_iota(jnp.int32, (count, count), 1)
    ordered_ref[...] = dot(picks.astype(BF), values_ref[...], 1, 0).astype(BF)


def order_rows(values, slots):
    return kernel_call(
        order_kernel, "order_rows", (values, slots), 3, out_shape=shaped(values.shape, BF)
    )


def restored(slots_ref, returned_ref):
    count = returned_ref.shape[0]
    picks = slots_ref[...] == lax.broadcasted_iota(jnp.int32, (count, count), 0)
    return dot(picks.astype(BF), returned_ref[...], 1, 0)


def output_kernel(returned_ref, slots_ref, stream_ref, out_ref):
    out_ref[...] = (stream_ref[...] + restored(slots_ref, returned_ref)).astype(BF)


def output_rows(returned, slots, stream):
    return kernel_call(
        output_kernel,
        "output_rows",
        (returned, slots, stream),
        4,
        out_shape=shaped(returned.shape, BF),
    )


def entry_kernel(
    returned_ref,
    slots_ref,
    cot_ref,
    mixed_ref,
    place_ref,
    stream_ref,
    attended_ref,
    send_ref,
    keep_ref,
    whole_ref,
):
    stream = cot_ref[...].astype(F32) + restored(slots_ref, returned_ref)
    stream_ref[...] = stream
    attended = stream.astype(BF)
    attended_ref[...] = attended
    whole_ref[...] = dot(mixed_ref[...], attended, 0, 0).astype(BF)
    split_cores(whole_ref, place_ref, send_ref, keep_ref)


def gradient_entry(returned, slots, cot, mixed, place, copies, after):
    count, width = cot.shape
    half = (copies, width // (CORES * copies), width)
    return kernel_call(
        entry_kernel,
        "gradient_entry",
        (returned, slots, cot, mixed, place),
        5,
        after,
        grid=(1,),
        in_specs=[fixed(count, width), fixed(1, count), fixed(count, width), fixed(count, width)]
        + [scalar()],
        out_specs=[fixed(count, width), fixed(count, width), fixed(*half), fixed(*half)],
        out_shape=[shaped((count, width), F32), shaped((count, width), BF)] + [shaped(half, BF)] * 2,
        scratch_shapes=[pltpu.VMEM((width, width), BF)],
    )


def attention_kernel(
    head_size,
    tokens_ref,
    gain_ref,
    bias_ref,
    segment_ref,
    slots_ref,
    wq_hbm,
    wk_hbm,
    wv_hbm,
    wo_hbm,
    normed_hbm,
    q_hbm,
    k_hbm,
    v_hbm,
    mixed_hbm,
    probs_hbm,
    stream_hbm,
    ordered_ref,
    mask_ref,
    weight_ref,
    normed_ref,
    q_ref,
    k_ref,
    v_ref,
    mixed_ref,
    probs_ref,
    stream_ref,
    in_sem,
    out_sem,
):
    count, width = tokens_ref.shape
    blocks, _ = query_blocks(count)
    per = GROUP // head_size
    weights = [
        pltpu.make_async_copy(array, weight_ref.at[i], in_sem.at[i])
        for i, array in enumerate((wq_hbm, wk_hbm, wv_hbm, wo_hbm))
    ]
    for copy in weights:
        copy.start()
    sent = []

    def send(buffer_ref, array_ref):
        sent.append(pltpu.make_async_copy(buffer_ref, array_ref, out_sem.at[len(sent)]))
        sent[-1].start()

    values = tokens_ref[...].astype(F32)
    unit, _ = standardized(values)
    normed = unit * gain_ref[...].astype(F32) + bias_ref[...].astype(F32)
    normed_ref[...] = normed.astype(BF)
    send(normed_ref, normed_hbm)
    segment = segment_ref[...]
    column = as_column(segment)
    for first, size, keys, place in blocks:
        shape = (keys, size)
        query = first + lax.broadcasted_iota(jnp.int32, shape, 1)
        later = lax.broadcasted_iota(jnp.int32, shape, 0) <= query
        same = column[:keys] == segment[:, first : first + size]
        mask_ref[place : place + keys, :] = jnp.where(later & same, 0.0, NEG_FILL)

    for i, (out_ref, out_hbm) in enumerate(((q_ref, q_hbm), (k_ref, k_hbm), (v_ref, v_hbm))):
        weights[i].wait()
        out_ref[...] = dot(normed_ref[...], weight_ref[i], 1, 0).astype(BF)
        send(out_ref, out_hbm)
    scale = head_size**-0.5 * LOG2E
    for group in range(width // GROUP):
        lanes = slice(group * GROUP, (group + 1) * GROUP)
        queries = q_ref[:, lanes]
        for first, size, keys, place in blocks:
            scores = dot(k_ref[:keys, lanes], stacked(queries, first, size, head_size), 1, 1)
            masks = mask_ref[place : place + keys, :]
            parts = []
            for head in range(per):
                own = scores[:, head * size : (head + 1) * size] * scale + masks
                terms = jnp.exp2(own - jnp.max(own, axis=0, keepdims=True))
                probs = (terms * (1.0 / jnp.sum(terms, axis=0, keepdims=True))).astype(BF)
                probs_ref[group * per + head, place : place + keys, :] = probs
                parts.append(probs)
            mixed = dot(jnp.concatenate(parts, 1), v_ref[:keys, lanes], 0, 0)
            mixed_ref[first : first + size, lanes] = picked(mixed, size, head_size).astype(BF)
        heads = pl.ds(group * per, per)
        send(probs_ref.at[heads], probs_hbm.at[heads])
    send(mixed_ref, mixed_hbm)
    weights[3].wait()
    stream = tokens_ref[...].astype(F32) + dot(mixed_ref[...], weight_ref[3], 1, 0)
    stream_ref[...] = stream
    send(stream_ref, stream_hbm)
    picks = as_column(slots_ref[...]) == lax.broadcasted_iota(jnp.int32, (count, count), 1)
    ordered_ref[...] = dot(picks.astype(BF), stream.astype(BF), 1, 0).astype(BF)
    for copy in sent:
        copy.wait()


def attention_forward(tokens, gain, bias, segment, slots, wq, wk, wv, wo):
    count, width = tokens.shape
    blocks, area = query_blocks(count)
    size = blocks[0][1]
    rows = [shaped((count, width), BF)] * 5
    kept = rows + [shaped((HEADS, area, size), BF), shaped((count, width), F32)]
    return kernel_call(
        functools.partial(attention_kernel, width // HEADS),
        "attention_forward",
        (tokens, gain, bias, segment, slots, wq, wk, wv, wo),
        17,
        in_specs=[in_vmem()] * 5 + [anywhere()] * 4,
        out_specs=[anywhere()] * 7 + [in_vmem()],
        out_shape=kept + [shaped((count, width), BF)],
        scratch_shapes=[pltpu.VMEM((area, size), F32), pltpu.VMEM((4, width, width), BF)]
        + [pltpu.VMEM(array.shape, array.dtype) for array in kept]
        + [pltpu.SemaphoreType.DMA((4,)), pltpu.SemaphoreType.DMA((6 + width // GROUP,))],
    )


def backward_kernel(head_size, first_call, last_call, *refs):
    attended_ref, normed_ref, q_ref, k_ref, v_ref, mixed_ref, probs_ref = refs[:7]
    wo_ref, wq_ref, wk_ref, wv_ref, place_ref = refs[7:12]
    refs = refs[12:]
    if not first_call:
        before_ref, refs = refs[0], refs[1:]
    if last_call:
        tokens_ref, gain_ref, grad_stream_ref, send_ref, keep_ref, grad_ref, sums_ref = refs[:7]
        whole_ref, total_ref = refs[7:]
    else:
        send_ref, keep_ref, total_ref, whole_ref = refs
    step = pl.program_id(0)
    count = attended_ref.shape[0]
    blocks, _ = query_blocks(count)
    per = GROUP // head_size

    @pl.when(step == 0)
    def _():
        total_ref[...] = jnp.zeros_like(total_ref) if first_call else before_ref[...]

    queries, key_rows, value_rows = q_ref[...], k_ref[...], v_ref[...]
    grad_mixed = dot(attended_ref[...], wo_ref[...], 1, 1).astype(BF)
    products = grad_mixed.astype(F32) * mixed_ref[...].astype(F32)
    high = products.astype(BF)
    low = (products - high.astype(F32)).astype(BF)
    lane = lax.broadcasted_iota(jnp.int32, (16, GROUP), 1) // head_size
    heads = (lane == lax.broadcasted_iota(jnp.int32, (16, GROUP), 0)).astype(BF)
    centre = dot(heads, high, 1, 1) + dot(heads, low, 1, 1)
    grad_q = []
    grad_k = jnp.zeros((count, GROUP), F32)
    grad_v = jnp.zeros((count, GROUP), F32)
    for first, size, keys, place in blocks:
        grads = stacked(grad_mixed, first, size, head_size)
        grad_probs = dot(value_rows[:keys], grads, 1, 1)
        probs, scores = [], []
        for head in range(per):
            own = probs_ref[head, place : place + keys, :]
            off = grad_probs[:, head * size : (head + 1) * size]
            off = off - centre[head : head + 1, first : first + size]
            probs.append(own)
            scores.append((own.astype(F32) * off).astype(BF))
        probs = jnp.concatenate(probs, 1)
        scores = jnp.concatenate(scores, 1)
        grad_q.append(picked(dot(scores, key_rows[:keys], 0, 0), size, head_size))
        more_v = dot(probs, grads, 1, 0)
        more_k = dot(scores, stacked(queries, first, size, head_size), 1, 0)
        if keys < count:
            rest = jnp.zeros((count - keys, GROUP), F32)
            more_v = jnp.concatenate([more_v, rest], 0)
            more_k = jnp.concatenate([more_k, rest], 0)
        grad_v = grad_v + more_v
        grad_k = grad_k + more_k
    scale = head_size**-0.5
    grad_q = (jnp.concatenate(grad_q, 0) * scale).astype(BF)
    grad_k = (grad_k * scale).astype(BF)
    grad_v = grad_v.astype(BF)
    joined = jnp.concatenate([grad_q, grad_k, grad_v], 1)
    whole_ref[...] = dot(normed_ref[...], joined, 0, 0).astype(BF)
    split_cores(whole_ref, place_ref, send_ref, keep_ref)
    total_ref[...] += (
        dot(grad_q, wq_ref[...], 1, 1)
        + dot(grad_k, wk_ref[...], 1, 1)
        + dot(grad_v, wv_ref[...], 1, 1)
    )

    if last_call:

        @pl.when(step == pl.num_programs(0) - 1)
        def _():
            unit, inverse = standardized(tokens_ref[...].astype(F32))
            total = total_ref[...]
            sums_ref[0:1, :] = jnp.sum(total * unit, axis=0, keepdims=True)
            sums_ref[1:2, :] = jnp.sum(total, axis=0, keepdims=True)
            grad = norm_backward(total * gain_ref[...].astype(F32), unit, inverse)
            grad_ref[...] = (grad_stream_ref[...] + grad).astype(BF)


def attention_backward(groups, saved, attended, weights, place, copies, after, before=None, end=None):
    normed, q, k, v, mixed, probs = saved
    count, width = attended.shape
    head_size = width // HEADS
    _, area, size = probs.shape
    start, stop = groups
    first_call, last_call = before is None, end is not None
    all_rows = fixed(count, width)
    part = pl.BlockSpec((count, GROUP), lambda g: (0, start + g))
    columns = pl.BlockSpec((width, GROUP), lambda g: (0, start + g))
    rows = width // (CORES * copies)
    half = shaped((copies, rows, 3 * GROUP * (stop - start)), BF)
    half_spec = pl.BlockSpec((copies, rows, 3 * GROUP), lambda g: (0, 0, g))
    specs = [all_rows, all_rows, part, part, part, part]
    specs += [pl.BlockSpec((GROUP // head_size, area, size), lambda g: (start + g, 0, 0))]
    specs += [pl.BlockSpec((GROUP, width), lambda g: (start + g, 0)), columns, columns, columns]
    specs += [scalar()]
    operands = [attended, normed, q, k, v, mixed, probs, *weights, place]
    scratch = [pltpu.VMEM((width, 3 * GROUP), BF)]
    if not first_call:
        specs.append(all_rows)
        operands.append(before)
    if last_call:
        specs += [all_rows, fixed(1, width), all_rows]
        operands += end
        outs = [half, half, shaped((count, width), BF), shaped((8, width), F32)]
        out_specs = [half_spec, half_spec, all_rows, fixed(8, width)]
        scratch.append(pltpu.VMEM((count, width), F32))
    else:
        outs = [half, half, shaped((count, width), F32)]
        out_specs = [half_spec, half_spec, all_rows]
    return kernel_call(
        functools.partial(backward_kernel, head_size, first_call, last_call),
        "attention_backward",
        operands,
        8 * (stop - start),
        after,
        grid=(stop - start,),
        in_specs=specs,
        out_specs=out_specs,
        out_shape=outs,
        scratch_shapes=scratch,
    )


def tiles_of(size):
    return [slice(at, at + TILE) for at in range(0, size, TILE)]


class Tiles:
    def __init__(self, array_ref, buffer_ref, sems, axis, inward):
        self.copies = []
        for tile in range(buffer_ref.shape[0]):
            span = pl.ds(tile * TILE, TILE)
            outside = array_ref.at[span, :] if axis == 0 else array_ref.at[:, span]
            ends = (outside, buffer_ref.at[tile]) if inward else (buffer_ref.at[tile], outside)
            self.copies.append(pltpu.make_async_copy(*ends, sems.at[tile]))

    def start(self, tile):
        self.copies[tile].start()

    def wait(self, tile):
        self.copies[tile].wait()


def tile_buffers(*arrays):
    scratch = []
    for rows, columns, axis in arrays:
        count = (columns if axis else rows) // TILE
        shape = (count, rows, TILE) if axis else (count, TILE, columns)
        scratch.append(pltpu.VMEM(shape, BF))
    scratch += [pltpu.SemaphoreType.DMA(buffer.shape[:1]) for buffer in scratch]
    return scratch


def times_out_kernel(rows_ref, wout_hbm, out_hbm, wout_ref, out_ref, wout_sem, out_sem):
    weights = Tiles(wout_hbm, wout_ref, wout_sem, 0, True)
    results = Tiles(out_hbm, out_ref, out_sem, 1, False)
    count = wout_ref.shape[0]
    for tile in range(count):
        weights.start(tile)
    for tile in range(count):
        weights.wait(tile)
        out_ref[tile] = dot(rows_ref[...], wout_ref[tile], 1, 1).astype(BF)
        results.start(tile)
    for tile in range(count):
        results.wait(tile)


def times_out(rows, wout, after=()):
    count, width = rows.shape
    hidden = wout.shape[0]
    return kernel_call(
        times_out_kernel,
        "rows_times_w_out",
        (rows, wout),
        7,
        after,
        in_specs=[in_vmem(), anywhere()],
        out_specs=anywhere(),
        out_shape=shaped((count, hidden), BF),
        scratch_shapes=tile_buffers((hidden, width, 0), (count, hidden, 1)),
    )


def branch_kernel(
    active_hbm, wout_hbm, gate_ref, out_ref, active_ref, wout_ref, active_sem, wout_sem
):
    weights = Tiles(wout_hbm, wout_ref, wout_sem, 0, True)
    actives = Tiles(active_hbm, active_ref, active_sem, 1, True)
    count = wout_ref.shape[0]
    for tile in range(count):
        weights.start(tile)
        actives.start(tile)
    total = None
    for tile in range(count):
        weights.wait(tile)
        actives.wait(tile)
        more = dot(active_ref[tile], wout_ref[tile], 1, 0)
        total = more if total is None else total + more
    out_ref[...] = (total * gate_ref[:, :1]).astype(BF)


def branch_rows(active, wout, gating, after=()):
    count, hidden = active.shape
    width = wout.shape[1]
    return kernel_call(
        branch_kernel,
        "branch",
        (active, wout, gating),
        7,
        after,
        in_specs=[anywhere(), anywhere(), in_vmem()],
        out_shape=shaped((count, width), BF),
        scratch_shapes=tile_buffers((count, hidden, 1), (hidden, width, 0)),
    )


def gelu_parts(hidden):
    slant = 0.7978845608028654
    bend = slant * 0.044715
    square = hidden * hidden
    half = 0.5 + 0.5 * jnp.tanh(hidden * (slant + bend * square))
    active = hidden * half
    return active, half + active * (1.0 - half) * (2 * slant + 6 * bend * square)


def expert_kernel(own, rows_ref, u_hbm, win_hbm, gain_ref, bias_ref, center_ref, *refs):
    active_hbm, hidden_hbm, normed_hbm, gate_ref = refs[:4]
    refs = refs[4:]
    if own:
        grad_ref, sums_ref, unit_ref, total_ref = refs[:4]
        refs = refs[4:]
    normed_ref, normed_sem, u_ref, win_ref, active_ref, hidden_ref = refs[:6]
    u_sem, win_sem, active_sem, hidden_sem = refs[6:]
    weights = Tiles(win_hbm, win_ref, win_sem, 1, True)
    us = Tiles(u_hbm, u_ref, u_sem, 1, True)
    actives = Tiles(active_hbm, active_ref, active_sem, 1, False)
    hiddens = Tiles(hidden_hbm, hidden_ref, hidden_sem, 1, False)
    count = win_ref.shape[0]
    for tile in range(count):
        weights.start(tile)
        us.start(tile)
    rows = rows_ref[...].astype(F32)
    unit, inverse = standardized(rows)
    if own:
        unit_ref[...] = unit
    normed_ref[...] = (unit * gain_ref[...].astype(F32) + bias_ref[...].astype(F32)).astype(BF)
    normed_out = pltpu.make_async_copy(normed_ref, normed_hbm, normed_sem)
    normed_out.start()
    score = jnp.sum(rows * center_ref[...].astype(F32), axis=-1, keepdims=True)
    gating = 1.0 / (1.0 + jnp.exp(-score))
    gate_ref[...] = jnp.broadcast_to(gating, gate_ref.shape)
    lanes = gate_ref.shape[1]
    scores = jnp.zeros((rows.shape[0], lanes), F32)
    for tile in range(count):
        weights.wait(tile)
        us.wait(tile)
        active, slope = gelu_parts(dot(normed_ref[...], win_ref[tile], 1, 0))
        active = active.astype(BF)
        active_ref[tile] = active
        actives.start(tile)
        u = u_ref[tile].astype(F32)
        hidden_ref[tile] = (slope * (u * gate_ref[:, :1])).astype(BF)
        hiddens.start(tile)
        if own:
            products = active.astype(F32) * u
            for place in range(0, products.shape[1], lanes):
                scores = scores + products[:, place : place + lanes]
            more = dot(hidden_ref[tile], win_ref[tile], 1, 1)
            if tile:
                total_ref[...] += more
            else:
                total_ref[...] = more
    if own:
        total = total_ref[...]
        gating = gate_ref[:, :1]
        grad_gating = jnp.sum(scores, axis=-1, keepdims=True)
        grad_score = grad_gating * gating * (1.0 - gating)
        unit = unit_ref[...]
        rows = rows_ref[...].astype(F32)
        sums_ref[0:1, :] = jnp.sum(total * unit, axis=0, keepdims=True)
        sums_ref[1:2, :] = jnp.sum(total, axis=0, keepdims=True)
        sums_ref[2:3, :] = jnp.sum(rows * grad_score, axis=0, keepdims=True)
        grad = norm_backward(total * gain_ref[...].astype(F32), unit, inverse)
        grad_ref[...] = (grad + grad_score * center_ref[...].astype(F32)).astype(BF)
    normed_out.wait()
    for tile in range(count):
        actives.wait(tile)
        hiddens.wait(tile)


def expert_pass(own, rows, u, win, gain, bias, center, after=()):
    count, width = rows.shape
    hidden = win.shape[1]
    outs = [shaped((count, hidden), BF)] * 2 + [shaped((count, width), BF)]
    outs += [shaped((count, 128), F32)]
    out_specs = [anywhere()] * 3 + [in_vmem()]
    scratch = []
    if own:
        outs += [shaped((count, width), BF), shaped((8, width), F32)]
        out_specs += [in_vmem()] * 2
        scratch = [pltpu.VMEM((count, width), F32)] * 2
    scratch += [pltpu.VMEM((count, width), BF), pltpu.SemaphoreType.DMA(())]
    wide = (count, hidden, 1)
    return kernel_call(
        functools.partial(expert_kernel, own),
        "expert_own" if own else "expert_other",
        (rows, u, win, gain, bias, center),
        19 if own else 12,
        after,
        in_specs=[in_vmem()] + [anywhere()] * 2 + [in_vmem()] * 3,
        out_specs=out_specs,
        out_shape=outs,
        scratch_shapes=scratch + tile_buffers(wide, (width, hidden, 1), wide, wide),
    )


def grad_in_kernel(copy_ref, left_ref, left_other_ref, right_ref, right_other_ref, out_ref):
    del copy_ref
    out_ref[...] = dot(left_ref[...], right_ref[...], 0, 0) + dot(
        left_other_ref[...], right_other_ref[...], 0, 0
    )


def grad_in(copy, copies, normed, normed_other, hidden, hidden_other, after=()):
    count, width = normed.shape
    part = width // copies
    tile = min(2 * TILE, hidden.shape[1])
    left = pl.BlockSpec((count, part), lambda i, copy: (0, copy[0]))
    right = pl.BlockSpec((count, tile), lambda i, copy: (0, i))
    return kernel_call(
        grad_in_kernel,
        "grad_w_in",
        (copy, normed, normed_other, hidden, hidden_other),
        10,
        after,
        grid_spec=(
            1,
            (hidden.shape[1] // tile,),
            [left, left, right, right],
            pl.BlockSpec((part, tile), lambda i, copy: (0, i)),
        ),
        out_shape=shaped((part, hidden.shape[1]), F32),
    )


def grad_out_kernel(
    copy_ref,
    left_ref,
    left_other_ref,
    cot_ref,
    cot_other_ref,
    gate_ref,
    gate_other_ref,
    out_ref,
    right_ref,
    right_other_ref,
):
    del copy_ref

    @pl.when(pl.program_id(0) == 0)
    def _():
        right_ref[...] = (gate_ref[:, :1] * cot_ref[...].astype(F32)).astype(BF)
        right_other_ref[...] = (gate_other_ref[:, :1] * cot_other_ref[...].astype(F32)).astype(BF)

    out_ref[...] = dot(left_ref[...], right_ref[...], 0, 0) + dot(
        left_other_ref[...], right_other_ref[...], 0, 0
    )


def grad_out(copy, copies, active, active_other, cot, cot_other, gate, gate_other, after=()):
    count, width = cot.shape
    part = active.shape[1] // copies
    tile = min(TILE, part)
    tiles = part // tile
    left = pl.BlockSpec((count, tile), lambda i, copy: (0, copy[0] * tiles + i))
    right = pl.BlockSpec((count, width), lambda i, copy: (0, 0))
    gates = pl.BlockSpec(gate.shape, lambda i, copy: (0, 0))
    return kernel_call(
        grad_out_kernel,
        "grad_w_out",
        (copy, active, active_other, cot, cot_other, gate, gate_other),
        10,
        after,
        grid_spec=(
            1,
            (tiles,),
            [left, left, right, right, gates, gates],
            pl.BlockSpec((tile, width), lambda i, copy: (i, 0)),
        ),
        out_shape=shaped((part, width), F32),
        scratch_shapes=[pltpu.VMEM((count, width), BF)] * 2,
    )


def finish_kernel(many, extra, place_ref, *refs):
    parts, outs = refs[: 2 * many], refs[2 * many + extra :]
    place = place_ref[0]
    rows = parts[0].shape[0]
    here = pl.ds(pl.multiple_of(place * rows, rows), rows)
    away = pl.ds(pl.multiple_of((1 - place) * rows, rows), rows)
    for i in range(many):
        outs[i][here, :] = parts[2 * i][...].astype(F32)
        outs[i][away, :] = parts[2 * i + 1][...].astype(F32)


def finished(own, got, place, many, groups, total, before=None):
    start, stop = groups
    rows = own.shape[0]
    part = [
        pl.BlockSpec((rows, GROUP), functools.partial(lambda i, g: (0, many * g + i), i))
        for i in range(many)
    ]
    extra = list(before or ())
    return kernel_call(
        functools.partial(finish_kernel, many, len(extra)),
        "gradients_out",
        [place] + [own, got] * many + extra,
        2 * many,
        grid=(stop - start,),
        in_specs=[scalar()] + [spec for spec in part for _ in range(2)] + [anywhere()] * len(extra),
        out_specs=[pl.BlockSpec((CORES * rows, GROUP), lambda g: (0, start + g))] * many,
        out_shape=[shaped((CORES * rows, total), F32)] * many,
        input_output_aliases={1 + 2 * many + i: i for i in range(len(extra))},
    )


def expert_levels(size):
    levels, stride = [], 1
    while stride < size:
        levels.append((stride, 2 if (size // stride) % 2 == 0 else size // stride))
        stride *= levels[-1][1]
    return levels


def turned(axis, stride, length, step):
    pairs = []
    for index in range(lax.axis_size(axis)):
        place = (index // stride) % length
        pairs.append((index, index + ((place + step) % length - place) * stride))
    return pairs


def scatter_level(rows, axis, stride, length):
    place = (lax.axis_index(axis) // stride) % length
    count = rows.shape[0] // length
    total = lax.dynamic_slice_in_dim(rows, place * count, count, 0).astype(F32)
    for step in range(1, length):
        part = lax.dynamic_slice_in_dim(rows, ((place + step) % length) * count, count, 0)
        part = lax.ppermute(part, axis, turned(axis, stride, length, step))
        total = total + part.astype(F32)
    return total.astype(rows.dtype)


def gather_level(rows, axis, stride, length):
    place = (lax.axis_index(axis) // stride) % length
    count = rows.shape[0]
    parts = [rows] + [
        lax.ppermute(rows, axis, turned(axis, stride, length, step)) for step in range(1, length)
    ]
    if length == 2:
        return jnp.where(
            place == 0, jnp.concatenate(parts, 0), jnp.concatenate([parts[1], parts[0]], 0)
        )
    whole = jnp.zeros((length * count, rows.shape[1]), rows.dtype)
    for step, part in enumerate(parts):
        whole = lax.dynamic_update_slice_in_dim(whole, part, ((place - step) % length) * count, 0)
    return whole


def tied(values, *others):
    return lax.optimization_barrier((values, others))[0]


class RowSum:
    def __init__(self, send, keep):
        levels = expert_levels(lax.axis_size("expert"))
        self.held = (send, keep)
        self.todo = [self.cores, functools.partial(self.scatter, "batch", 1, lax.axis_size("batch"))]
        self.todo += [functools.partial(self.scatter, "expert", *at) for at in levels[1:-1]]
        self.todo += [functools.partial(self.whole, "expert", *levels[-1])]
        self.todo += [functools.partial(self.gather, "expert", *at) for at in levels[-2:0:-1]]
        self.todo.append(self.partner)

    def step(self):
        if self.todo:
            self.todo.pop(0)()

    def cores(self):
        send, keep = self.held
        got = lax.ppermute(send, "expert", turned("expert", 1, CORES, 1))
        total = (keep.astype(F32) + got.astype(F32)).astype(BF)
        self.held = total.reshape(-1, total.shape[-1])

    def scatter(self, *level):
        self.held = scatter_level(self.held, *level)

    def gather(self, *level):
        self.held = gather_level(self.held, *level)

    def partner(self):
        self.held = (self.held, lax.ppermute(self.held, "expert", turned("expert", 1, CORES, 1)))

    def whole(self, axis, stride, length):
        total = self.held.astype(F32)
        for step in range(1, length):
            part = lax.ppermute(self.held, axis, turned(axis, stride, length, step))
            total = total + part.astype(F32)
        self.held = total.astype(BF)


class SmallSum:
    def __init__(self, values):
        self.held = values
        bits = []
        while 1 << len(bits) < lax.axis_size("expert"):
            bits.append(functools.partial(self.doubled, 1 << len(bits)))
        self.todo = [self.copies] + bits

    def step(self):
        if self.todo:
            self.todo.pop(0)()

    def copies(self):
        copies, place = lax.axis_size("batch"), lax.axis_index("batch")
        total = lax.dynamic_index_in_dim(self.held, place, 0, True)
        for step in range(1, copies):
            part = lax.dynamic_index_in_dim(self.held, (place + step) % copies, 0, True)
            total = total + lax.ppermute(part, "batch", turned("batch", 1, copies, step))
        self.held = total

    def doubled(self, bit):
        pairs = [(i, i ^ bit) for i in range(lax.axis_size("expert"))]
        self.held = self.held + lax.ppermute(self.held, "expert", pairs)


def local(
    tokens,
    cotangent,
    segment_ids,
    routing,
    ln_gain,
    ln_bias,
    w_query,
    w_key,
    w_value,
    w_output,
    expert_gain,
    expert_bias,
    centroid,
    w_in,
    w_out,
):
    count, width = tokens.shape
    owners = lax.axis_size("expert")
    copies = lax.axis_size("batch")
    copy = lax.axis_index("batch")
    place = (lax.axis_index("expert") % CORES).astype(jnp.int32)[None]
    send_rows = count // owners
    win = w_in[0]
    wout = w_out[0]

    def exchanged(values):
        return lax.all_to_all(
            values.reshape(owners, send_rows, width),
            "expert",
            split_axis=0,
            concat_axis=0,
            tiled=True,
        ).reshape(count, width)

    def from_copy(values, step):
        return lax.ppermute(values, "batch", turned("batch", 1, copies, step))

    paired = copies == 2
    cot_rows = exchanged(order_rows(cotangent, routing))
    *saved, stream, ordered = attention_forward(
        tokens,
        ln_gain[None],
        ln_bias[None],
        segment_ids,
        routing,
        w_query,
        w_key,
        w_value,
        w_output,
    )
    mixed = saved[4]
    rows = exchanged(ordered)
    cot_other = from_copy(cot_rows, 1) if paired else None
    u = times_out(cot_rows, wout)
    rows, u = tied((rows, u))
    rows_other = from_copy(rows, 1) if paired else None
    vectors = (expert_gain, expert_bias, centroid)
    active, grad_hidden, expert_normed, gating, grad_rows, sums = expert_pass(
        True, rows, u, win, *vectors
    )

    grad_returned = exchanged(grad_rows)
    branch = branch_rows(active, wout, gating, [grad_rows])
    if paired:
        u_other = times_out(cot_other, wout, [branch])
        active_o, hidden_o, normed_o, gating_o = expert_pass(
            False, rows_other, u_other, win, *vectors, [u_other]
        )
        branch, active_o = tied((branch, active_o))
    grad_returned = tied(grad_returned, branch)

    grad_stream, attended, send, keep = gradient_entry(
        grad_returned, routing, cotangent, mixed, place, copies, [branch]
    )
    sum_o = RowSum(send, keep)
    sum_o.step()
    sum_o.held, attended = tied((sum_o.held, attended))
    weights = (w_output, w_query, w_key, w_value)
    groups = width // GROUP
    middle = groups // 2
    send, keep, before = attention_backward(
        (0, middle), saved, attended, weights, place, copies, [sum_o.held]
    )
    sum_o.step()
    sum_o.held, send, keep = tied((sum_o.held, send, keep))
    sum_a = RowSum(send, keep)
    sum_a.step()
    sum_a.held, sum_o.held = tied((sum_a.held, sum_o.held))
    send, keep, grad_tokens, norm_sums = attention_backward(
        (middle, groups),
        saved,
        attended,
        weights,
        place,
        copies,
        [sum_o.held, sum_a.held],
        before,
        [tokens, ln_gain[None], grad_stream],
    )
    sum_o.step()
    sum_a.step()
    sum_a.held, sum_o.held, send, keep = tied((sum_a.held, sum_o.held, send, keep))
    sum_b = RowSum(send, keep)
    sum_b.step()

    gate_vector = jnp.where(
        jnp.arange(owners) == lax.axis_index("expert"),
        jnp.sum(gating[:, 0]) / (count * copies),
        0.0,
    )
    packed = SmallSum(
        jnp.concatenate(
            [
                norm_sums[0].reshape(copies, -1),
                norm_sums[1].reshape(copies, -1),
                gate_vector.reshape(copies, -1),
            ],
            axis=1,
        )
    )
    small = sums[:3].reshape(3, copies, width // copies)
    which = copy.astype(jnp.int32)[None]
    slot = 0
    done = ()
    parts = (sum_o, sum_a, sum_b, packed)
    while sum_b.todo:
        held, branch, small, done = tied(([part.held for part in parts], branch, small, done))
        for part, value in zip(parts, held):
            part.held = value
        if slot == 0:
            branch = exchanged(branch)
            if paired:
                grad_w_out = grad_out(
                    which, copies, active, active_o, cot_rows, cot_other, gating, gating_o,
                    [sum_b.held],
                )
                done = (grad_w_out,)
        if slot == 1 and paired:
            (grad_w_out,) = done
            grad_w_in = grad_in(
                which, copies, expert_normed, normed_o, grad_hidden, hidden_o, [sum_b.held]
            )
            done = (grad_w_out, grad_w_in)
        if slot == 3:
            small_total = lax.dynamic_index_in_dim(small, copy, 1, False)
            for step in range(1, copies):
                away = lax.dynamic_index_in_dim(small, (copy + step) % copies, 1, False)
                small_total = small_total + from_copy(away, step)
            outputs = output_rows(branch, routing, stream)
        for part in (sum_b, sum_a, sum_o, packed):
            part.step()
        slot += 1
    while packed.todo:
        packed.step()
    (grad_wo,) = finished(*sum_o.held, place, 1, (0, groups), width)
    before = finished(*sum_a.held, place, 3, (0, middle), width)
    grad_wq, grad_wk, grad_wv = finished(*sum_b.held, place, 3, (middle, groups), width, before)
    if paired:
        grad_w_out, grad_w_in = done
    else:
        produced = (gating[:, :1] * cot_rows.astype(F32)).astype(BF)
        grad_w_in, grad_w_out = (
            lax.psum_scatter(
                dot(left, right, 0, 0).astype(BF), "batch", scatter_dimension=0, tiled=True
            ).astype(F32)
            for left, right in ((expert_normed, grad_hidden), (active, produced))
        )
    part = width // copies
    packed = packed.held[0]
    return (
        outputs,
        grad_tokens,
        packed[:part],
        packed[part : 2 * part],
        grad_wq,
        grad_wk,
        grad_wv,
        grad_wo,
        small_total[0][None],
        small_total[1][None],
        small_total[2][None],
        grad_w_in[None],
        grad_w_out[None],
        packed[2 * part :],
    )


def solution(mesh):
    both = P(("expert", "batch"), None)
    per_expert = P("expert", None)
    matrices = P("expert", None, None)
    return jax.shard_map(
        local,
        mesh=mesh,
        in_specs=(both,) * 4 + (P(),) * 6 + (per_expert,) * 3 + (matrices,) * 2,
        out_specs=(both, both)
        + (P("batch"),) * 2
        + (P("batch", None),) * 4
        + (P("expert", "batch"),) * 3
        + (P("expert", "batch", None),) * 2
        + (P("batch"),),
        check_vma=False,
    )
```

```python
import functools

import jax
import jax.numpy as jnp
from jax import lax
from jax.experimental import pallas as pl
from jax.experimental.pallas import tpu as pltpu
from jax.sharding import PartitionSpec as P

HEADS = 16
NORM_EPSILON = 1e-05
NEG_FILL = -1e30
LOG2E = 1.4426950408889634
GROUP = 256
CORES = 2
TILE = 512
COST = 1.15e9
VMEM_MIB = {'gradient_entry': 20, 'attention_backward': 44, 'tokens_gradient': 44, 'grad_w_out': 20, 'gradients_out': 16, 'output_rows': 16}
BF = jnp.bfloat16
F32 = jnp.float32


def dot(a, b, ca, cb):
    return lax.dot_general(a, b, (((ca,), (cb,)), ((), ())), preferred_element_type=F32)


def kernel_call(body, name, operands, micros, after=(), in_specs=None, grid_spec=None, **more):
    given, extra = len(operands), len(after)

    def run(*refs):
        body(*refs[:given], *refs[given + extra :])

    unread = [anywhere()] * extra
    if grid_spec is not None:
        prefetched, grid, in_specs, out_specs = grid_spec
        more["grid_spec"] = pltpu.PrefetchScalarGridSpec(
            num_scalar_prefetch=prefetched,
            grid=grid,
            in_specs=in_specs + unread,
            out_specs=out_specs,
            scratch_shapes=more.pop("scratch_shapes", ()),
        )
    else:
        if in_specs is None:
            in_specs = [in_vmem()] * given
        more["in_specs"] = in_specs + unread
    return pl.pallas_call(
        run,
        name=name,
        compiler_params=pltpu.CompilerParams(vmem_limit_bytes=VMEM_MIB.get(name, 60) << 20),
        cost_estimate=pl.CostEstimate(
            flops=int(micros * COST), transcendentals=0, bytes_accessed=0
        ),
        **more,
    )(*operands, *after)


def shaped(shape, kind):
    return jax.ShapeDtypeStruct(shape, kind)


def fixed(*shape):
    return pl.BlockSpec(shape, lambda *place: (0,) * len(shape))


def in_vmem():
    return pl.BlockSpec(memory_space=pltpu.VMEM)


def anywhere():
    return pl.BlockSpec(memory_space=pl.ANY)


def scalar():
    return pl.BlockSpec(memory_space=pltpu.SMEM)


def as_column(row):
    return jnp.transpose(jnp.broadcast_to(row, (8, row.shape[1])))[:, :1]


def standardized(values):
    center = values - jnp.mean(values, axis=-1, keepdims=True)
    spread = jnp.mean(center * center, axis=-1, keepdims=True)
    inverse = lax.rsqrt(spread + NORM_EPSILON)
    return center * inverse, inverse


def norm_backward(grad, unit, inverse):
    mean = jnp.mean(grad, axis=-1, keepdims=True)
    slope = jnp.mean(grad * unit, axis=-1, keepdims=True)
    return inverse * (grad - mean - unit * slope)


def query_blocks(count):
    size = min(256, count)
    blocks, place = [], 0
    for first in range(0, count, size):
        blocks.append((first, size, first + size, place))
        place += first + size
    return blocks, place


def stacked(part, first, size, head_size):
    lane = lax.broadcasted_iota(jnp.int32, (1, GROUP), 1) // head_size
    rows = part[first : first + size]
    return jnp.concatenate(
        [
            jnp.where(lane == head, rows, jnp.zeros_like(rows))
            for head in range(GROUP // head_size)
        ],
        0,
    )


def picked(rows, size, head_size):
    lane = lax.broadcasted_iota(jnp.int32, (1, GROUP), 1) // head_size
    out = rows[:size]
    for head in range(1, GROUP // head_size):
        out = jnp.where(lane == head, rows[head * size : (head + 1) * size], out)
    return out


def split_cores(whole_ref, place_ref, send_ref, keep_ref):
    copies, rows, _ = send_ref.shape
    place = place_ref[0]
    for copy in range(copies):
        start = copy * CORES * rows
        keep = pl.multiple_of(start + place * rows, rows)
        send = pl.multiple_of(start + (1 - place) * rows, rows)
        keep_ref[copy] = whole_ref[pl.ds(keep, rows), :]
        send_ref[copy] = whole_ref[pl.ds(send, rows), :]


def order_kernel(values_ref, slots_ref, ordered_ref):
    count = values_ref.shape[0]
    picks = as_column(slots_ref[...]) == lax.broadcasted_iota(jnp.int32, (count, count), 1)
    ordered_ref[...] = dot(picks.astype(BF), values_ref[...], 1, 0).astype(BF)


def order_rows(values, slots):
    return kernel_call(
        order_kernel, "order_rows", (values, slots), 3, out_shape=shaped(values.shape, BF)
    )


def restored(slots_ref, returned_ref):
    count = returned_ref.shape[0]
    picks = slots_ref[...] == lax.broadcasted_iota(jnp.int32, (count, count), 0)
    return dot(picks.astype(BF), returned_ref[...], 1, 0)


def output_kernel(returned_ref, slots_ref, stream_ref, out_ref):
    out_ref[...] = (stream_ref[...] + restored(slots_ref, returned_ref)).astype(BF)


def output_rows(returned, slots, stream, after=()):
    return kernel_call(
        output_kernel,
        "output_rows",
        (returned, slots, stream),
        4,
        after,
        out_shape=shaped(returned.shape, BF),
    )


def entry_kernel(
    returned_ref, slots_ref, cot_ref, mixed_ref, place_ref, attended_ref, send_ref, keep_ref, whole_ref
):
    stream = cot_ref[...].astype(F32) + restored(slots_ref, returned_ref)
    attended = stream.astype(BF)
    attended_ref[...] = attended
    whole_ref[...] = dot(mixed_ref[...], attended, 0, 0).astype(BF)
    split_cores(whole_ref, place_ref, send_ref, keep_ref)


def gradient_entry(returned, slots, cot, mixed, place, copies, after):
    count, width = cot.shape
    half = (copies, width // (CORES * copies), width)
    return kernel_call(
        entry_kernel,
        "gradient_entry",
        (returned, slots, cot, mixed, place),
        4,
        after,
        in_specs=[in_vmem()] * 4 + [scalar()],
        out_shape=[shaped((count, width), BF)] + [shaped(half, BF)] * 2,
        scratch_shapes=[pltpu.VMEM((width, width), BF)],
    )


def attention_kernel(
    head_size,
    tokens_ref,
    gain_ref,
    bias_ref,
    segment_ref,
    slots_ref,
    wq_hbm,
    wk_hbm,
    wv_hbm,
    wo_hbm,
    normed_hbm,
    q_hbm,
    k_hbm,
    v_hbm,
    mixed_hbm,
    probs_hbm,
    stream_hbm,
    ordered_ref,
    mask_ref,
    weight_ref,
    normed_ref,
    q_ref,
    k_ref,
    v_ref,
    mixed_ref,
    probs_ref,
    stream_ref,
    in_sem,
    out_sem,
):
    count, width = tokens_ref.shape
    blocks, _ = query_blocks(count)
    per = GROUP // head_size
    weights = [
        pltpu.make_async_copy(array, weight_ref.at[i], in_sem.at[i])
        for i, array in enumerate((wq_hbm, wk_hbm, wv_hbm, wo_hbm))
    ]
    for copy in weights:
        copy.start()
    sent = []

    def send(buffer_ref, array_ref):
        sent.append(pltpu.make_async_copy(buffer_ref, array_ref, out_sem.at[len(sent)]))
        sent[-1].start()

    values = tokens_ref[...].astype(F32)
    unit, _ = standardized(values)
    normed = unit * gain_ref[...].astype(F32) + bias_ref[...].astype(F32)
    normed_ref[...] = normed.astype(BF)
    send(normed_ref, normed_hbm)
    segment = segment_ref[...]
    column = as_column(segment)
    for first, size, keys, place in blocks:
        shape = (keys, size)
        query = first + lax.broadcasted_iota(jnp.int32, shape, 1)
        later = lax.broadcasted_iota(jnp.int32, shape, 0) <= query
        same = column[:keys] == segment[:, first : first + size]
        mask_ref[place : place + keys, :] = jnp.where(later & same, 0.0, NEG_FILL)

    for i, (out_ref, out_hbm) in enumerate(((q_ref, q_hbm), (k_ref, k_hbm), (v_ref, v_hbm))):
        weights[i].wait()
        out_ref[...] = dot(normed_ref[...], weight_ref[i], 1, 0).astype(BF)
        send(out_ref, out_hbm)
    scale = head_size**-0.5 * LOG2E
    for group in range(width // GROUP):
        lanes = slice(group * GROUP, (group + 1) * GROUP)
        queries = q_ref[:, lanes]
        for first, size, keys, place in blocks:
            scores = dot(k_ref[:keys, lanes], stacked(queries, first, size, head_size), 1, 1)
            masks = mask_ref[place : place + keys, :]
            parts = []
            for head in range(per):
                own = scores[:, head * size : (head + 1) * size] * scale + masks
                terms = jnp.exp2(own - jnp.max(own, axis=0, keepdims=True))
                probs = (terms * (1.0 / jnp.sum(terms, axis=0, keepdims=True))).astype(BF)
                probs_ref[group * per + head, place : place + keys, :] = probs
                parts.append(probs)
            mixed = dot(jnp.concatenate(parts, 1), v_ref[:keys, lanes], 0, 0)
            mixed_ref[first : first + size, lanes] = picked(mixed, size, head_size).astype(BF)
        heads = pl.ds(group * per, per)
        send(probs_ref.at[heads], probs_hbm.at[heads])
    send(mixed_ref, mixed_hbm)
    weights[3].wait()
    stream = tokens_ref[...].astype(F32) + dot(mixed_ref[...], weight_ref[3], 1, 0)
    stream_ref[...] = stream
    send(stream_ref, stream_hbm)
    picks = as_column(slots_ref[...]) == lax.broadcasted_iota(jnp.int32, (count, count), 1)
    ordered_ref[...] = dot(picks.astype(BF), stream.astype(BF), 1, 0).astype(BF)
    for copy in sent:
        copy.wait()


def attention_forward(tokens, gain, bias, segment, slots, wq, wk, wv, wo):
    count, width = tokens.shape
    blocks, area = query_blocks(count)
    size = blocks[0][1]
    rows = [shaped((count, width), BF)] * 5
    kept = rows + [shaped((HEADS, area, size), BF), shaped((count, width), F32)]
    return kernel_call(
        functools.partial(attention_kernel, width // HEADS),
        "attention_forward",
        (tokens, gain, bias, segment, slots, wq, wk, wv, wo),
        17,
        in_specs=[in_vmem()] * 5 + [anywhere()] * 4,
        out_specs=[anywhere()] * 7 + [in_vmem()],
        out_shape=kept + [shaped((count, width), BF)],
        scratch_shapes=[pltpu.VMEM((area, size), F32), pltpu.VMEM((4, width, width), BF)]
        + [pltpu.VMEM(array.shape, array.dtype) for array in kept]
        + [pltpu.SemaphoreType.DMA((4,)), pltpu.SemaphoreType.DMA((6 + width // GROUP,))],
    )


def backward_kernel(
    head_size,
    attended_ref,
    normed_ref,
    q_ref,
    k_ref,
    v_ref,
    mixed_ref,
    probs_ref,
    wo_ref,
    place_ref,
    send_ref,
    keep_ref,
    grads_ref,
    whole_ref,
):
    count = attended_ref.shape[0]
    blocks, _ = query_blocks(count)
    per = GROUP // head_size
    scale = head_size**-0.5
    queries, key_rows, value_rows = q_ref[...], k_ref[...], v_ref[...]
    grad_mixed = dot(attended_ref[...], wo_ref[...], 1, 1).astype(BF)
    products = grad_mixed.astype(F32) * mixed_ref[...].astype(F32)
    high = products.astype(BF)
    low = (products - high.astype(F32)).astype(BF)
    lane = lax.broadcasted_iota(jnp.int32, (16, GROUP), 1) // head_size
    heads = (lane == lax.broadcasted_iota(jnp.int32, (16, GROUP), 0)).astype(BF)
    centre = dot(heads, high, 1, 1) + dot(heads, low, 1, 1)
    grad_q = []
    grad_k = jnp.zeros((count, GROUP), F32)
    grad_v = jnp.zeros((count, GROUP), F32)
    for first, size, keys, place in blocks:
        grads = stacked(grad_mixed, first, size, head_size)
        grad_probs = dot(value_rows[:keys], grads, 1, 1)
        probs, scores = [], []
        for head in range(per):
            own = probs_ref[head, place : place + keys, :]
            off = grad_probs[:, head * size : (head + 1) * size]
            off = off - centre[head : head + 1, first : first + size]
            probs.append(own)
            scores.append((own.astype(F32) * off).astype(BF))
        probs = jnp.concatenate(probs, 1)
        scores = jnp.concatenate(scores, 1)
        grad_q.append(picked(dot(scores, key_rows[:keys], 0, 0), size, head_size))
        more_v = dot(probs, grads, 1, 0)
        more_k = dot(scores, stacked(queries, first, size, head_size), 1, 0)
        if keys < count:
            rest = jnp.zeros((count - keys, GROUP), F32)
            more_v = jnp.concatenate([more_v, rest], 0)
            more_k = jnp.concatenate([more_k, rest], 0)
        grad_v = grad_v + more_v
        grad_k = grad_k + more_k
    grad_q = jnp.concatenate(grad_q, 0) * scale
    joined = [grad.astype(BF) for grad in (grad_q, grad_k * scale, grad_v)]
    for i, grad in enumerate(joined):
        grads_ref[i] = grad
    whole_ref[...] = dot(normed_ref[...], jnp.concatenate(joined, 1), 0, 0).astype(BF)
    split_cores(whole_ref, place_ref, send_ref, keep_ref)


def attention_backward(groups, saved, attended, w_output, place, copies, after):
    normed, q, k, v, mixed, probs = saved
    count, width = attended.shape
    head_size = width // HEADS
    _, area, size = probs.shape
    start, stop = groups
    all_rows = fixed(count, width)
    part = pl.BlockSpec((count, GROUP), lambda g: (0, start + g))
    rows = width // (CORES * copies)
    half = shaped((copies, rows, 3 * GROUP * (stop - start)), BF)
    half_spec = pl.BlockSpec((copies, rows, 3 * GROUP), lambda g: (0, 0, g))
    specs = [all_rows, all_rows, part, part, part, part]
    specs += [pl.BlockSpec((GROUP // head_size, area, size), lambda g: (start + g, 0, 0))]
    specs += [pl.BlockSpec((GROUP, width), lambda g: (start + g, 0)), scalar()]
    return kernel_call(
        functools.partial(backward_kernel, head_size),
        "attention_backward",
        (attended, normed, q, k, v, mixed, probs, w_output, place),
        6 * (stop - start),
        after,
        grid=(stop - start,),
        in_specs=specs,
        out_specs=[half_spec, half_spec, pl.BlockSpec((3, count, GROUP), lambda g: (0, 0, g))],
        out_shape=[half, half, shaped((3, count, GROUP * (stop - start)), BF)],
        scratch_shapes=[pltpu.VMEM((width, 3 * GROUP), BF)],
    )


def tokens_kernel(parts, *refs):
    grads, weights = refs[:parts], refs[parts : parts + 3]
    tokens_ref, gain_ref, returned_ref, slots_ref, cot_ref = refs[parts + 3 : parts + 8]
    grad_ref, sums_ref, weight_ref, sems = refs[parts + 8 :]
    copies = [
        pltpu.make_async_copy(weight, weight_ref.at[i], sems.at[i])
        for i, weight in enumerate(weights)
    ]
    for copy in copies:
        copy.start()
    total = None
    for i in range(3):
        copies[i].wait()
        at = 0
        for grad in grads:
            columns = grad.shape[2]
            more = dot(grad[i], weight_ref[i, :, at : at + columns], 1, 1)
            total = more if total is None else total + more
            at += columns
    unit, inverse = standardized(tokens_ref[...].astype(F32))
    sums_ref[0:1, :] = jnp.sum(total * unit, axis=0, keepdims=True)
    sums_ref[1:2, :] = jnp.sum(total, axis=0, keepdims=True)
    grad = norm_backward(total * gain_ref[...].astype(F32), unit, inverse)
    stream = cot_ref[...].astype(F32) + restored(slots_ref, returned_ref)
    grad_ref[...] = (stream + grad).astype(BF)


def tokens_gradient(grads, weights, tokens, gain, returned, slots, cot, after):
    count, width = tokens.shape
    operands = (*grads, *weights, tokens, gain, returned, slots, cot)
    return kernel_call(
        functools.partial(tokens_kernel, len(grads)),
        "tokens_gradient",
        operands,
        9,
        after,
        in_specs=[in_vmem()] * len(grads) + [anywhere()] * 3 + [in_vmem()] * 5,
        out_shape=[shaped((count, width), BF), shaped((8, width), F32)],
        scratch_shapes=[pltpu.VMEM((3, width, width), BF), pltpu.SemaphoreType.DMA((3,))],
    )


def tiles_of(size):
    return [slice(at, at + TILE) for at in range(0, size, TILE)]


class Tiles:
    def __init__(self, array_ref, buffer_ref, sems, axis, inward):
        self.copies = []
        for tile in range(buffer_ref.shape[0]):
            span = pl.ds(tile * TILE, TILE)
            outside = array_ref.at[span, :] if axis == 0 else array_ref.at[:, span]
            ends = (outside, buffer_ref.at[tile]) if inward else (buffer_ref.at[tile], outside)
            self.copies.append(pltpu.make_async_copy(*ends, sems.at[tile]))

    def start(self, tile):
        self.copies[tile].start()

    def wait(self, tile):
        self.copies[tile].wait()


def tile_buffers(*arrays):
    scratch = []
    for rows, columns, axis in arrays:
        count = (columns if axis else rows) // TILE
        shape = (count, rows, TILE) if axis else (count, TILE, columns)
        scratch.append(pltpu.VMEM(shape, BF))
    scratch += [pltpu.SemaphoreType.DMA(buffer.shape[:1]) for buffer in scratch]
    return scratch


def times_out_kernel(rows_ref, wout_hbm, out_hbm, wout_ref, out_ref, wout_sem, out_sem):
    weights = Tiles(wout_hbm, wout_ref, wout_sem, 0, True)
    results = Tiles(out_hbm, out_ref, out_sem, 1, False)
    count = wout_ref.shape[0]
    for tile in range(count):
        weights.start(tile)
    for tile in range(count):
        weights.wait(tile)
        out_ref[tile] = dot(rows_ref[...], wout_ref[tile], 1, 1).astype(BF)
        results.start(tile)
    for tile in range(count):
        results.wait(tile)


def times_out(rows, wout, after=()):
    count, width = rows.shape
    hidden = wout.shape[0]
    return kernel_call(
        times_out_kernel,
        "rows_times_w_out",
        (rows, wout),
        7,
        after,
        in_specs=[in_vmem(), anywhere()],
        out_specs=anywhere(),
        out_shape=shaped((count, hidden), BF),
        scratch_shapes=tile_buffers((hidden, width, 0), (count, hidden, 1)),
    )


def branch_kernel(
    active_hbm, wout_hbm, gate_ref, out_ref, active_ref, wout_ref, active_sem, wout_sem
):
    weights = Tiles(wout_hbm, wout_ref, wout_sem, 0, True)
    actives = Tiles(active_hbm, active_ref, active_sem, 1, True)
    count = wout_ref.shape[0]
    for tile in range(count):
        weights.start(tile)
        actives.start(tile)
    total = None
    for tile in range(count):
        weights.wait(tile)
        actives.wait(tile)
        more = dot(active_ref[tile], wout_ref[tile], 1, 0)
        total = more if total is None else total + more
    out_ref[...] = (total * gate_ref[:, :1]).astype(BF)


def branch_rows(active, wout, gating, after=()):
    count, hidden = active.shape
    width = wout.shape[1]
    return kernel_call(
        branch_kernel,
        "branch",
        (active, wout, gating),
        7,
        after,
        in_specs=[anywhere(), anywhere(), in_vmem()],
        out_shape=shaped((count, width), BF),
        scratch_shapes=tile_buffers((count, hidden, 1), (hidden, width, 0)),
    )


def gelu_parts(hidden):
    slant = 0.7978845608028654
    bend = slant * 0.044715
    square = hidden * hidden
    half = 0.5 + 0.5 * jnp.tanh(hidden * (slant + bend * square))
    active = hidden * half
    return active, half + active * (1.0 - half) * (2 * slant + 6 * bend * square)


def expert_start(rows_ref, gain_ref, bias_ref, center_ref, normed_ref, gate_ref):
    rows = rows_ref[...].astype(F32)
    unit, inverse = standardized(rows)
    normed_ref[...] = (unit * gain_ref[...].astype(F32) + bias_ref[...].astype(F32)).astype(BF)
    score = jnp.sum(rows * center_ref[...].astype(F32), axis=-1, keepdims=True)
    gating = 1.0 / (1.0 + jnp.exp(-score))
    gate_ref[...] = jnp.broadcast_to(gating, gate_ref.shape)
    return unit, inverse


def own_kernel(
    rows_ref,
    u_hbm,
    win_hbm,
    gain_ref,
    bias_ref,
    center_ref,
    active_hbm,
    hidden_hbm,
    normed_hbm,
    gate_ref,
    grad_ref,
    sums_ref,
    unit_ref,
    total_ref,
    normed_ref,
    normed_sem,
    u_ref,
    win_ref,
    active_ref,
    hidden_ref,
    u_sem,
    win_sem,
    active_sem,
    hidden_sem,
):
    weights = Tiles(win_hbm, win_ref, win_sem, 1, True)
    us = Tiles(u_hbm, u_ref, u_sem, 1, True)
    actives = Tiles(active_hbm, active_ref, active_sem, 1, False)
    hiddens = Tiles(hidden_hbm, hidden_ref, hidden_sem, 1, False)
    count = win_ref.shape[0]
    for tile in range(count):
        weights.start(tile)
        us.start(tile)
    unit, inverse = expert_start(rows_ref, gain_ref, bias_ref, center_ref, normed_ref, gate_ref)
    unit_ref[...] = unit
    normed_out = pltpu.make_async_copy(normed_ref, normed_hbm, normed_sem)
    normed_out.start()
    lanes = gate_ref.shape[1]
    scores = jnp.zeros((unit.shape[0], lanes), F32)
    for tile in range(count):
        weights.wait(tile)
        us.wait(tile)
        active, slope = gelu_parts(dot(normed_ref[...], win_ref[tile], 1, 0))
        active = active.astype(BF)
        active_ref[tile] = active
        actives.start(tile)
        u = u_ref[tile].astype(F32)
        hidden_ref[tile] = (slope * (u * gate_ref[:, :1])).astype(BF)
        hiddens.start(tile)
        products = active.astype(F32) * u
        for place in range(0, products.shape[1], lanes):
            scores = scores + products[:, place : place + lanes]
        more = dot(hidden_ref[tile], win_ref[tile], 1, 1)
        if tile:
            total_ref[...] += more
        else:
            total_ref[...] = more
    total = total_ref[...]
    gating = gate_ref[:, :1]
    grad_gating = jnp.sum(scores, axis=-1, keepdims=True)
    grad_score = grad_gating * gating * (1.0 - gating)
    unit = unit_ref[...]
    rows = rows_ref[...].astype(F32)
    sums_ref[0:1, :] = jnp.sum(total * unit, axis=0, keepdims=True)
    sums_ref[1:2, :] = jnp.sum(total, axis=0, keepdims=True)
    sums_ref[2:3, :] = jnp.sum(rows * grad_score, axis=0, keepdims=True)
    grad = norm_backward(total * gain_ref[...].astype(F32), unit, inverse)
    grad_ref[...] = (grad + grad_score * center_ref[...].astype(F32)).astype(BF)
    normed_out.wait()
    for tile in range(count):
        actives.wait(tile)
        hiddens.wait(tile)


def expert_own(rows, u, win, gain, bias, center, after=()):
    count, width = rows.shape
    hidden = win.shape[1]
    outs = [shaped((count, hidden), BF)] * 2 + [shaped((count, width), BF)]
    outs += [shaped((count, 128), F32), shaped((count, width), BF), shaped((8, width), F32)]
    wide = (count, hidden, 1)
    return kernel_call(
        own_kernel,
        "expert_own",
        (rows, u, win, gain, bias, center),
        19,
        after,
        in_specs=[in_vmem()] + [anywhere()] * 2 + [in_vmem()] * 3,
        out_specs=[anywhere()] * 3 + [in_vmem()] * 3,
        out_shape=outs,
        scratch_shapes=[pltpu.VMEM((count, width), F32)] * 2
        + [pltpu.VMEM((count, width), BF), pltpu.SemaphoreType.DMA(())]
        + tile_buffers(wide, (width, hidden, 1), wide, wide),
    )


def other_kernel(
    rows_ref,
    cot_ref,
    copy_ref,
    win_hbm,
    wout_hbm,
    gain_ref,
    bias_ref,
    center_ref,
    active_hbm,
    hidden_hbm,
    normed_hbm,
    gate_ref,
    normed_ref,
    normed_sem,
    produced_ref,
    win_ref,
    wout_ref,
    active_ref,
    hidden_ref,
    win_sem,
    wout_sem,
    active_sem,
    hidden_sem,
):
    weights = Tiles(win_hbm, win_ref, win_sem, 1, True)
    back = Tiles(wout_hbm, wout_ref, wout_sem, 0, True)
    hiddens = Tiles(hidden_hbm, hidden_ref, hidden_sem, 1, False)
    count = win_ref.shape[0]
    part = active_hbm.shape[1] // TILE
    for tile in range(count):
        weights.start(tile)
        back.start(tile)
    expert_start(rows_ref, gain_ref, bias_ref, center_ref, normed_ref, gate_ref)
    normed_out = pltpu.make_async_copy(normed_ref, normed_hbm, normed_sem)
    normed_out.start()
    produced_ref[...] = (gate_ref[:, :1] * cot_ref[...].astype(F32)).astype(BF)

    def active_out(tile):
        place = tile % part
        return pltpu.make_async_copy(
            active_ref.at[tile],
            active_hbm.at[:, pl.ds(place * TILE, TILE)],
            active_sem.at[place],
        )

    for tile in range(count):
        weights.wait(tile)
        back.wait(tile)
        active, slope = gelu_parts(dot(normed_ref[...], win_ref[tile], 1, 0))
        active_ref[tile] = active.astype(BF)

        @pl.when(copy_ref[0] == tile // part)
        def _(tile=tile):
            active_out(tile).start()

        hidden_ref[tile] = (slope * dot(produced_ref[...], wout_ref[tile], 1, 1)).astype(BF)
        hiddens.start(tile)
    normed_out.wait()
    for tile in range(part):
        active_out(tile).wait()
    for tile in range(count):
        hiddens.wait(tile)


def expert_other(rows, cot, copy, copies, win, wout, gain, bias, center, after=()):
    count, width = rows.shape
    hidden = win.shape[1]
    wide = (count, hidden, 1)
    outs = [shaped((count, hidden // copies), BF), shaped((count, hidden), BF)]
    outs += [shaped((count, width), BF), shaped((count, 128), F32)]
    buffers = tile_buffers((width, hidden, 1), (hidden, width, 0), wide, wide)
    return kernel_call(
        other_kernel,
        "expert_other",
        (rows, cot, copy, win, wout, gain, bias, center),
        18,
        after,
        in_specs=[in_vmem()] * 2 + [scalar()] + [anywhere()] * 2 + [in_vmem()] * 3,
        out_specs=[anywhere()] * 3 + [in_vmem()],
        out_shape=outs,
        scratch_shapes=[pltpu.VMEM((count, width), BF), pltpu.SemaphoreType.DMA(())]
        + [pltpu.VMEM((count, width), BF)]
        + buffers,
    )


def grad_in_kernel(copy_ref, left_ref, left_other_ref, right_ref, right_other_ref, out_ref):
    del copy_ref
    out_ref[...] = dot(left_ref[...], right_ref[...], 0, 0) + dot(
        left_other_ref[...], right_other_ref[...], 0, 0
    )


def grad_in(copy, copies, normed, normed_other, hidden, hidden_other, after=()):
    count, width = normed.shape
    part = width // copies
    tile = min(2 * TILE, hidden.shape[1])
    left = pl.BlockSpec((count, part), lambda i, copy: (0, copy[0]))
    right = pl.BlockSpec((count, tile), lambda i, copy: (0, i))
    return kernel_call(
        grad_in_kernel,
        "grad_w_in",
        (copy, normed, normed_other, hidden, hidden_other),
        10,
        after,
        grid_spec=(
            1,
            (hidden.shape[1] // tile,),
            [left, left, right, right],
            pl.BlockSpec((part, tile), lambda i, copy: (0, i)),
        ),
        out_shape=shaped((part, hidden.shape[1]), F32),
    )


def grad_out_kernel(
    copy_ref,
    left_ref,
    left_other_ref,
    cot_ref,
    cot_other_ref,
    gate_ref,
    gate_other_ref,
    out_ref,
    right_ref,
    right_other_ref,
):
    del copy_ref

    @pl.when(pl.program_id(0) == 0)
    def _():
        right_ref[...] = (gate_ref[:, :1] * cot_ref[...].astype(F32)).astype(BF)
        right_other_ref[...] = (gate_other_ref[:, :1] * cot_other_ref[...].astype(F32)).astype(BF)

    out_ref[...] = dot(left_ref[...], right_ref[...], 0, 0) + dot(
        left_other_ref[...], right_other_ref[...], 0, 0
    )


def grad_out(copy, copies, active, active_other, cot, cot_other, gate, gate_other, after=()):
    count, width = cot.shape
    part = active.shape[1] // copies
    tile = min(TILE, part)
    tiles = part // tile
    left = pl.BlockSpec((count, tile), lambda i, copy: (0, copy[0] * tiles + i))
    left_other = pl.BlockSpec((count, tile), lambda i, copy: (0, i))
    right = pl.BlockSpec((count, width), lambda i, copy: (0, 0))
    gates = pl.BlockSpec(gate.shape, lambda i, copy: (0, 0))
    return kernel_call(
        grad_out_kernel,
        "grad_w_out",
        (copy, active, active_other, cot, cot_other, gate, gate_other),
        10,
        after,
        grid_spec=(
            1,
            (tiles,),
            [left, left_other, right, right, gates, gates],
            pl.BlockSpec((tile, width), lambda i, copy: (i, 0)),
        ),
        out_shape=shaped((part, width), F32),
        scratch_shapes=[pltpu.VMEM((count, width), BF)] * 2,
    )


def finish_kernel(many, extra, place_ref, *refs):
    parts, outs = refs[: 2 * many], refs[2 * many + extra :]
    place = place_ref[0]
    rows = parts[0].shape[0]
    here = pl.ds(pl.multiple_of(place * rows, rows), rows)
    away = pl.ds(pl.multiple_of((1 - place) * rows, rows), rows)
    for i in range(many):
        outs[i][here, :] = parts[2 * i][...].astype(F32)
        outs[i][away, :] = parts[2 * i + 1][...].astype(F32)


def finished(own, got, *, place, many, groups, total, before=None):
    start, stop = groups
    rows = own.shape[0]
    part = [
        pl.BlockSpec((rows, GROUP), functools.partial(lambda i, g: (0, many * g + i), i))
        for i in range(many)
    ]
    extra = list(before or ())
    return kernel_call(
        functools.partial(finish_kernel, many, len(extra)),
        "gradients_out",
        [place] + [own, got] * many + extra,
        2 * many,
        grid=(stop - start,),
        in_specs=[scalar()] + [spec for spec in part for _ in range(2)] + [anywhere()] * len(extra),
        out_specs=[pl.BlockSpec((CORES * rows, GROUP), lambda g: (0, start + g))] * many,
        out_shape=[shaped((CORES * rows, total), F32)] * many,
        input_output_aliases={1 + 2 * many + i: i for i in range(len(extra))},
    )


def expert_levels(size):
    levels, stride = [], 1
    while stride < size:
        levels.append((stride, 2 if (size // stride) % 2 == 0 else size // stride))
        stride *= levels[-1][1]
    return levels


def turned(axis, stride, length, step):
    pairs = []
    for index in range(lax.axis_size(axis)):
        place = (index // stride) % length
        pairs.append((index, index + ((place + step) % length - place) * stride))
    return pairs


def scatter_level(rows, axis, stride, length, outer=1):
    place = (lax.axis_index(axis) // stride) % length
    columns = rows.shape[1]
    split = rows.reshape(outer, length, -1, columns)
    total = lax.dynamic_index_in_dim(split, place, 1, False).astype(F32)
    for step in range(1, length):
        part = lax.dynamic_index_in_dim(split, (place + step) % length, 1, False)
        part = lax.ppermute(part, axis, turned(axis, stride, length, step))
        total = total + part.astype(F32)
    return total.astype(rows.dtype).reshape(-1, columns)


def gather_level(rows, axis, stride, length):
    place = (lax.axis_index(axis) // stride) % length
    count = rows.shape[0]
    parts = [rows] + [
        lax.ppermute(rows, axis, turned(axis, stride, length, step)) for step in range(1, length)
    ]
    if length == 2:
        return jnp.where(
            place == 0, jnp.concatenate(parts, 0), jnp.concatenate([parts[1], parts[0]], 0)
        )
    whole = jnp.zeros((length * count, rows.shape[1]), rows.dtype)
    for step, part in enumerate(parts):
        whole = lax.dynamic_update_slice_in_dim(whole, part, ((place - step) % length) * count, 0)
    return whole


def tied(values, *others):
    return lax.optimization_barrier((values, others))[0]


class RowSum:
    def __init__(self, send, keep, copies_second=False):
        levels = expert_levels(lax.axis_size("expert"))
        copies = lax.axis_size("batch")
        self.held = (send, keep)
        scatters = [("batch", 1, copies)] + [("expert", *at) for at in levels[1:-1]]
        if copies_second and len(scatters) > 1:
            scatters[:2] = [(*scatters[1], copies), scatters[0]]
        self.todo = [self.cores] + [functools.partial(self.scatter, *at) for at in scatters]
        self.todo += [functools.partial(self.whole, "expert", *levels[-1])]
        self.todo += [functools.partial(self.gather, "expert", *at) for at in levels[-2:0:-1]]
        self.todo.append(self.partner)

    def step(self):
        if self.todo:
            self.todo.pop(0)()

    def cores(self):
        send, keep = self.held
        got = lax.ppermute(send, "expert", turned("expert", 1, CORES, 1))
        total = (keep.astype(F32) + got.astype(F32)).astype(BF)
        self.held = total.reshape(-1, total.shape[-1])

    def scatter(self, *level):
        self.held = scatter_level(self.held, *level)

    def gather(self, *level):
        self.held = gather_level(self.held, *level)

    def partner(self):
        self.held = (self.held, lax.ppermute(self.held, "expert", turned("expert", 1, CORES, 1)))

    def whole(self, axis, stride, length):
        total = self.held.astype(F32)
        for step in range(1, length):
            part = lax.ppermute(self.held, axis, turned(axis, stride, length, step))
            total = total + part.astype(F32)
        self.held = total.astype(BF)


class SmallSum:
    def __init__(self, values):
        self.held = values
        bits = []
        while 1 << len(bits) < lax.axis_size("expert"):
            bits.append(functools.partial(self.doubled, 1 << len(bits)))
        self.todo = [self.copies] + bits

    def step(self):
        if self.todo:
            self.todo.pop(0)()

    def copies(self):
        copies, place = lax.axis_size("batch"), lax.axis_index("batch")
        total = lax.dynamic_index_in_dim(self.held, place, 0, True)
        for step in range(1, copies):
            part = lax.dynamic_index_in_dim(self.held, (place + step) % copies, 0, True)
            total = total + lax.ppermute(part, "batch", turned("batch", 1, copies, step))
        self.held = total

    def doubled(self, bit):
        pairs = [(i, i ^ bit) for i in range(lax.axis_size("expert"))]
        self.held = self.held + lax.ppermute(self.held, "expert", pairs)


def local(
    tokens,
    cotangent,
    segment_ids,
    routing,
    ln_gain,
    ln_bias,
    w_query,
    w_key,
    w_value,
    w_output,
    expert_gain,
    expert_bias,
    centroid,
    w_in,
    w_out,
):
    count, width = tokens.shape
    owners = lax.axis_size("expert")
    copies = lax.axis_size("batch")
    copy = lax.axis_index("batch")
    place = (lax.axis_index("expert") % CORES).astype(jnp.int32)[None]
    send_rows = count // owners
    win = w_in[0]
    wout = w_out[0]

    def exchanged(values):
        return lax.all_to_all(
            values.reshape(owners, send_rows, width),
            "expert",
            split_axis=0,
            concat_axis=0,
            tiled=True,
        ).reshape(count, width)

    def from_copy(values, step):
        return lax.ppermute(values, "batch", turned("batch", 1, copies, step))

    paired = copies == 2
    cot_rows = exchanged(order_rows(cotangent, routing))
    *saved, stream, ordered = attention_forward(
        tokens,
        ln_gain[None],
        ln_bias[None],
        segment_ids,
        routing,
        w_query,
        w_key,
        w_value,
        w_output,
    )
    mixed = saved[4]
    rows = exchanged(ordered)
    cot_other = from_copy(cot_rows, 1) if paired else None
    u = times_out(cot_rows, wout)
    rows, u = tied((rows, u))
    rows_other = from_copy(rows, 1) if paired else None
    vectors = (expert_gain, expert_bias, centroid)
    active, grad_hidden, expert_normed, gating, grad_rows, sums = expert_own(
        rows, u, win, *vectors
    )

    grad_returned = exchanged(grad_rows)
    branch = branch_rows(active, wout, gating, [grad_rows])
    which = copy.astype(jnp.int32)[None]
    if paired:
        active_o, hidden_o, normed_o, gating_o = expert_other(
            rows_other, cot_other, which, copies, win, wout, *vectors, [branch]
        )
        branch, active_o = tied((branch, active_o))
    grad_returned = tied(grad_returned, branch)

    attended, send, keep = gradient_entry(
        grad_returned, routing, cotangent, mixed, place, copies, [branch]
    )
    sum_o = RowSum(send, keep, True)
    groups = width // GROUP
    middle = groups // 2
    backward = functools.partial(attention_backward, saved=saved, attended=attended, w_output=w_output)
    send, keep, grads_a = backward((0, middle), place=place, copies=copies, after=[attended])
    sum_o.step()
    sum_o.held, send, keep = tied((sum_o.held, send, keep))
    sum_a = RowSum(send, keep)
    sum_a.step()
    sum_a.held, sum_o.held = tied((sum_a.held, sum_o.held))
    send, keep, grads_b = backward((middle, groups), place=place, copies=copies, after=[sum_a.held])
    sum_o.step()
    sum_a.step()
    sum_a.held, sum_o.held, send, keep = tied((sum_a.held, sum_o.held, send, keep))
    sum_b = RowSum(send, keep)
    sum_b.step()
    sum_o.step()
    branch = exchanged(tied(branch, grads_b))

    gate_vector = jnp.where(
        jnp.arange(owners) == lax.axis_index("expert"),
        jnp.sum(gating[:, 0]) / (count * copies),
        0.0,
    )
    small = sums[:3].reshape(3, copies, width // copies)
    slot = 0
    done = []
    packed = None
    finish = functools.partial(finished, place=place, total=width)
    while sum_b.todo:
        parts = [part for part in (sum_b, sum_a, sum_o, packed) if part is not None]
        if slot:
            held, small, done = tied(([part.held for part in parts], small, done))
            for part, value in zip(parts, held):
                part.held = value
        if slot == 0 and paired:
            done.append(
                grad_out(
                    which, copies, active, active_o, cot_rows, cot_other, gating, gating_o,
                    [sum_b.held],
                )
            )
        if slot == 0:
            small_total = lax.dynamic_index_in_dim(small, copy, 1, False)
            for step in range(1, copies):
                away = lax.dynamic_index_in_dim(small, (copy + step) % copies, 1, False)
                small_total = small_total + from_copy(away, step)
            small = small_total
        if slot == 0:
            grad_tokens, norm_sums = tokens_gradient(
                (grads_a, grads_b),
                (w_query, w_key, w_value),
                tokens,
                ln_gain[None],
                grad_returned,
                routing,
                cotangent,
                [sum_b.held],
            )
            done += [grad_tokens, norm_sums]
        if slot == 1:
            norm_sums = done.pop()
            packed = SmallSum(
                jnp.concatenate(
                    [
                        norm_sums[0].reshape(copies, -1),
                        norm_sums[1].reshape(copies, -1),
                        gate_vector.reshape(copies, -1),
                    ],
                    axis=1,
                )
            )
        if slot == 2:
            if paired:
                done.append(
                    grad_in(
                        which, copies, expert_normed, normed_o, grad_hidden, hidden_o, [sum_b.held]
                    )
                )
        if slot == 4:
            branch = tied(branch, sum_b.held)
            outputs = output_rows(branch, routing, stream)
            done.append(outputs)
        if not sum_o.todo and sum_o.held:
            (grad_wo,) = finish(*sum_o.held, many=1, groups=(0, groups))
            done.append(grad_wo)
            sum_o.held = ()
        if not sum_a.todo and sum_a.held:
            before = finish(*sum_a.held, many=3, groups=(0, middle))
            done.extend(before)
            sum_a.held = ()
        for part in (sum_b, sum_a, sum_o, packed):
            if part is not None:
                part.step()
        slot += 1
    while packed.todo:
        packed.step()
    grad_wq, grad_wk, grad_wv = finish(
        *sum_b.held, many=3, groups=(middle, groups), before=before
    )
    small_total = small
    if paired:
        grad_w_out, grad_w_in = done[0], done[2]
    else:
        produced = (gating[:, :1] * cot_rows.astype(F32)).astype(BF)
        grad_w_in, grad_w_out = (
            lax.psum_scatter(
                dot(left, right, 0, 0).astype(BF), "batch", scatter_dimension=0, tiled=True
            ).astype(F32)
            for left, right in ((expert_normed, grad_hidden), (active, produced))
        )
    part = width // copies
    packed = packed.held[0]
    return (
        outputs,
        grad_tokens,
        packed[:part],
        packed[part : 2 * part],
        grad_wq,
        grad_wk,
        grad_wv,
        grad_wo,
        small_total[0][None],
        small_total[1][None],
        small_total[2][None],
        grad_w_in[None],
        grad_w_out[None],
        packed[2 * part :],
    )


def solution(mesh):
    both = P(("expert", "batch"), None)
    per_expert = P("expert", None)
    matrices = P("expert", None, None)
    return jax.shard_map(
        local,
        mesh=mesh,
        in_specs=(both,) * 4 + (P(),) * 6 + (per_expert,) * 3 + (matrices,) * 2,
        out_specs=(both, both)
        + (P("batch"),) * 2
        + (P("batch", None),) * 4
        + (P("expert", "batch"),) * 3
        + (P("expert", "batch", None),) * 2
        + (P("batch"),),
        check_vma=False,
    )
```

```python
import functools

import jax
import jax.numpy as jnp
from jax import lax
from jax.experimental import pallas as pl
from jax.experimental.pallas import tpu as pltpu
from jax.sharding import PartitionSpec as P

HEADS = 16
NORM_EPSILON = 1e-05
NEG_FILL = -1e30
LOG2E = 1.4426950408889634
GROUP = 256
CORES = 2
TILE = 512
COST = 1.15e9
VMEM_MIB = {'gradient_entry': 20, 'attention_backward': 44, 'tokens_gradient': 44, 'grad_w_out': 20, 'gradients_out': 16, 'output_rows': 16}
BF = jnp.bfloat16
F32 = jnp.float32


def dot(a, b, ca, cb):
    return lax.dot_general(a, b, (((ca,), (cb,)), ((), ())), preferred_element_type=F32)


def kernel_call(body, name, operands, micros, after=(), in_specs=None, grid_spec=None, **more):
    given, extra = len(operands), len(after)

    def run(*refs):
        body(*refs[:given], *refs[given + extra :])

    unread = [anywhere()] * extra
    if grid_spec is not None:
        prefetched, grid, in_specs, out_specs = grid_spec
        more["grid_spec"] = pltpu.PrefetchScalarGridSpec(
            num_scalar_prefetch=prefetched,
            grid=grid,
            in_specs=in_specs + unread,
            out_specs=out_specs,
            scratch_shapes=more.pop("scratch_shapes", ()),
        )
    else:
        if in_specs is None:
            in_specs = [in_vmem()] * given
        more["in_specs"] = in_specs + unread
    return pl.pallas_call(
        run,
        name=name,
        compiler_params=pltpu.CompilerParams(vmem_limit_bytes=VMEM_MIB.get(name, 60) << 20),
        cost_estimate=pl.CostEstimate(
            flops=int(micros * COST), transcendentals=0, bytes_accessed=0
        ),
        **more,
    )(*operands, *after)


def shaped(shape, kind):
    return jax.ShapeDtypeStruct(shape, kind)


def fixed(*shape):
    return pl.BlockSpec(shape, lambda *place: (0,) * len(shape))


def in_vmem():
    return pl.BlockSpec(memory_space=pltpu.VMEM)


def anywhere():
    return pl.BlockSpec(memory_space=pl.ANY)


def scalar():
    return pl.BlockSpec(memory_space=pltpu.SMEM)


def as_column(row):
    return jnp.transpose(jnp.broadcast_to(row, (8, row.shape[1])))[:, :1]


def standardized(values):
    center = values - jnp.mean(values, axis=-1, keepdims=True)
    spread = jnp.mean(center * center, axis=-1, keepdims=True)
    inverse = lax.rsqrt(spread + NORM_EPSILON)
    return center * inverse, inverse


def norm_backward(grad, unit, inverse):
    mean = jnp.mean(grad, axis=-1, keepdims=True)
    slope = jnp.mean(grad * unit, axis=-1, keepdims=True)
    return inverse * (grad - mean - unit * slope)


def query_blocks(count):
    size = min(256, count)
    blocks, place = [], 0
    for first in range(0, count, size):
        blocks.append((first, size, first + size, place))
        place += first + size
    return blocks, place


def stacked(part, first, size, head_size):
    lane = lax.broadcasted_iota(jnp.int32, (1, GROUP), 1) // head_size
    rows = part[first : first + size]
    return jnp.concatenate(
        [
            jnp.where(lane == head, rows, jnp.zeros_like(rows))
            for head in range(GROUP // head_size)
        ],
        0,
    )


def picked(rows, size, head_size):
    lane = lax.broadcasted_iota(jnp.int32, (1, GROUP), 1) // head_size
    out = rows[:size]
    for head in range(1, GROUP // head_size):
        out = jnp.where(lane == head, rows[head * size : (head + 1) * size], out)
    return out


def split_cores(whole_ref, place_ref, send_ref, keep_ref):
    copies, rows, _ = send_ref.shape
    place = place_ref[0]
    for copy in range(copies):
        start = copy * CORES * rows
        keep = pl.multiple_of(start + place * rows, rows)
        send = pl.multiple_of(start + (1 - place) * rows, rows)
        keep_ref[copy] = whole_ref[pl.ds(keep, rows), :]
        send_ref[copy] = whole_ref[pl.ds(send, rows), :]


def order_kernel(values_ref, slots_ref, ordered_ref):
    count = values_ref.shape[0]
    picks = as_column(slots_ref[...]) == lax.broadcasted_iota(jnp.int32, (count, count), 1)
    ordered_ref[...] = dot(picks.astype(BF), values_ref[...], 1, 0).astype(BF)


def order_rows(values, slots):
    return kernel_call(
        order_kernel, "order_rows", (values, slots), 3, out_shape=shaped(values.shape, BF)
    )


def restored(slots_ref, returned_ref):
    count = returned_ref.shape[0]
    picks = slots_ref[...] == lax.broadcasted_iota(jnp.int32, (count, count), 0)
    return dot(picks.astype(BF), returned_ref[...], 1, 0)


def output_kernel(returned_ref, slots_ref, stream_ref, out_ref):
    out_ref[...] = (stream_ref[...] + restored(slots_ref, returned_ref)).astype(BF)


def output_rows(returned, slots, stream, after=()):
    return kernel_call(
        output_kernel,
        "output_rows",
        (returned, slots, stream),
        4,
        after,
        out_shape=shaped(returned.shape, BF),
    )


def entry_kernel(
    returned_ref, slots_ref, cot_ref, mixed_ref, place_ref, attended_ref, send_ref, keep_ref, whole_ref
):
    stream = cot_ref[...].astype(F32) + restored(slots_ref, returned_ref)
    attended = stream.astype(BF)
    attended_ref[...] = attended
    whole_ref[...] = dot(mixed_ref[...], attended, 0, 0).astype(BF)
    split_cores(whole_ref, place_ref, send_ref, keep_ref)


def gradient_entry(returned, slots, cot, mixed, place, copies, after):
    count, width = cot.shape
    half = (copies, width // (CORES * copies), width)
    return kernel_call(
        entry_kernel,
        "gradient_entry",
        (returned, slots, cot, mixed, place),
        4,
        after,
        in_specs=[in_vmem()] * 4 + [scalar()],
        out_shape=[shaped((count, width), BF)] + [shaped(half, BF)] * 2,
        scratch_shapes=[pltpu.VMEM((width, width), BF)],
    )


def attention_kernel(
    head_size,
    tokens_ref,
    gain_ref,
    bias_ref,
    segment_ref,
    slots_ref,
    wq_hbm,
    wk_hbm,
    wv_hbm,
    wo_hbm,
    normed_hbm,
    q_hbm,
    k_hbm,
    v_hbm,
    mixed_hbm,
    probs_hbm,
    stream_hbm,
    ordered_ref,
    mask_ref,
    weight_ref,
    normed_ref,
    q_ref,
    k_ref,
    v_ref,
    mixed_ref,
    probs_ref,
    stream_ref,
    in_sem,
    out_sem,
):
    count, width = tokens_ref.shape
    blocks, _ = query_blocks(count)
    per = GROUP // head_size
    weights = [
        pltpu.make_async_copy(array, weight_ref.at[i], in_sem.at[i])
        for i, array in enumerate((wq_hbm, wk_hbm, wv_hbm, wo_hbm))
    ]
    for copy in weights:
        copy.start()
    sent = []

    def send(buffer_ref, array_ref):
        sent.append(pltpu.make_async_copy(buffer_ref, array_ref, out_sem.at[len(sent)]))
        sent[-1].start()

    values = tokens_ref[...].astype(F32)
    unit, _ = standardized(values)
    normed = unit * gain_ref[...].astype(F32) + bias_ref[...].astype(F32)
    normed_ref[...] = normed.astype(BF)
    send(normed_ref, normed_hbm)
    segment = segment_ref[...]
    column = as_column(segment)
    for first, size, keys, place in blocks:
        shape = (keys, size)
        query = first + lax.broadcasted_iota(jnp.int32, shape, 1)
        later = lax.broadcasted_iota(jnp.int32, shape, 0) <= query
        same = column[:keys] == segment[:, first : first + size]
        mask_ref[place : place + keys, :] = jnp.where(later & same, 0.0, NEG_FILL)

    for i, (out_ref, out_hbm) in enumerate(((q_ref, q_hbm), (k_ref, k_hbm), (v_ref, v_hbm))):
        weights[i].wait()
        out_ref[...] = dot(normed_ref[...], weight_ref[i], 1, 0).astype(BF)
        send(out_ref, out_hbm)
    scale = head_size**-0.5 * LOG2E
    for group in range(width // GROUP):
        lanes = slice(group * GROUP, (group + 1) * GROUP)
        queries = q_ref[:, lanes]
        for first, size, keys, place in blocks:
            scores = dot(k_ref[:keys, lanes], stacked(queries, first, size, head_size), 1, 1)
            masks = mask_ref[place : place + keys, :]
            parts = []
            for head in range(per):
                own = scores[:, head * size : (head + 1) * size] * scale + masks
                terms = jnp.exp2(own - jnp.max(own, axis=0, keepdims=True))
                probs = (terms * (1.0 / jnp.sum(terms, axis=0, keepdims=True))).astype(BF)
                probs_ref[group * per + head, place : place + keys, :] = probs
                parts.append(probs)
            mixed = dot(jnp.concatenate(parts, 1), v_ref[:keys, lanes], 0, 0)
            mixed_ref[first : first + size, lanes] = picked(mixed, size, head_size).astype(BF)
        heads = pl.ds(group * per, per)
        send(probs_ref.at[heads], probs_hbm.at[heads])
    send(mixed_ref, mixed_hbm)
    weights[3].wait()
    stream = tokens_ref[...].astype(F32) + dot(mixed_ref[...], weight_ref[3], 1, 0)
    stream_ref[...] = stream
    send(stream_ref, stream_hbm)
    picks = as_column(slots_ref[...]) == lax.broadcasted_iota(jnp.int32, (count, count), 1)
    ordered_ref[...] = dot(picks.astype(BF), stream.astype(BF), 1, 0).astype(BF)
    for copy in sent:
        copy.wait()


def attention_forward(tokens, gain, bias, segment, slots, wq, wk, wv, wo):
    count, width = tokens.shape
    blocks, area = query_blocks(count)
    size = blocks[0][1]
    rows = [shaped((count, width), BF)] * 5
    kept = rows + [shaped((HEADS, area, size), BF), shaped((count, width), F32)]
    return kernel_call(
        functools.partial(attention_kernel, width // HEADS),
        "attention_forward",
        (tokens, gain, bias, segment, slots, wq, wk, wv, wo),
        17,
        in_specs=[in_vmem()] * 5 + [anywhere()] * 4,
        out_specs=[anywhere()] * 7 + [in_vmem()],
        out_shape=kept + [shaped((count, width), BF)],
        scratch_shapes=[pltpu.VMEM((area, size), F32), pltpu.VMEM((4, width, width), BF)]
        + [pltpu.VMEM(array.shape, array.dtype) for array in kept]
        + [pltpu.SemaphoreType.DMA((4,)), pltpu.SemaphoreType.DMA((6 + width // GROUP,))],
    )


def backward_kernel(
    head_size,
    attended_ref,
    normed_ref,
    q_ref,
    k_ref,
    v_ref,
    mixed_ref,
    probs_ref,
    wo_ref,
    place_ref,
    send_ref,
    keep_ref,
    grads_ref,
    whole_ref,
):
    count = attended_ref.shape[0]
    blocks, _ = query_blocks(count)
    per = GROUP // head_size
    scale = head_size**-0.5
    queries, key_rows, value_rows = q_ref[...], k_ref[...], v_ref[...]
    grad_mixed = dot(attended_ref[...], wo_ref[...], 1, 1).astype(BF)
    products = grad_mixed.astype(F32) * mixed_ref[...].astype(F32)
    high = products.astype(BF)
    low = (products - high.astype(F32)).astype(BF)
    lane = lax.broadcasted_iota(jnp.int32, (16, GROUP), 1) // head_size
    heads = (lane == lax.broadcasted_iota(jnp.int32, (16, GROUP), 0)).astype(BF)
    centre = dot(heads, high, 1, 1) + dot(heads, low, 1, 1)
    grad_q = []
    grad_k = jnp.zeros((count, GROUP), F32)
    grad_v = jnp.zeros((count, GROUP), F32)
    for first, size, keys, place in blocks:
        grads = stacked(grad_mixed, first, size, head_size)
        grad_probs = dot(value_rows[:keys], grads, 1, 1)
        probs, scores = [], []
        for head in range(per):
            own = probs_ref[head, place : place + keys, :]
            off = grad_probs[:, head * size : (head + 1) * size]
            off = off - centre[head : head + 1, first : first + size]
            probs.append(own)
            scores.append((own.astype(F32) * off).astype(BF))
        probs = jnp.concatenate(probs, 1)
        scores = jnp.concatenate(scores, 1)
        grad_q.append(picked(dot(scores, key_rows[:keys], 0, 0), size, head_size))
        more_v = dot(probs, grads, 1, 0)
        more_k = dot(scores, stacked(queries, first, size, head_size), 1, 0)
        if keys < count:
            rest = jnp.zeros((count - keys, GROUP), F32)
            more_v = jnp.concatenate([more_v, rest], 0)
            more_k = jnp.concatenate([more_k, rest], 0)
        grad_v = grad_v + more_v
        grad_k = grad_k + more_k
    grad_q = jnp.concatenate(grad_q, 0) * scale
    joined = [grad.astype(BF) for grad in (grad_q, grad_k * scale, grad_v)]
    for i, grad in enumerate(joined):
        grads_ref[i] = grad
    whole_ref[...] = dot(normed_ref[...], jnp.concatenate(joined, 1), 0, 0).astype(BF)
    split_cores(whole_ref, place_ref, send_ref, keep_ref)


def attention_backward(groups, saved, attended, w_output, place, copies, after):
    normed, q, k, v, mixed, probs = saved
    count, width = attended.shape
    head_size = width // HEADS
    _, area, size = probs.shape
    start, stop = groups
    all_rows = fixed(count, width)
    part = pl.BlockSpec((count, GROUP), lambda g: (0, start + g))
    rows = width // (CORES * copies)
    half = shaped((copies, rows, 3 * GROUP * (stop - start)), BF)
    half_spec = pl.BlockSpec((copies, rows, 3 * GROUP), lambda g: (0, 0, g))
    specs = [all_rows, all_rows, part, part, part, part]
    specs += [pl.BlockSpec((GROUP // head_size, area, size), lambda g: (start + g, 0, 0))]
    specs += [pl.BlockSpec((GROUP, width), lambda g: (start + g, 0)), scalar()]
    return kernel_call(
        functools.partial(backward_kernel, head_size),
        "attention_backward",
        (attended, normed, q, k, v, mixed, probs, w_output, place),
        6 * (stop - start),
        after,
        grid=(stop - start,),
        in_specs=specs,
        out_specs=[half_spec, half_spec, pl.BlockSpec((3, count, GROUP), lambda g: (0, 0, g))],
        out_shape=[half, half, shaped((3, count, GROUP * (stop - start)), BF)],
        scratch_shapes=[pltpu.VMEM((width, 3 * GROUP), BF)],
    )


def tokens_kernel(parts, *refs):
    grads, weights = refs[:parts], refs[parts : parts + 3]
    tokens_ref, gain_ref, returned_ref, slots_ref, cot_ref = refs[parts + 3 : parts + 8]
    grad_ref, sums_ref, weight_ref, sems = refs[parts + 8 :]
    copies = [
        pltpu.make_async_copy(weight, weight_ref.at[i], sems.at[i])
        for i, weight in enumerate(weights)
    ]
    for copy in copies:
        copy.start()
    total = None
    for i in range(3):
        copies[i].wait()
        at = 0
        for grad in grads:
            columns = grad.shape[2]
            more = dot(grad[i], weight_ref[i, :, at : at + columns], 1, 1)
            total = more if total is None else total + more
            at += columns
    unit, inverse = standardized(tokens_ref[...].astype(F32))
    sums_ref[0:1, :] = jnp.sum(total * unit, axis=0, keepdims=True)
    sums_ref[1:2, :] = jnp.sum(total, axis=0, keepdims=True)
    grad = norm_backward(total * gain_ref[...].astype(F32), unit, inverse)
    stream = cot_ref[...].astype(F32) + restored(slots_ref, returned_ref)
    grad_ref[...] = (stream + grad).astype(BF)


def tokens_gradient(grads, weights, tokens, gain, returned, slots, cot, after):
    count, width = tokens.shape
    operands = (*grads, *weights, tokens, gain, returned, slots, cot)
    return kernel_call(
        functools.partial(tokens_kernel, len(grads)),
        "tokens_gradient",
        operands,
        9,
        after,
        in_specs=[in_vmem()] * len(grads) + [anywhere()] * 3 + [in_vmem()] * 5,
        out_shape=[shaped((count, width), BF), shaped((8, width), F32)],
        scratch_shapes=[pltpu.VMEM((3, width, width), BF), pltpu.SemaphoreType.DMA((3,))],
    )


def tiles_of(size):
    return [slice(at, at + TILE) for at in range(0, size, TILE)]


class Tiles:
    def __init__(self, array_ref, buffer_ref, sems, axis, inward):
        self.copies = []
        size = buffer_ref.shape[2 if axis else 1]
        for tile in range(buffer_ref.shape[0]):
            span = pl.ds(tile * size, size)
            outside = array_ref.at[span, :] if axis == 0 else array_ref.at[:, span]
            ends = (outside, buffer_ref.at[tile]) if inward else (buffer_ref.at[tile], outside)
            self.copies.append(pltpu.make_async_copy(*ends, sems.at[tile]))

    def start(self, tile):
        self.copies[tile].start()

    def wait(self, tile):
        self.copies[tile].wait()


def tile_buffers(*arrays, size=TILE):
    scratch = []
    for rows, columns, axis in arrays:
        count = (columns if axis else rows) // size
        shape = (count, rows, size) if axis else (count, size, columns)
        scratch.append(pltpu.VMEM(shape, BF))
    scratch += [pltpu.SemaphoreType.DMA(buffer.shape[:1]) for buffer in scratch]
    return scratch


def times_out_kernel(rows_ref, wout_hbm, out_hbm, wout_ref, out_ref, wout_sem, out_sem):
    weights = Tiles(wout_hbm, wout_ref, wout_sem, 0, True)
    results = Tiles(out_hbm, out_ref, out_sem, 1, False)
    count = wout_ref.shape[0]
    for tile in range(count):
        weights.start(tile)
    for tile in range(count):
        weights.wait(tile)
        out_ref[tile] = dot(rows_ref[...], wout_ref[tile], 1, 1).astype(BF)
        results.start(tile)
    for tile in range(count):
        results.wait(tile)


def times_out(rows, wout, after=()):
    count, width = rows.shape
    hidden = wout.shape[0]
    return kernel_call(
        times_out_kernel,
        "rows_times_w_out",
        (rows, wout),
        7,
        after,
        in_specs=[in_vmem(), anywhere()],
        out_specs=anywhere(),
        out_shape=shaped((count, hidden), BF),
        scratch_shapes=tile_buffers((hidden, width, 0), (count, hidden, 1)),
    )


def branch_kernel(
    active_hbm, wout_hbm, gate_ref, out_ref, active_ref, wout_ref, active_sem, wout_sem
):
    weights = Tiles(wout_hbm, wout_ref, wout_sem, 0, True)
    actives = Tiles(active_hbm, active_ref, active_sem, 1, True)
    count = wout_ref.shape[0]
    for tile in range(count):
        weights.start(tile)
        actives.start(tile)
    total = None
    for tile in range(count):
        weights.wait(tile)
        actives.wait(tile)
        more = dot(active_ref[tile], wout_ref[tile], 1, 0)
        total = more if total is None else total + more
    out_ref[...] = (total * gate_ref[:, :1]).astype(BF)


def branch_rows(active, wout, gating, after=()):
    count, hidden = active.shape
    width = wout.shape[1]
    return kernel_call(
        branch_kernel,
        "branch",
        (active, wout, gating),
        7,
        after,
        in_specs=[anywhere(), anywhere(), in_vmem()],
        out_shape=shaped((count, width), BF),
        scratch_shapes=tile_buffers((count, hidden, 1), (hidden, width, 0)),
    )


def gelu_parts(hidden):
    slant = 0.7978845608028654
    bend = slant * 0.044715
    square = hidden * hidden
    half = 0.5 + 0.5 * jnp.tanh(hidden * (slant + bend * square))
    active = hidden * half
    return active, half + active * (1.0 - half) * (2 * slant + 6 * bend * square)


def expert_start(rows_ref, gain_ref, bias_ref, center_ref, normed_ref, gate_ref):
    rows = rows_ref[...].astype(F32)
    unit, inverse = standardized(rows)
    normed_ref[...] = (unit * gain_ref[...].astype(F32) + bias_ref[...].astype(F32)).astype(BF)
    score = jnp.sum(rows * center_ref[...].astype(F32), axis=-1, keepdims=True)
    gating = 1.0 / (1.0 + jnp.exp(-score))
    gate_ref[...] = jnp.broadcast_to(gating, gate_ref.shape)
    return unit, inverse


def own_kernel(
    rows_ref,
    u_hbm,
    win_hbm,
    gain_ref,
    bias_ref,
    center_ref,
    active_hbm,
    hidden_hbm,
    normed_hbm,
    gate_ref,
    grad_ref,
    sums_ref,
    unit_ref,
    total_ref,
    normed_ref,
    normed_sem,
    u_ref,
    win_ref,
    active_ref,
    hidden_ref,
    u_sem,
    win_sem,
    active_sem,
    hidden_sem,
):
    weights = Tiles(win_hbm, win_ref, win_sem, 1, True)
    us = Tiles(u_hbm, u_ref, u_sem, 1, True)
    actives = Tiles(active_hbm, active_ref, active_sem, 1, False)
    hiddens = Tiles(hidden_hbm, hidden_ref, hidden_sem, 1, False)
    count = win_ref.shape[0]
    for tile in range(count):
        weights.start(tile)
        us.start(tile)
    unit, inverse = expert_start(rows_ref, gain_ref, bias_ref, center_ref, normed_ref, gate_ref)
    unit_ref[...] = unit
    normed_out = pltpu.make_async_copy(normed_ref, normed_hbm, normed_sem)
    normed_out.start()
    lanes = gate_ref.shape[1]
    scores = jnp.zeros((unit.shape[0], lanes), F32)
    for tile in range(count):
        weights.wait(tile)
        us.wait(tile)
        active, slope = gelu_parts(dot(normed_ref[...], win_ref[tile], 1, 0))
        active = active.astype(BF)
        active_ref[tile] = active
        actives.start(tile)
        u = u_ref[tile].astype(F32)
        hidden_ref[tile] = (slope * (u * gate_ref[:, :1])).astype(BF)
        hiddens.start(tile)
        products = active.astype(F32) * u
        for place in range(0, products.shape[1], lanes):
            scores = scores + products[:, place : place + lanes]
        more = dot(hidden_ref[tile], win_ref[tile], 1, 1)
        if tile:
            total_ref[...] += more
        else:
            total_ref[...] = more
    total = total_ref[...]
    gating = gate_ref[:, :1]
    grad_gating = jnp.sum(scores, axis=-1, keepdims=True)
    grad_score = grad_gating * gating * (1.0 - gating)
    unit = unit_ref[...]
    rows = rows_ref[...].astype(F32)
    sums_ref[0:1, :] = jnp.sum(total * unit, axis=0, keepdims=True)
    sums_ref[1:2, :] = jnp.sum(total, axis=0, keepdims=True)
    sums_ref[2:3, :] = jnp.sum(rows * grad_score, axis=0, keepdims=True)
    grad = norm_backward(total * gain_ref[...].astype(F32), unit, inverse)
    grad_ref[...] = (grad + grad_score * center_ref[...].astype(F32)).astype(BF)
    normed_out.wait()
    for tile in range(count):
        actives.wait(tile)
        hiddens.wait(tile)


def expert_own(rows, u, win, gain, bias, center, after=()):
    count, width = rows.shape
    hidden = win.shape[1]
    outs = [shaped((count, hidden), BF)] * 2 + [shaped((count, width), BF)]
    outs += [shaped((count, 128), F32), shaped((count, width), BF), shaped((8, width), F32)]
    wide = (count, hidden, 1)
    return kernel_call(
        own_kernel,
        "expert_own",
        (rows, u, win, gain, bias, center),
        19,
        after,
        in_specs=[in_vmem()] + [anywhere()] * 2 + [in_vmem()] * 3,
        out_specs=[anywhere()] * 3 + [in_vmem()] * 3,
        out_shape=outs,
        scratch_shapes=[pltpu.VMEM((count, width), F32)] * 2
        + [pltpu.VMEM((count, width), BF), pltpu.SemaphoreType.DMA(())]
        + tile_buffers(wide, (width, hidden, 1), wide, wide),
    )


def other_kernel(
    rows_ref,
    cot_ref,
    copy_ref,
    win_hbm,
    wout_hbm,
    gain_ref,
    bias_ref,
    center_ref,
    active_hbm,
    hidden_hbm,
    normed_hbm,
    gate_ref,
    normed_ref,
    normed_sem,
    produced_ref,
    win_ref,
    wout_ref,
    active_ref,
    hidden_ref,
    win_sem,
    wout_sem,
    active_sem,
    hidden_sem,
):
    weights = Tiles(win_hbm, win_ref, win_sem, 1, True)
    back = Tiles(wout_hbm, wout_ref, wout_sem, 0, True)
    hiddens = Tiles(hidden_hbm, hidden_ref, hidden_sem, 1, False)
    count = win_ref.shape[0]
    size = win_ref.shape[2]
    part = active_hbm.shape[1] // size
    for tile in range(count):
        weights.start(tile)
        back.start(tile)
    expert_start(rows_ref, gain_ref, bias_ref, center_ref, normed_ref, gate_ref)
    normed_out = pltpu.make_async_copy(normed_ref, normed_hbm, normed_sem)
    normed_out.start()
    produced_ref[...] = (gate_ref[:, :1] * cot_ref[...].astype(F32)).astype(BF)

    def active_out(tile):
        place = tile % part
        return pltpu.make_async_copy(
            active_ref.at[tile],
            active_hbm.at[:, pl.ds(place * size, size)],
            active_sem.at[place],
        )

    for tile in range(count):
        weights.wait(tile)
        back.wait(tile)
        active, slope = gelu_parts(dot(normed_ref[...], win_ref[tile], 1, 0))
        active_ref[tile] = active.astype(BF)

        @pl.when(copy_ref[0] == tile // part)
        def _(tile=tile):
            active_out(tile).start()

        hidden_ref[tile] = (slope * dot(produced_ref[...], wout_ref[tile], 1, 1)).astype(BF)
        hiddens.start(tile)
    normed_out.wait()
    for tile in range(part):
        active_out(tile).wait()
    for tile in range(count):
        hiddens.wait(tile)


def expert_other(rows, cot, copy, copies, win, wout, gain, bias, center, after=()):
    count, width = rows.shape
    hidden = win.shape[1]
    wide = (count, hidden, 1)
    outs = [shaped((count, hidden // copies), BF), shaped((count, hidden), BF)]
    outs += [shaped((count, width), BF), shaped((count, 128), F32)]
    size = min(2 * TILE, hidden // copies)
    buffers = tile_buffers((width, hidden, 1), (hidden, width, 0), wide, wide, size=size)
    return kernel_call(
        other_kernel,
        "expert_other",
        (rows, cot, copy, win, wout, gain, bias, center),
        18,
        after,
        in_specs=[in_vmem()] * 2 + [scalar()] + [anywhere()] * 2 + [in_vmem()] * 3,
        out_specs=[anywhere()] * 3 + [in_vmem()],
        out_shape=outs,
        scratch_shapes=[pltpu.VMEM((count, width), BF), pltpu.SemaphoreType.DMA(())]
        + [pltpu.VMEM((count, width), BF)]
        + buffers,
    )


def grad_in_kernel(copy_ref, left_ref, left_other_ref, right_ref, right_other_ref, out_ref):
    del copy_ref
    out_ref[...] = dot(left_ref[...], right_ref[...], 0, 0) + dot(
        left_other_ref[...], right_other_ref[...], 0, 0
    )


def grad_in(copy, copies, normed, normed_other, hidden, hidden_other, after=()):
    count, width = normed.shape
    part = width // copies
    tile = min(2 * TILE, hidden.shape[1])
    left = pl.BlockSpec((count, part), lambda i, copy: (0, copy[0]))
    right = pl.BlockSpec((count, tile), lambda i, copy: (0, i))
    return kernel_call(
        grad_in_kernel,
        "grad_w_in",
        (copy, normed, normed_other, hidden, hidden_other),
        10,
        after,
        grid_spec=(
            1,
            (hidden.shape[1] // tile,),
            [left, left, right, right],
            pl.BlockSpec((part, tile), lambda i, copy: (0, i)),
        ),
        out_shape=shaped((part, hidden.shape[1]), F32),
    )


def grad_out_kernel(
    copy_ref,
    left_ref,
    left_other_ref,
    cot_ref,
    cot_other_ref,
    gate_ref,
    gate_other_ref,
    out_ref,
    right_ref,
    right_other_ref,
):
    del copy_ref

    @pl.when(pl.program_id(0) == 0)
    def _():
        right_ref[...] = (gate_ref[:, :1] * cot_ref[...].astype(F32)).astype(BF)
        right_other_ref[...] = (gate_other_ref[:, :1] * cot_other_ref[...].astype(F32)).astype(BF)

    out_ref[...] = dot(left_ref[...], right_ref[...], 0, 0) + dot(
        left_other_ref[...], right_other_ref[...], 0, 0
    )


def grad_out(copy, copies, active, active_other, cot, cot_other, gate, gate_other, after=()):
    count, width = cot.shape
    part = active.shape[1] // copies
    tile = min(TILE, part)
    tiles = part // tile
    left = pl.BlockSpec((count, tile), lambda i, copy: (0, copy[0] * tiles + i))
    left_other = pl.BlockSpec((count, tile), lambda i, copy: (0, i))
    right = pl.BlockSpec((count, width), lambda i, copy: (0, 0))
    gates = pl.BlockSpec(gate.shape, lambda i, copy: (0, 0))
    return kernel_call(
        grad_out_kernel,
        "grad_w_out",
        (copy, active, active_other, cot, cot_other, gate, gate_other),
        10,
        after,
        grid_spec=(
            1,
            (tiles,),
            [left, left_other, right, right, gates, gates],
            pl.BlockSpec((tile, width), lambda i, copy: (i, 0)),
        ),
        out_shape=shaped((part, width), F32),
        scratch_shapes=[pltpu.VMEM((count, width), BF)] * 2,
    )


def finish_kernel(many, extra, place_ref, *refs):
    parts, outs = refs[: 2 * many], refs[2 * many + extra :]
    place = place_ref[0]
    rows = parts[0].shape[0]
    here = pl.ds(pl.multiple_of(place * rows, rows), rows)
    away = pl.ds(pl.multiple_of((1 - place) * rows, rows), rows)
    for i in range(many):
        outs[i][here, :] = parts[2 * i][...].astype(F32)
        outs[i][away, :] = parts[2 * i + 1][...].astype(F32)


def finished(own, got, *, place, many, groups, total, before=None):
    start, stop = groups
    rows = own.shape[0]
    part = [
        pl.BlockSpec((rows, GROUP), functools.partial(lambda i, g: (0, many * g + i), i))
        for i in range(many)
    ]
    extra = list(before or ())
    return kernel_call(
        functools.partial(finish_kernel, many, len(extra)),
        "gradients_out",
        [place] + [own, got] * many + extra,
        2 * many,
        grid=(stop - start,),
        in_specs=[scalar()] + [spec for spec in part for _ in range(2)] + [anywhere()] * len(extra),
        out_specs=[pl.BlockSpec((CORES * rows, GROUP), lambda g: (0, start + g))] * many,
        out_shape=[shaped((CORES * rows, total), F32)] * many,
        input_output_aliases={1 + 2 * many + i: i for i in range(len(extra))},
    )


def expert_levels(size):
    levels, stride = [], 1
    while stride < size:
        levels.append((stride, 2 if (size // stride) % 2 == 0 else size // stride))
        stride *= levels[-1][1]
    return levels


def turned(axis, stride, length, step):
    pairs = []
    for index in range(lax.axis_size(axis)):
        place = (index // stride) % length
        pairs.append((index, index + ((place + step) % length - place) * stride))
    return pairs


def scatter_level(rows, axis, stride, length, outer=1):
    place = (lax.axis_index(axis) // stride) % length
    columns = rows.shape[1]
    split = rows.reshape(outer, length, -1, columns)
    total = lax.dynamic_index_in_dim(split, place, 1, False).astype(F32)
    for step in range(1, length):
        part = lax.dynamic_index_in_dim(split, (place + step) % length, 1, False)
        part = lax.ppermute(part, axis, turned(axis, stride, length, step))
        total = total + part.astype(F32)
    return total.astype(rows.dtype).reshape(-1, columns)


def gather_level(rows, axis, stride, length):
    place = (lax.axis_index(axis) // stride) % length
    count = rows.shape[0]
    parts = [rows] + [
        lax.ppermute(rows, axis, turned(axis, stride, length, step)) for step in range(1, length)
    ]
    if length == 2:
        return jnp.where(
            place == 0, jnp.concatenate(parts, 0), jnp.concatenate([parts[1], parts[0]], 0)
        )
    whole = jnp.zeros((length * count, rows.shape[1]), rows.dtype)
    for step, part in enumerate(parts):
        whole = lax.dynamic_update_slice_in_dim(whole, part, ((place - step) % length) * count, 0)
    return whole


def tied(values, *others):
    return lax.optimization_barrier((values, others))[0]


class RowSum:
    def __init__(self, send, keep, copies_second=False):
        levels = expert_levels(lax.axis_size("expert"))
        copies = lax.axis_size("batch")
        self.held = (send, keep)
        scatters = [("batch", 1, copies)] + [("expert", *at) for at in levels[1:-1]]
        if copies_second and len(scatters) > 1:
            scatters[:2] = [(*scatters[1], copies), scatters[0]]
        self.todo = [self.cores] + [functools.partial(self.scatter, *at) for at in scatters]
        self.todo += [functools.partial(self.whole, "expert", *levels[-1])]
        self.todo += [functools.partial(self.gather, "expert", *at) for at in levels[-2:0:-1]]
        self.todo.append(self.partner)

    def step(self):
        if self.todo:
            self.todo.pop(0)()

    def cores(self):
        send, keep = self.held
        got = lax.ppermute(send, "expert", turned("expert", 1, CORES, 1))
        total = (keep.astype(F32) + got.astype(F32)).astype(BF)
        self.held = total.reshape(-1, total.shape[-1])

    def scatter(self, *level):
        self.held = scatter_level(self.held, *level)

    def gather(self, *level):
        self.held = gather_level(self.held, *level)

    def partner(self):
        self.held = (self.held, lax.ppermute(self.held, "expert", turned("expert", 1, CORES, 1)))

    def whole(self, axis, stride, length):
        total = self.held.astype(F32)
        for step in range(1, length):
            part = lax.ppermute(self.held, axis, turned(axis, stride, length, step))
            total = total + part.astype(F32)
        self.held = total.astype(BF)


class SmallSum:
    def __init__(self, values):
        self.held = values
        bits = []
        while 1 << len(bits) < lax.axis_size("expert"):
            bits.append(functools.partial(self.doubled, 1 << len(bits)))
        self.todo = [self.copies] + bits

    def step(self):
        if self.todo:
            self.todo.pop(0)()

    def copies(self):
        copies, place = lax.axis_size("batch"), lax.axis_index("batch")
        total = lax.dynamic_index_in_dim(self.held, place, 0, True)
        for step in range(1, copies):
            part = lax.dynamic_index_in_dim(self.held, (place + step) % copies, 0, True)
            total = total + lax.ppermute(part, "batch", turned("batch", 1, copies, step))
        self.held = total

    def doubled(self, bit):
        pairs = [(i, i ^ bit) for i in range(lax.axis_size("expert"))]
        self.held = self.held + lax.ppermute(self.held, "expert", pairs)


def local(
    tokens,
    cotangent,
    segment_ids,
    routing,
    ln_gain,
    ln_bias,
    w_query,
    w_key,
    w_value,
    w_output,
    expert_gain,
    expert_bias,
    centroid,
    w_in,
    w_out,
):
    count, width = tokens.shape
    owners = lax.axis_size("expert")
    copies = lax.axis_size("batch")
    copy = lax.axis_index("batch")
    place = (lax.axis_index("expert") % CORES).astype(jnp.int32)[None]
    send_rows = count // owners
    win = w_in[0]
    wout = w_out[0]

    def exchanged(values):
        return lax.all_to_all(
            values.reshape(owners, send_rows, width),
            "expert",
            split_axis=0,
            concat_axis=0,
            tiled=True,
        ).reshape(count, width)

    def from_copy(values, step):
        return lax.ppermute(values, "batch", turned("batch", 1, copies, step))

    paired = copies == 2
    cot_rows = exchanged(order_rows(cotangent, routing))
    *saved, stream, ordered = attention_forward(
        tokens,
        ln_gain[None],
        ln_bias[None],
        segment_ids,
        routing,
        w_query,
        w_key,
        w_value,
        w_output,
    )
    mixed = saved[4]
    rows = exchanged(ordered)
    cot_other = from_copy(cot_rows, 1) if paired else None
    u = times_out(cot_rows, wout)
    rows, u = tied((rows, u))
    rows_other = from_copy(rows, 1) if paired else None
    vectors = (expert_gain, expert_bias, centroid)
    active, grad_hidden, expert_normed, gating, grad_rows, sums = expert_own(
        rows, u, win, *vectors
    )

    grad_returned = exchanged(grad_rows)
    branch = branch_rows(active, wout, gating, [grad_rows])
    which = copy.astype(jnp.int32)[None]
    if paired:
        active_o, hidden_o, normed_o, gating_o = expert_other(
            rows_other, cot_other, which, copies, win, wout, *vectors, [branch]
        )
        branch, active_o = tied((branch, active_o))
    grad_returned = tied(grad_returned, branch)

    attended, send, keep = gradient_entry(
        grad_returned, routing, cotangent, mixed, place, copies, [branch]
    )
    sum_o = RowSum(send, keep, True)
    groups = width // GROUP
    middle = groups // 2
    backward = functools.partial(attention_backward, saved=saved, attended=attended, w_output=w_output)
    send, keep, grads_a = backward((0, middle), place=place, copies=copies, after=[attended])
    sum_o.step()
    sum_o.held, send, keep = tied((sum_o.held, send, keep))
    sum_a = RowSum(send, keep)
    sum_a.step()
    sum_a.held, sum_o.held = tied((sum_a.held, sum_o.held))
    send, keep, grads_b = backward((middle, groups), place=place, copies=copies, after=[sum_a.held])
    sum_o.step()
    sum_a.step()
    sum_a.held, sum_o.held, send, keep = tied((sum_a.held, sum_o.held, send, keep))
    sum_b = RowSum(send, keep)
    sum_b.step()
    sum_o.step()
    branch = exchanged(tied(branch, grads_b))

    gate_vector = jnp.where(
        jnp.arange(owners) == lax.axis_index("expert"),
        jnp.sum(gating[:, 0]) / (count * copies),
        0.0,
    )
    small = sums[:3].reshape(3, copies, width // copies)
    slot = 0
    done = []
    packed = None
    finish = functools.partial(finished, place=place, total=width)
    while sum_b.todo:
        parts = [part for part in (sum_b, sum_a, sum_o, packed) if part is not None]
        if slot:
            held, small, done = tied(([part.held for part in parts], small, done))
            for part, value in zip(parts, held):
                part.held = value
        if slot == 0 and paired:
            done.append(
                grad_out(
                    which, copies, active, active_o, cot_rows, cot_other, gating, gating_o,
                    [sum_b.held],
                )
            )
        if slot == 0:
            small_total = lax.dynamic_index_in_dim(small, copy, 1, False)
            for step in range(1, copies):
                away = lax.dynamic_index_in_dim(small, (copy + step) % copies, 1, False)
                small_total = small_total + from_copy(away, step)
            small = small_total
        if slot == 0:
            grad_tokens, norm_sums = tokens_gradient(
                (grads_a, grads_b),
                (w_query, w_key, w_value),
                tokens,
                ln_gain[None],
                grad_returned,
                routing,
                cotangent,
                [sum_b.held],
            )
            done += [grad_tokens, norm_sums]
        if slot == 1:
            norm_sums = done.pop()
            packed = SmallSum(
                jnp.concatenate(
                    [
                        norm_sums[0].reshape(copies, -1),
                        norm_sums[1].reshape(copies, -1),
                        gate_vector.reshape(copies, -1),
                    ],
                    axis=1,
                )
            )
        if slot == 2:
            if paired:
                done.append(
                    grad_in(
                        which, copies, expert_normed, normed_o, grad_hidden, hidden_o, [sum_b.held]
                    )
                )
        if slot == 4:
            branch = tied(branch, sum_b.held)
            outputs = output_rows(branch, routing, stream)
            done.append(outputs)
        if not sum_o.todo and sum_o.held:
            (grad_wo,) = finish(*sum_o.held, many=1, groups=(0, groups))
            done.append(grad_wo)
            sum_o.held = ()
        if not sum_a.todo and sum_a.held:
            before = finish(*sum_a.held, many=3, groups=(0, middle))
            done.extend(before)
            sum_a.held = ()
        if slot == 0:
            sum_a.held, sum_o.held = tied((sum_a.held, sum_o.held), sum_b.held)
        for part in (sum_b, sum_a, sum_o, packed):
            if part is not None:
                part.step()
        slot += 1
    while packed.todo:
        packed.step()
    grad_wq, grad_wk, grad_wv = finish(
        *sum_b.held, many=3, groups=(middle, groups), before=before
    )
    small_total = small
    if paired:
        grad_w_out, grad_w_in = done[0], done[2]
    else:
        produced = (gating[:, :1] * cot_rows.astype(F32)).astype(BF)
        grad_w_in, grad_w_out = (
            lax.psum_scatter(
                dot(left, right, 0, 0).astype(BF), "batch", scatter_dimension=0, tiled=True
            ).astype(F32)
            for left, right in ((expert_normed, grad_hidden), (active, produced))
        )
    part = width // copies
    packed = packed.held[0]
    return (
        outputs,
        grad_tokens,
        packed[:part],
        packed[part : 2 * part],
        grad_wq,
        grad_wk,
        grad_wv,
        grad_wo,
        small_total[0][None],
        small_total[1][None],
        small_total[2][None],
        grad_w_in[None],
        grad_w_out[None],
        packed[2 * part :],
    )


def solution(mesh):
    both = P(("expert", "batch"), None)
    per_expert = P("expert", None)
    matrices = P("expert", None, None)
    return jax.shard_map(
        local,
        mesh=mesh,
        in_specs=(both,) * 4 + (P(),) * 6 + (per_expert,) * 3 + (matrices,) * 2,
        out_specs=(both, both)
        + (P("batch"),) * 2
        + (P("batch", None),) * 4
        + (P("expert", "batch"),) * 3
        + (P("expert", "batch", None),) * 2
        + (P("batch"),),
        check_vma=False,
    )
```

```python
import functools

import jax
import jax.numpy as jnp
from jax import lax
from jax.experimental import pallas as pl
from jax.experimental.pallas import tpu as pltpu
from jax.sharding import PartitionSpec as P

HEADS = 16
NORM_EPSILON = 1e-05
NEG_FILL = -1e30
LOG2E = 1.4426950408889634
GROUP = 256
CORES = 2
TILE = 512
COST = 1.15e9
VMEM_MIB = {'gradient_entry': 20, 'attention_backward': 44, 'tokens_gradient': 44, 'grad_w_out': 20, 'gradients_out': 16, 'output_rows': 16}
BF = jnp.bfloat16
F32 = jnp.float32


def dot(a, b, ca, cb):
    return lax.dot_general(a, b, (((ca,), (cb,)), ((), ())), preferred_element_type=F32)


def kernel_call(body, name, operands, micros, after=(), in_specs=None, grid_spec=None, **more):
    given, extra = len(operands), len(after)

    def run(*refs):
        body(*refs[:given], *refs[given + extra :])

    unread = [anywhere()] * extra
    if grid_spec is not None:
        prefetched, grid, in_specs, out_specs = grid_spec
        more["grid_spec"] = pltpu.PrefetchScalarGridSpec(
            num_scalar_prefetch=prefetched,
            grid=grid,
            in_specs=in_specs + unread,
            out_specs=out_specs,
            scratch_shapes=more.pop("scratch_shapes", ()),
        )
    else:
        if in_specs is None:
            in_specs = [in_vmem()] * given
        more["in_specs"] = in_specs + unread
    return pl.pallas_call(
        run,
        name=name,
        compiler_params=pltpu.CompilerParams(vmem_limit_bytes=VMEM_MIB.get(name, 60) << 20),
        cost_estimate=pl.CostEstimate(
            flops=int(micros * COST), transcendentals=0, bytes_accessed=0
        ),
        **more,
    )(*operands, *after)


def shaped(shape, kind):
    return jax.ShapeDtypeStruct(shape, kind)


def fixed(*shape):
    return pl.BlockSpec(shape, lambda *place: (0,) * len(shape))


def in_vmem():
    return pl.BlockSpec(memory_space=pltpu.VMEM)


def anywhere():
    return pl.BlockSpec(memory_space=pl.ANY)


def scalar():
    return pl.BlockSpec(memory_space=pltpu.SMEM)


def as_column(row):
    return jnp.transpose(jnp.broadcast_to(row, (8, row.shape[1])))[:, :1]


def standardized(values):
    center = values - jnp.mean(values, axis=-1, keepdims=True)
    spread = jnp.mean(center * center, axis=-1, keepdims=True)
    inverse = lax.rsqrt(spread + NORM_EPSILON)
    return center * inverse, inverse


def norm_backward(grad, unit, inverse):
    mean = jnp.mean(grad, axis=-1, keepdims=True)
    slope = jnp.mean(grad * unit, axis=-1, keepdims=True)
    return inverse * (grad - mean - unit * slope)


def query_blocks(count):
    size = min(256, count)
    blocks, place = [], 0
    for first in range(0, count, size):
        blocks.append((first, size, first + size, place))
        place += first + size
    return blocks, place


def stacked(part, first, size, head_size):
    lane = lax.broadcasted_iota(jnp.int32, (1, GROUP), 1) // head_size
    rows = part[first : first + size]
    return jnp.concatenate(
        [
            jnp.where(lane == head, rows, jnp.zeros_like(rows))
            for head in range(GROUP // head_size)
        ],
        0,
    )


def picked(rows, size, head_size):
    lane = lax.broadcasted_iota(jnp.int32, (1, GROUP), 1) // head_size
    out = rows[:size]
    for head in range(1, GROUP // head_size):
        out = jnp.where(lane == head, rows[head * size : (head + 1) * size], out)
    return out


def split_cores(whole_ref, place_ref, send_ref, keep_ref):
    copies, rows, _ = send_ref.shape
    place = place_ref[0]
    for copy in range(copies):
        start = copy * CORES * rows
        keep = pl.multiple_of(start + place * rows, rows)
        send = pl.multiple_of(start + (1 - place) * rows, rows)
        keep_ref[copy] = whole_ref[pl.ds(keep, rows), :]
        send_ref[copy] = whole_ref[pl.ds(send, rows), :]


def order_kernel(values_ref, slots_ref, ordered_ref):
    count = values_ref.shape[0]
    picks = as_column(slots_ref[...]) == lax.broadcasted_iota(jnp.int32, (count, count), 1)
    ordered_ref[...] = dot(picks.astype(BF), values_ref[...], 1, 0).astype(BF)


def order_rows(values, slots):
    return kernel_call(
        order_kernel, "order_rows", (values, slots), 3, out_shape=shaped(values.shape, BF)
    )


def restored(slots_ref, returned_ref):
    count = returned_ref.shape[0]
    picks = slots_ref[...] == lax.broadcasted_iota(jnp.int32, (count, count), 0)
    return dot(picks.astype(BF), returned_ref[...], 1, 0)


def output_kernel(returned_ref, slots_ref, stream_ref, out_ref):
    out_ref[...] = (stream_ref[...] + restored(slots_ref, returned_ref)).astype(BF)


def output_rows(returned, slots, stream, after=()):
    return kernel_call(
        output_kernel,
        "output_rows",
        (returned, slots, stream),
        4,
        after,
        out_shape=shaped(returned.shape, BF),
    )


def entry_kernel(
    returned_ref, slots_ref, cot_ref, mixed_ref, place_ref, attended_ref, send_ref, keep_ref, whole_ref
):
    stream = cot_ref[...].astype(F32) + restored(slots_ref, returned_ref)
    attended = stream.astype(BF)
    attended_ref[...] = attended
    whole_ref[...] = dot(mixed_ref[...], attended, 0, 0).astype(BF)
    split_cores(whole_ref, place_ref, send_ref, keep_ref)


def gradient_entry(returned, slots, cot, mixed, place, copies, after):
    count, width = cot.shape
    half = (copies, width // (CORES * copies), width)
    return kernel_call(
        entry_kernel,
        "gradient_entry",
        (returned, slots, cot, mixed, place),
        4,
        after,
        in_specs=[in_vmem()] * 4 + [scalar()],
        out_shape=[shaped((count, width), BF)] + [shaped(half, BF)] * 2,
        scratch_shapes=[pltpu.VMEM((width, width), BF)],
    )


def attention_kernel(
    head_size,
    tokens_ref,
    gain_ref,
    bias_ref,
    segment_ref,
    slots_ref,
    wq_hbm,
    wk_hbm,
    wv_hbm,
    wo_hbm,
    normed_hbm,
    q_hbm,
    k_hbm,
    v_hbm,
    mixed_hbm,
    probs_hbm,
    stream_hbm,
    ordered_ref,
    mask_ref,
    weight_ref,
    normed_ref,
    q_ref,
    k_ref,
    v_ref,
    mixed_ref,
    probs_ref,
    stream_ref,
    in_sem,
    out_sem,
):
    count, width = tokens_ref.shape
    blocks, _ = query_blocks(count)
    per = GROUP // head_size
    weights = [
        pltpu.make_async_copy(array, weight_ref.at[i], in_sem.at[i])
        for i, array in enumerate((wq_hbm, wk_hbm, wv_hbm, wo_hbm))
    ]
    for copy in weights:
        copy.start()
    sent = []

    def send(buffer_ref, array_ref):
        sent.append(pltpu.make_async_copy(buffer_ref, array_ref, out_sem.at[len(sent)]))
        sent[-1].start()

    values = tokens_ref[...].astype(F32)
    unit, _ = standardized(values)
    normed = unit * gain_ref[...].astype(F32) + bias_ref[...].astype(F32)
    normed_ref[...] = normed.astype(BF)
    send(normed_ref, normed_hbm)
    segment = segment_ref[...]
    column = as_column(segment)
    for first, size, keys, place in blocks:
        shape = (keys, size)
        query = first + lax.broadcasted_iota(jnp.int32, shape, 1)
        later = lax.broadcasted_iota(jnp.int32, shape, 0) <= query
        same = column[:keys] == segment[:, first : first + size]
        mask_ref[place : place + keys, :] = jnp.where(later & same, 0.0, NEG_FILL)

    for i, (out_ref, out_hbm) in enumerate(((q_ref, q_hbm), (k_ref, k_hbm), (v_ref, v_hbm))):
        weights[i].wait()
        out_ref[...] = dot(normed_ref[...], weight_ref[i], 1, 0).astype(BF)
        send(out_ref, out_hbm)
    scale = head_size**-0.5 * LOG2E
    for group in range(width // GROUP):
        lanes = slice(group * GROUP, (group + 1) * GROUP)
        queries = q_ref[:, lanes]
        for first, size, keys, place in blocks:
            scores = dot(k_ref[:keys, lanes], stacked(queries, first, size, head_size), 1, 1)
            masks = mask_ref[place : place + keys, :]
            parts = []
            for head in range(per):
                own = scores[:, head * size : (head + 1) * size] * scale + masks
                terms = jnp.exp2(own - jnp.max(own, axis=0, keepdims=True))
                probs = (terms * (1.0 / jnp.sum(terms, axis=0, keepdims=True))).astype(BF)
                probs_ref[group * per + head, place : place + keys, :] = probs
                parts.append(probs)
            mixed = dot(jnp.concatenate(parts, 1), v_ref[:keys, lanes], 0, 0)
            mixed_ref[first : first + size, lanes] = picked(mixed, size, head_size).astype(BF)
        heads = pl.ds(group * per, per)
        send(probs_ref.at[heads], probs_hbm.at[heads])
    send(mixed_ref, mixed_hbm)
    weights[3].wait()
    stream = tokens_ref[...].astype(F32) + dot(mixed_ref[...], weight_ref[3], 1, 0)
    stream_ref[...] = stream
    send(stream_ref, stream_hbm)
    picks = as_column(slots_ref[...]) == lax.broadcasted_iota(jnp.int32, (count, count), 1)
    ordered_ref[...] = dot(picks.astype(BF), stream.astype(BF), 1, 0).astype(BF)
    for copy in sent:
        copy.wait()


def attention_forward(tokens, gain, bias, segment, slots, wq, wk, wv, wo):
    count, width = tokens.shape
    blocks, area = query_blocks(count)
    size = blocks[0][1]
    rows = [shaped((count, width), BF)] * 5
    kept = rows + [shaped((HEADS, area, size), BF), shaped((count, width), F32)]
    return kernel_call(
        functools.partial(attention_kernel, width // HEADS),
        "attention_forward",
        (tokens, gain, bias, segment, slots, wq, wk, wv, wo),
        17,
        in_specs=[in_vmem()] * 5 + [anywhere()] * 4,
        out_specs=[anywhere()] * 7 + [in_vmem()],
        out_shape=kept + [shaped((count, width), BF)],
        scratch_shapes=[pltpu.VMEM((area, size), F32), pltpu.VMEM((4, width, width), BF)]
        + [pltpu.VMEM(array.shape, array.dtype) for array in kept]
        + [pltpu.SemaphoreType.DMA((4,)), pltpu.SemaphoreType.DMA((6 + width // GROUP,))],
    )


def backward_kernel(
    head_size,
    attended_ref,
    normed_ref,
    q_ref,
    k_ref,
    v_ref,
    mixed_ref,
    probs_ref,
    wo_ref,
    place_ref,
    send_ref,
    keep_ref,
    grads_ref,
    whole_ref,
):
    count = attended_ref.shape[0]
    blocks, _ = query_blocks(count)
    per = GROUP // head_size
    scale = head_size**-0.5
    queries, key_rows, value_rows = q_ref[...], k_ref[...], v_ref[...]
    grad_mixed = dot(attended_ref[...], wo_ref[...], 1, 1).astype(BF)
    products = grad_mixed.astype(F32) * mixed_ref[...].astype(F32)
    high = products.astype(BF)
    low = (products - high.astype(F32)).astype(BF)
    lane = lax.broadcasted_iota(jnp.int32, (16, GROUP), 1) // head_size
    heads = (lane == lax.broadcasted_iota(jnp.int32, (16, GROUP), 0)).astype(BF)
    centre = dot(heads, high, 1, 1) + dot(heads, low, 1, 1)
    grad_q = []
    grad_k = jnp.zeros((count, GROUP), F32)
    grad_v = jnp.zeros((count, GROUP), F32)
    for first, size, keys, place in blocks:
        grads = stacked(grad_mixed, first, size, head_size)
        grad_probs = dot(value_rows[:keys], grads, 1, 1)
        probs, scores = [], []
        for head in range(per):
            own = probs_ref[head, place : place + keys, :]
            off = grad_probs[:, head * size : (head + 1) * size]
            off = off - centre[head : head + 1, first : first + size]
            probs.append(own)
            scores.append((own.astype(F32) * off).astype(BF))
        probs = jnp.concatenate(probs, 1)
        scores = jnp.concatenate(scores, 1)
        grad_q.append(picked(dot(scores, key_rows[:keys], 0, 0), size, head_size))
        more_v = dot(probs, grads, 1, 0)
        more_k = dot(scores, stacked(queries, first, size, head_size), 1, 0)
        if keys < count:
            rest = jnp.zeros((count - keys, GROUP), F32)
            more_v = jnp.concatenate([more_v, rest], 0)
            more_k = jnp.concatenate([more_k, rest], 0)
        grad_v = grad_v + more_v
        grad_k = grad_k + more_k
    grad_q = jnp.concatenate(grad_q, 0) * scale
    joined = [grad.astype(BF) for grad in (grad_q, grad_k * scale, grad_v)]
    for i, grad in enumerate(joined):
        grads_ref[i] = grad
    whole_ref[...] = dot(normed_ref[...], jnp.concatenate(joined, 1), 0, 0).astype(BF)
    split_cores(whole_ref, place_ref, send_ref, keep_ref)


def attention_backward(groups, saved, attended, w_output, place, copies, after):
    normed, q, k, v, mixed, probs = saved
    count, width = attended.shape
    head_size = width // HEADS
    _, area, size = probs.shape
    start, stop = groups
    all_rows = fixed(count, width)
    part = pl.BlockSpec((count, GROUP), lambda g: (0, start + g))
    rows = width // (CORES * copies)
    half = shaped((copies, rows, 3 * GROUP * (stop - start)), BF)
    half_spec = pl.BlockSpec((copies, rows, 3 * GROUP), lambda g: (0, 0, g))
    specs = [all_rows, all_rows, part, part, part, part]
    specs += [pl.BlockSpec((GROUP // head_size, area, size), lambda g: (start + g, 0, 0))]
    specs += [pl.BlockSpec((GROUP, width), lambda g: (start + g, 0)), scalar()]
    return kernel_call(
        functools.partial(backward_kernel, head_size),
        "attention_backward",
        (attended, normed, q, k, v, mixed, probs, w_output, place),
        6 * (stop - start),
        after,
        grid=(stop - start,),
        in_specs=specs,
        out_specs=[half_spec, half_spec, pl.BlockSpec((3, count, GROUP), lambda g: (0, 0, g))],
        out_shape=[half, half, shaped((3, count, GROUP * (stop - start)), BF)],
        scratch_shapes=[pltpu.VMEM((width, 3 * GROUP), BF)],
    )


def tokens_kernel(parts, *refs):
    grads, weights = refs[:parts], refs[parts : parts + 3]
    tokens_ref, gain_ref, returned_ref, slots_ref, cot_ref = refs[parts + 3 : parts + 8]
    grad_ref, sums_ref, weight_ref, sems = refs[parts + 8 :]
    copies = [
        pltpu.make_async_copy(weight, weight_ref.at[i], sems.at[i])
        for i, weight in enumerate(weights)
    ]
    for copy in copies:
        copy.start()
    total = None
    for i in range(3):
        copies[i].wait()
        at = 0
        for grad in grads:
            columns = grad.shape[2]
            more = dot(grad[i], weight_ref[i, :, at : at + columns], 1, 1)
            total = more if total is None else total + more
            at += columns
    unit, inverse = standardized(tokens_ref[...].astype(F32))
    sums_ref[0:1, :] = jnp.sum(total * unit, axis=0, keepdims=True)
    sums_ref[1:2, :] = jnp.sum(total, axis=0, keepdims=True)
    grad = norm_backward(total * gain_ref[...].astype(F32), unit, inverse)
    stream = cot_ref[...].astype(F32) + restored(slots_ref, returned_ref)
    grad_ref[...] = (stream + grad).astype(BF)


def tokens_gradient(grads, weights, tokens, gain, returned, slots, cot, after):
    count, width = tokens.shape
    operands = (*grads, *weights, tokens, gain, returned, slots, cot)
    return kernel_call(
        functools.partial(tokens_kernel, len(grads)),
        "tokens_gradient",
        operands,
        9,
        after,
        in_specs=[in_vmem()] * len(grads) + [anywhere()] * 3 + [in_vmem()] * 5,
        out_shape=[shaped((count, width), BF), shaped((8, width), F32)],
        scratch_shapes=[pltpu.VMEM((3, width, width), BF), pltpu.SemaphoreType.DMA((3,))],
    )


def tiles_of(size):
    return [slice(at, at + TILE) for at in range(0, size, TILE)]


class Tiles:
    def __init__(self, array_ref, buffer_ref, sems, axis, inward):
        self.copies = []
        size = buffer_ref.shape[2 if axis else 1]
        for tile in range(buffer_ref.shape[0]):
            span = pl.ds(tile * size, size)
            outside = array_ref.at[span, :] if axis == 0 else array_ref.at[:, span]
            ends = (outside, buffer_ref.at[tile]) if inward else (buffer_ref.at[tile], outside)
            self.copies.append(pltpu.make_async_copy(*ends, sems.at[tile]))

    def start(self, tile):
        self.copies[tile].start()

    def wait(self, tile):
        self.copies[tile].wait()


def tile_buffers(*arrays, size=TILE):
    scratch = []
    for rows, columns, axis in arrays:
        count = (columns if axis else rows) // size
        shape = (count, rows, size) if axis else (count, size, columns)
        scratch.append(pltpu.VMEM(shape, BF))
    scratch += [pltpu.SemaphoreType.DMA(buffer.shape[:1]) for buffer in scratch]
    return scratch


def times_out_kernel(rows_ref, wout_hbm, out_hbm, wout_ref, out_ref, wout_sem, out_sem):
    weights = Tiles(wout_hbm, wout_ref, wout_sem, 0, True)
    results = Tiles(out_hbm, out_ref, out_sem, 1, False)
    count = wout_ref.shape[0]
    for tile in range(count):
        weights.start(tile)
    for tile in range(count):
        weights.wait(tile)
        out_ref[tile] = dot(rows_ref[...], wout_ref[tile], 1, 1).astype(BF)
        results.start(tile)
    for tile in range(count):
        results.wait(tile)


def times_out(rows, wout, after=()):
    count, width = rows.shape
    hidden = wout.shape[0]
    return kernel_call(
        times_out_kernel,
        "rows_times_w_out",
        (rows, wout),
        7,
        after,
        in_specs=[in_vmem(), anywhere()],
        out_specs=anywhere(),
        out_shape=shaped((count, hidden), BF),
        scratch_shapes=tile_buffers((hidden, width, 0), (count, hidden, 1)),
    )


def branch_kernel(
    active_hbm, wout_hbm, gate_ref, out_ref, active_ref, wout_ref, active_sem, wout_sem
):
    weights = Tiles(wout_hbm, wout_ref, wout_sem, 0, True)
    actives = Tiles(active_hbm, active_ref, active_sem, 1, True)
    count = wout_ref.shape[0]
    for tile in range(count):
        weights.start(tile)
        actives.start(tile)
    total = None
    for tile in range(count):
        weights.wait(tile)
        actives.wait(tile)
        more = dot(active_ref[tile], wout_ref[tile], 1, 0)
        total = more if total is None else total + more
    out_ref[...] = (total * gate_ref[:, :1]).astype(BF)


def branch_rows(active, wout, gating, after=()):
    count, hidden = active.shape
    width = wout.shape[1]
    return kernel_call(
        branch_kernel,
        "branch",
        (active, wout, gating),
        7,
        after,
        in_specs=[anywhere(), anywhere(), in_vmem()],
        out_shape=shaped((count, width), BF),
        scratch_shapes=tile_buffers((count, hidden, 1), (hidden, width, 0)),
    )


def gelu_parts(hidden):
    slant = 0.7978845608028654
    bend = slant * 0.044715
    square = hidden * hidden
    half = 0.5 + 0.5 * jnp.tanh(hidden * (slant + bend * square))
    active = hidden * half
    return active, half + active * (1.0 - half) * (2 * slant + 6 * bend * square)


def expert_start(rows_ref, gain_ref, bias_ref, center_ref, normed_ref, gate_ref):
    rows = rows_ref[...].astype(F32)
    unit, inverse = standardized(rows)
    normed_ref[...] = (unit * gain_ref[...].astype(F32) + bias_ref[...].astype(F32)).astype(BF)
    score = jnp.sum(rows * center_ref[...].astype(F32), axis=-1, keepdims=True)
    gating = 1.0 / (1.0 + jnp.exp(-score))
    gate_ref[...] = jnp.broadcast_to(gating, gate_ref.shape)
    return unit, inverse


def own_kernel(
    rows_ref,
    u_hbm,
    win_hbm,
    gain_ref,
    bias_ref,
    center_ref,
    active_hbm,
    hidden_hbm,
    normed_hbm,
    gate_ref,
    grad_ref,
    sums_ref,
    unit_ref,
    total_ref,
    normed_ref,
    normed_sem,
    u_ref,
    win_ref,
    active_ref,
    hidden_ref,
    u_sem,
    win_sem,
    active_sem,
    hidden_sem,
):
    weights = Tiles(win_hbm, win_ref, win_sem, 1, True)
    us = Tiles(u_hbm, u_ref, u_sem, 1, True)
    actives = Tiles(active_hbm, active_ref, active_sem, 1, False)
    hiddens = Tiles(hidden_hbm, hidden_ref, hidden_sem, 1, False)
    count = win_ref.shape[0]
    for tile in range(count):
        weights.start(tile)
        us.start(tile)
    unit, inverse = expert_start(rows_ref, gain_ref, bias_ref, center_ref, normed_ref, gate_ref)
    unit_ref[...] = unit
    normed_out = pltpu.make_async_copy(normed_ref, normed_hbm, normed_sem)
    normed_out.start()
    lanes = gate_ref.shape[1]
    scores = jnp.zeros((unit.shape[0], lanes), F32)
    for tile in range(count):
        weights.wait(tile)
        us.wait(tile)
        active, slope = gelu_parts(dot(normed_ref[...], win_ref[tile], 1, 0))
        active = active.astype(BF)
        active_ref[tile] = active
        actives.start(tile)
        u = u_ref[tile].astype(F32)
        hidden_ref[tile] = (slope * (u * gate_ref[:, :1])).astype(BF)
        hiddens.start(tile)
        products = active.astype(F32) * u
        for place in range(0, products.shape[1], lanes):
            scores = scores + products[:, place : place + lanes]
        more = dot(hidden_ref[tile], win_ref[tile], 1, 1)
        if tile:
            total_ref[...] += more
        else:
            total_ref[...] = more
    total = total_ref[...]
    gating = gate_ref[:, :1]
    grad_gating = jnp.sum(scores, axis=-1, keepdims=True)
    grad_score = grad_gating * gating * (1.0 - gating)
    unit = unit_ref[...]
    rows = rows_ref[...].astype(F32)
    sums_ref[0:1, :] = jnp.sum(total * unit, axis=0, keepdims=True)
    sums_ref[1:2, :] = jnp.sum(total, axis=0, keepdims=True)
    sums_ref[2:3, :] = jnp.sum(rows * grad_score, axis=0, keepdims=True)
    grad = norm_backward(total * gain_ref[...].astype(F32), unit, inverse)
    grad_ref[...] = (grad + grad_score * center_ref[...].astype(F32)).astype(BF)
    normed_out.wait()
    for tile in range(count):
        actives.wait(tile)
        hiddens.wait(tile)


def expert_own(rows, u, win, gain, bias, center, after=()):
    count, width = rows.shape
    hidden = win.shape[1]
    outs = [shaped((count, hidden), BF)] * 2 + [shaped((count, width), BF)]
    outs += [shaped((count, 128), F32), shaped((count, width), BF), shaped((8, width), F32)]
    wide = (count, hidden, 1)
    return kernel_call(
        own_kernel,
        "expert_own",
        (rows, u, win, gain, bias, center),
        19,
        after,
        in_specs=[in_vmem()] + [anywhere()] * 2 + [in_vmem()] * 3,
        out_specs=[anywhere()] * 3 + [in_vmem()] * 3,
        out_shape=outs,
        scratch_shapes=[pltpu.VMEM((count, width), F32)] * 2
        + [pltpu.VMEM((count, width), BF), pltpu.SemaphoreType.DMA(())]
        + tile_buffers(wide, (width, hidden, 1), wide, wide),
    )


def other_kernel(
    rows_ref,
    cot_ref,
    copy_ref,
    win_hbm,
    wout_hbm,
    gain_ref,
    bias_ref,
    center_ref,
    active_hbm,
    hidden_hbm,
    normed_hbm,
    gate_ref,
    normed_ref,
    normed_sem,
    produced_ref,
    win_ref,
    wout_ref,
    active_ref,
    hidden_ref,
    win_sem,
    wout_sem,
    active_sem,
    hidden_sem,
):
    weights = Tiles(win_hbm, win_ref, win_sem, 1, True)
    back = Tiles(wout_hbm, wout_ref, wout_sem, 0, True)
    hiddens = Tiles(hidden_hbm, hidden_ref, hidden_sem, 1, False)
    count = win_ref.shape[0]
    size = win_ref.shape[2]
    part = active_hbm.shape[1] // size
    for tile in range(count):
        weights.start(tile)
        back.start(tile)
    expert_start(rows_ref, gain_ref, bias_ref, center_ref, normed_ref, gate_ref)
    normed_out = pltpu.make_async_copy(normed_ref, normed_hbm, normed_sem)
    normed_out.start()
    produced_ref[...] = (gate_ref[:, :1] * cot_ref[...].astype(F32)).astype(BF)

    def active_out(tile):
        place = tile % part
        return pltpu.make_async_copy(
            active_ref.at[tile],
            active_hbm.at[:, pl.ds(place * size, size)],
            active_sem.at[place],
        )

    for tile in range(count):
        weights.wait(tile)
        back.wait(tile)
        active, slope = gelu_parts(dot(normed_ref[...], win_ref[tile], 1, 0))
        active_ref[tile] = active.astype(BF)

        @pl.when(copy_ref[0] == tile // part)
        def _(tile=tile):
            active_out(tile).start()

        hidden_ref[tile] = (slope * dot(produced_ref[...], wout_ref[tile], 1, 1)).astype(BF)
        hiddens.start(tile)
    normed_out.wait()
    for tile in range(part):
        active_out(tile).wait()
    for tile in range(count):
        hiddens.wait(tile)


def expert_other(rows, cot, copy, copies, win, wout, gain, bias, center, after=()):
    count, width = rows.shape
    hidden = win.shape[1]
    wide = (count, hidden, 1)
    outs = [shaped((count, hidden // copies), BF), shaped((count, hidden), BF)]
    outs += [shaped((count, width), BF), shaped((count, 128), F32)]
    size = min(2 * TILE, hidden // copies)
    buffers = tile_buffers((width, hidden, 1), (hidden, width, 0), wide, wide, size=size)
    return kernel_call(
        other_kernel,
        "expert_other",
        (rows, cot, copy, win, wout, gain, bias, center),
        18,
        after,
        in_specs=[in_vmem()] * 2 + [scalar()] + [anywhere()] * 2 + [in_vmem()] * 3,
        out_specs=[anywhere()] * 3 + [in_vmem()],
        out_shape=outs,
        scratch_shapes=[pltpu.VMEM((count, width), BF), pltpu.SemaphoreType.DMA(())]
        + [pltpu.VMEM((count, width), BF)]
        + buffers,
    )


def grad_in_kernel(copy_ref, left_ref, left_other_ref, right_ref, right_other_ref, out_ref):
    del copy_ref
    out_ref[...] = dot(left_ref[...], right_ref[...], 0, 0) + dot(
        left_other_ref[...], right_other_ref[...], 0, 0
    )


def grad_in(copy, copies, normed, normed_other, hidden, hidden_other, after=()):
    count, width = normed.shape
    part = width // copies
    tile = min(2 * TILE, hidden.shape[1])
    left = pl.BlockSpec((count, part), lambda i, copy: (0, copy[0]))
    right = pl.BlockSpec((count, tile), lambda i, copy: (0, i))
    return kernel_call(
        grad_in_kernel,
        "grad_w_in",
        (copy, normed, normed_other, hidden, hidden_other),
        10,
        after,
        grid_spec=(
            1,
            (hidden.shape[1] // tile,),
            [left, left, right, right],
            pl.BlockSpec((part, tile), lambda i, copy: (0, i)),
        ),
        out_shape=shaped((part, hidden.shape[1]), F32),
    )


def grad_out_kernel(
    copy_ref,
    left_ref,
    left_other_ref,
    cot_ref,
    cot_other_ref,
    gate_ref,
    gate_other_ref,
    out_ref,
    right_ref,
    right_other_ref,
):
    del copy_ref

    @pl.when(pl.program_id(0) == 0)
    def _():
        right_ref[...] = (gate_ref[:, :1] * cot_ref[...].astype(F32)).astype(BF)
        right_other_ref[...] = (gate_other_ref[:, :1] * cot_other_ref[...].astype(F32)).astype(BF)

    out_ref[...] = dot(left_ref[...], right_ref[...], 0, 0) + dot(
        left_other_ref[...], right_other_ref[...], 0, 0
    )


def grad_out(copy, copies, active, active_other, cot, cot_other, gate, gate_other, after=()):
    count, width = cot.shape
    part = active.shape[1] // copies
    tile = min(TILE, part)
    tiles = part // tile
    left = pl.BlockSpec((count, tile), lambda i, copy: (0, copy[0] * tiles + i))
    left_other = pl.BlockSpec((count, tile), lambda i, copy: (0, i))
    right = pl.BlockSpec((count, width), lambda i, copy: (0, 0))
    gates = pl.BlockSpec(gate.shape, lambda i, copy: (0, 0))
    return kernel_call(
        grad_out_kernel,
        "grad_w_out",
        (copy, active, active_other, cot, cot_other, gate, gate_other),
        10,
        after,
        grid_spec=(
            1,
            (tiles,),
            [left, left_other, right, right, gates, gates],
            pl.BlockSpec((tile, width), lambda i, copy: (i, 0)),
        ),
        out_shape=shaped((part, width), F32),
        scratch_shapes=[pltpu.VMEM((count, width), BF)] * 2,
    )


def finish_kernel(many, extra, place_ref, *refs):
    parts, outs = refs[: 2 * many], refs[2 * many + extra :]
    place = place_ref[0]
    rows = parts[0].shape[0]
    here = pl.ds(pl.multiple_of(place * rows, rows), rows)
    away = pl.ds(pl.multiple_of((1 - place) * rows, rows), rows)
    for i in range(many):
        outs[i][here, :] = parts[2 * i][...].astype(F32)
        outs[i][away, :] = parts[2 * i + 1][...].astype(F32)


def finished(own, got, *, place, many, groups, total, before=None):
    start, stop = groups
    rows = own.shape[0]
    part = [
        pl.BlockSpec((rows, GROUP), functools.partial(lambda i, g: (0, many * g + i), i))
        for i in range(many)
    ]
    extra = list(before or ())
    return kernel_call(
        functools.partial(finish_kernel, many, len(extra)),
        "gradients_out",
        [place] + [own, got] * many + extra,
        2 * many,
        grid=(stop - start,),
        in_specs=[scalar()] + [spec for spec in part for _ in range(2)] + [anywhere()] * len(extra),
        out_specs=[pl.BlockSpec((CORES * rows, GROUP), lambda g: (0, start + g))] * many,
        out_shape=[shaped((CORES * rows, total), F32)] * many,
        input_output_aliases={1 + 2 * many + i: i for i in range(len(extra))},
    )


def expert_levels(size):
    levels, stride = [], 1
    while stride < size:
        levels.append((stride, 2 if (size // stride) % 2 == 0 else size // stride))
        stride *= levels[-1][1]
    return levels


def turned(axis, stride, length, step):
    pairs = []
    for index in range(lax.axis_size(axis)):
        place = (index // stride) % length
        pairs.append((index, index + ((place + step) % length - place) * stride))
    return pairs


def scatter_level(rows, axis, stride, length, outer=1):
    place = (lax.axis_index(axis) // stride) % length
    columns = rows.shape[1]
    split = rows.reshape(outer, length, -1, columns)
    total = lax.dynamic_index_in_dim(split, place, 1, False).astype(F32)
    for step in range(1, length):
        part = lax.dynamic_index_in_dim(split, (place + step) % length, 1, False)
        part = lax.ppermute(part, axis, turned(axis, stride, length, step))
        total = total + part.astype(F32)
    return total.astype(rows.dtype).reshape(-1, columns)


def gather_level(rows, axis, stride, length):
    place = (lax.axis_index(axis) // stride) % length
    count = rows.shape[0]
    parts = [rows] + [
        lax.ppermute(rows, axis, turned(axis, stride, length, step)) for step in range(1, length)
    ]
    if length == 2:
        return jnp.where(
            place == 0, jnp.concatenate(parts, 0), jnp.concatenate([parts[1], parts[0]], 0)
        )
    whole = jnp.zeros((length * count, rows.shape[1]), rows.dtype)
    for step, part in enumerate(parts):
        whole = lax.dynamic_update_slice_in_dim(whole, part, ((place - step) % length) * count, 0)
    return whole


def tied(values, *others):
    return lax.optimization_barrier((values, others))[0]


class RowSum:
    def __init__(self, send, keep, copies_second=False):
        levels = expert_levels(lax.axis_size("expert"))
        copies = lax.axis_size("batch")
        self.held = (send, keep)
        scatters = [("batch", 1, copies)] + [("expert", *at) for at in levels[1:-1]]
        if copies_second and len(scatters) > 1:
            scatters[:2] = [(*scatters[1], copies), scatters[0]]
        self.todo = [self.cores] + [functools.partial(self.scatter, *at) for at in scatters]
        self.todo += [functools.partial(self.whole, "expert", *levels[-1])]
        self.todo += [functools.partial(self.gather, "expert", *at) for at in levels[-2:0:-1]]
        self.todo.append(self.partner)

    def step(self):
        if self.todo:
            self.todo.pop(0)()

    def cores(self):
        send, keep = self.held
        got = lax.ppermute(send, "expert", turned("expert", 1, CORES, 1))
        total = (keep.astype(F32) + got.astype(F32)).astype(BF)
        self.held = total.reshape(-1, total.shape[-1])

    def scatter(self, *level):
        self.held = scatter_level(self.held, *level)

    def gather(self, *level):
        self.held = gather_level(self.held, *level)

    def partner(self):
        self.held = (self.held, lax.ppermute(self.held, "expert", turned("expert", 1, CORES, 1)))

    def whole(self, axis, stride, length):
        total = self.held.astype(F32)
        for step in range(1, length):
            part = lax.ppermute(self.held, axis, turned(axis, stride, length, step))
            total = total + part.astype(F32)
        self.held = total.astype(BF)


class SmallSum:
    def __init__(self, values):
        self.held = values
        bits = []
        while 1 << len(bits) < lax.axis_size("expert"):
            bits.append(functools.partial(self.doubled, 1 << len(bits)))
        self.todo = [self.copies] + bits

    def step(self):
        if self.todo:
            self.todo.pop(0)()

    def copies(self):
        copies, place = lax.axis_size("batch"), lax.axis_index("batch")
        total = lax.dynamic_index_in_dim(self.held, place, 0, True)
        for step in range(1, copies):
            part = lax.dynamic_index_in_dim(self.held, (place + step) % copies, 0, True)
            total = total + lax.ppermute(part, "batch", turned("batch", 1, copies, step))
        self.held = total

    def doubled(self, bit):
        pairs = [(i, i ^ bit) for i in range(lax.axis_size("expert"))]
        self.held = self.held + lax.ppermute(self.held, "expert", pairs)


def local(
    tokens,
    cotangent,
    segment_ids,
    routing,
    ln_gain,
    ln_bias,
    w_query,
    w_key,
    w_value,
    w_output,
    expert_gain,
    expert_bias,
    centroid,
    w_in,
    w_out,
):
    count, width = tokens.shape
    owners = lax.axis_size("expert")
    copies = lax.axis_size("batch")
    copy = lax.axis_index("batch")
    place = (lax.axis_index("expert") % CORES).astype(jnp.int32)[None]
    send_rows = count // owners
    win = w_in[0]
    wout = w_out[0]

    def exchanged(values):
        return lax.all_to_all(
            values.reshape(owners, send_rows, width),
            "expert",
            split_axis=0,
            concat_axis=0,
            tiled=True,
        ).reshape(count, width)

    def from_copy(values, step):
        return lax.ppermute(values, "batch", turned("batch", 1, copies, step))

    paired = copies == 2
    cot_rows = exchanged(order_rows(cotangent, routing))
    *saved, stream, ordered = attention_forward(
        tokens,
        ln_gain[None],
        ln_bias[None],
        segment_ids,
        routing,
        w_query,
        w_key,
        w_value,
        w_output,
    )
    mixed = saved[4]
    rows = exchanged(ordered)
    cot_other = from_copy(cot_rows, 1) if paired else None
    u = times_out(cot_rows, wout)
    rows, u = tied((rows, u))
    rows_other = from_copy(rows, 1) if paired else None
    vectors = (expert_gain, expert_bias, centroid)
    active, grad_hidden, expert_normed, gating, grad_rows, sums = expert_own(
        rows, u, win, *vectors
    )

    grad_returned = exchanged(grad_rows)
    branch = branch_rows(active, wout, gating, [grad_rows])
    which = copy.astype(jnp.int32)[None]
    if paired:
        active_o, hidden_o, normed_o, gating_o = expert_other(
            rows_other, cot_other, which, copies, win, wout, *vectors, [branch]
        )
        branch, active_o = tied((branch, active_o))
    grad_returned = tied(grad_returned, branch)

    attended, send, keep = gradient_entry(
        grad_returned, routing, cotangent, mixed, place, copies, [branch]
    )
    sum_o = RowSum(send, keep, True)
    groups = width // GROUP
    middle = groups // 2
    backward = functools.partial(attention_backward, saved=saved, attended=attended, w_output=w_output)
    send, keep, grads_a = backward((0, middle), place=place, copies=copies, after=[attended])
    sum_o.step()
    sum_o.held, send, keep = tied((sum_o.held, send, keep))
    sum_a = RowSum(send, keep)
    sum_a.step()
    sum_a.held, sum_o.held = tied((sum_a.held, sum_o.held))
    send, keep, grads_b = backward((middle, groups), place=place, copies=copies, after=[sum_a.held])
    sum_o.step()
    sum_a.step()
    sum_a.held, sum_o.held, send, keep = tied((sum_a.held, sum_o.held, send, keep))
    sum_b = RowSum(send, keep)
    sum_b.step()
    sum_o.step()
    branch = exchanged(tied(branch, grads_b))

    gate_vector = jnp.where(
        jnp.arange(owners) == lax.axis_index("expert"),
        jnp.sum(gating[:, 0]) / (count * copies),
        0.0,
    )
    small = sums[:3].reshape(3, copies, width // copies)
    slot = 0
    done = []
    packed = None
    finish = functools.partial(finished, place=place, total=width)
    while sum_b.todo:
        parts = [part for part in (sum_b, sum_a, sum_o, packed) if part is not None]
        if slot:
            held, small, done = tied(([part.held for part in parts], small, done))
            for part, value in zip(parts, held):
                part.held = value
        if slot == 0 and paired:
            done.append(
                grad_out(
                    which, copies, active, active_o, cot_rows, cot_other, gating, gating_o,
                    [sum_b.held],
                )
            )
        if slot == 0:
            grad_tokens, norm_sums = tokens_gradient(
                (grads_a, grads_b),
                (w_query, w_key, w_value),
                tokens,
                ln_gain[None],
                grad_returned,
                routing,
                cotangent,
                [sum_b.held],
            )
            done += [grad_tokens, norm_sums]
        if slot == 1:
            norm_sums = done.pop()
            packed = SmallSum(
                jnp.concatenate(
                    [
                        norm_sums[0].reshape(copies, -1),
                        norm_sums[1].reshape(copies, -1),
                        gate_vector.reshape(copies, -1),
                    ],
                    axis=1,
                )
            )
        if slot == 2:
            if paired:
                done.append(
                    grad_in(
                        which, copies, expert_normed, normed_o, grad_hidden, hidden_o, [sum_b.held]
                    )
                )
        if slot == 3:
            small_total = lax.dynamic_index_in_dim(small, copy, 1, False)
            for step in range(1, copies):
                away = lax.dynamic_index_in_dim(small, (copy + step) % copies, 1, False)
                small_total = small_total + from_copy(away, step)
            small = small_total
        if slot == 5:
            branch = tied(branch, sum_b.held)
            outputs = output_rows(branch, routing, stream)
            done.append(outputs)
        if not sum_o.todo and sum_o.held:
            (grad_wo,) = finish(*sum_o.held, many=1, groups=(0, groups))
            done.append(grad_wo)
            sum_o.held = ()
        if not sum_a.todo and sum_a.held:
            before = finish(*sum_a.held, many=3, groups=(0, middle))
            done.extend(before)
            sum_a.held = ()
        if slot == 0:
            sum_a.held, sum_o.held = tied((sum_a.held, sum_o.held), sum_b.held)
        for part in (sum_b, sum_a, sum_o, packed):
            if part is not None:
                part.step()
        slot += 1
    while packed.todo:
        packed.step()
    grad_wq, grad_wk, grad_wv = finish(
        *sum_b.held, many=3, groups=(middle, groups), before=before
    )
    small_total = small
    if paired:
        grad_w_out, grad_w_in = done[0], done[2]
    else:
        produced = (gating[:, :1] * cot_rows.astype(F32)).astype(BF)
        grad_w_in, grad_w_out = (
            lax.psum_scatter(
                dot(left, right, 0, 0).astype(BF), "batch", scatter_dimension=0, tiled=True
            ).astype(F32)
            for left, right in ((expert_normed, grad_hidden), (active, produced))
        )
    part = width // copies
    packed = packed.held[0]
    return (
        outputs,
        grad_tokens,
        packed[:part],
        packed[part : 2 * part],
        grad_wq,
        grad_wk,
        grad_wv,
        grad_wo,
        small_total[0][None],
        small_total[1][None],
        small_total[2][None],
        grad_w_in[None],
        grad_w_out[None],
        packed[2 * part :],
    )


def solution(mesh):
    both = P(("expert", "batch"), None)
    per_expert = P("expert", None)
    matrices = P("expert", None, None)
    return jax.shard_map(
        local,
        mesh=mesh,
        in_specs=(both,) * 4 + (P(),) * 6 + (per_expert,) * 3 + (matrices,) * 2,
        out_specs=(both, both)
        + (P("batch"),) * 2
        + (P("batch", None),) * 4
        + (P("expert", "batch"),) * 3
        + (P("expert", "batch", None),) * 2
        + (P("batch"),),
        check_vma=False,
    )
```
